32 devices in a mesh: dp: 8 (over z, x), rep: 4 (over y, core).
Axes of the slice: x: 2, y: 2, z: 4, core: 2. Of those that a mesh axis runs over, the one named last changes fastest.
Arguments:
- embeddings: bfloat16 [32768, 4096], P(('dp', 'rep'))
- assignment: int32 [32768], P(('dp', 'rep')), may hold values from 0 to 7
- block_mask: int32 [256], P(('dp', 'rep')), may hold values from 0 to 1, as said below
- cluster_cap: int32 [8], replicated, may hold values from 12 to 24, as said below
- adjacent: int32 [8], replicated, may hold values from 0 to 7, as said below
Outputs:
- keep: float32 [32768], P(('dp', 'rep'))
The draws below stay inside these ranges and needn't reach their ends.
Inputs may be any that keep to these rules, and one draw needn't show every extreme that they name: `cluster_cap`: caps are at most 24; in every draw some cluster has cap 24 and 24 or more active documents in every device block. `adjacent`: one cycle through all clusters: each cluster names another one, and is named by exactly one. `block_mask`: every device block of 1024 documents has an active block.
All inputs are finite; a program needn't handle non-finite values.
Results may differ from the reference program's by a relative error of at most 0.0003.
Values may be sent and summed in bfloat16 or wider, within the bound.
No kernel may reach another device: no remote copies, remote signals or barrier semaphores. Data moves between devices by JAX's collectives and lax.ppermute only.
A program may use at most 128 MiB of HBM per device.

```python
import math
import jax
import jax.numpy as jnp
from jax import lax

D = 4096
DOC_DEV = 1024
BLK = 128
CAPS = 24
CLUSTERS = 8
SLOTS = 192
GROUP = 768
DOCS = 32768
N_DP = 8
N_REP = 4


def hot_cluster(key):
    return jax.random.randint(jax.random.fold_in(key, 7), (), 0, CLUSTERS)


def cycle_table(key):
    shuffled = jax.random.permutation(jax.random.fold_in(key, 61), CLUSTERS).astype(jnp.int32)
    return jnp.zeros((CLUSTERS,), jnp.int32).at[shuffled].set(jnp.roll(shuffled, -1))


def doc_layout(key):
    hot = hot_cluster(key).astype(jnp.int32)
    cycle = cycle_table(key)
    cluster_ids = jnp.arange(CLUSTERS, dtype=jnp.int32)
    prev_hot = jnp.sum(cluster_ids * (cycle == hot).astype(jnp.int32)).astype(jnp.int32)
    shuffled = jax.random.permutation(jax.random.fold_in(key, 21), CLUSTERS).astype(jnp.int32)
    first_draw = jax.random.randint(jax.random.fold_in(key, 22), (DOCS,), 0, CLUSTERS)
    second_draw = jax.random.randint(jax.random.fold_in(key, 23), (DOCS,), 0, CLUSTERS)
    row_ids = jnp.arange(DOCS, dtype=jnp.int32)
    local_row = row_ids % DOC_DEV
    hot_row = local_row < CAPS
    base_assign = jnp.where(hot_row, hot, shuffled[jnp.minimum(first_draw, second_draw)]).astype(jnp.int32)
    edge_dup = ~hot_row & (jax.random.randint(jax.random.fold_in(key, 24), (DOCS,), 0, DOC_DEV) < 4)
    coin_dup = ~hot_row & (jax.random.randint(jax.random.fold_in(key, 25), (DOCS,), 0, 4) == 0)
    candidate = edge_dup | coin_dup
    parent = jax.random.randint(jax.random.fold_in(key, 26), (DOCS,), 0, DOCS).astype(jnp.int32)
    same_dup = coin_dup & ~edge_dup & ~candidate[parent]
    lane = row_ids // DOC_DEV % N_REP
    edge_source = jax.random.randint(jax.random.fold_in(key, 27), (DOCS,), 0, N_DP).astype(jnp.int32)
    edge_parent = ((edge_source * N_REP + lane) * DOC_DEV).astype(jnp.int32)
    assignment = jnp.where(edge_dup, prev_hot, jnp.where(same_dup, base_assign[parent], base_assign)).astype(jnp.int32)
    source_row = jnp.where(edge_dup, edge_parent, jnp.where(same_dup, parent, row_ids)).astype(jnp.int32)
    return (assignment, source_row, edge_dup | same_dup)


def draw_embeddings(key, part):
    assignment, source_row, duplicate = doc_layout(key)
    base_key = jax.random.fold_in(key, 11)
    noise_key = jax.random.fold_in(key, 12)
    row_ids = jnp.arange(DOCS, dtype=jnp.int32)
    centroids = jax.random.normal(jax.random.fold_in(key, 13), (CLUSTERS, D), jnp.float32)
    centre_weight = jax.random.uniform(jax.random.fold_in(key, 14), (DOCS,), jnp.float32, 0.0, 0.12)
    noise_level = jnp.exp(jax.random.uniform(jax.random.fold_in(key, 15), (DOCS,), jnp.float32, math.log(0.5), math.log(12.0)))
    noise_level = jnp.where(duplicate, noise_level, 0.0)

    def make_row(row_key):
        return jax.random.normal(row_key, (D,), jnp.float32)
    row_scale = jnp.exp(jax.random.uniform(jax.random.fold_in(key, 16), (DOCS,), jnp.float32, 0.0, math.log(10.0)))
    base_vals = jax.vmap(lambda index: make_row(jax.random.fold_in(base_key, index)))(source_row)
    noise_vals = jax.vmap(lambda index: make_row(jax.random.fold_in(noise_key, index)))(row_ids)
    rows = centre_weight[:, None] * centroids[assignment] + base_vals + noise_level[:, None] * noise_vals
    return (rows * row_scale[:, None]).astype(jnp.bfloat16)


def draw_assignment(key, part):
    assignment, source_row, duplicate = doc_layout(key)
    return assignment


def draw_block_mask(key, part):
    count_blocks = DOCS // BLK
    coin_flips = jax.random.randint(jax.random.fold_in(key, 31), (count_blocks,), 0, 4) != 0
    leading = jnp.arange(count_blocks, dtype=jnp.int32) % (DOC_DEV // BLK) == 0
    return jnp.where(coin_flips | leading, 1, 0).astype(jnp.int32)


def draw_cluster_cap(key, part):
    cap_vals = jax.random.randint(jax.random.fold_in(key, 41), (CLUSTERS,), CAPS // 2, CAPS + 1)
    return cap_vals.at[hot_cluster(key)].set(CAPS).astype(jnp.int32)


def draw_adjacent(key, part):
    return cycle_table(key)


def setup_inputs(seed: int = 0) -> dict:
    splits = jax.random.split(jax.random.key(seed), 6)
    embeddings = draw_embeddings(jax.random.fold_in(splits[5], 71), 0)
    assignment = draw_assignment(jax.random.fold_in(splits[5], 71), 0)
    block_mask = draw_block_mask(jax.random.fold_in(splits[5], 71), 0)
    cluster_cap = draw_cluster_cap(jax.random.fold_in(splits[5], 71), 0)
    adjacent = draw_adjacent(jax.random.fold_in(splits[5], 71), 0)
    return dict(embeddings=embeddings, assignment=assignment, block_mask=block_mask, cluster_cap=cluster_cap, adjacent=adjacent)


slope_gain = 64.0
inner_cut = 0.12
edge_cut = 0.06

def unit_rows(embeddings):
    values = embeddings.astype(jnp.float32)
    squares = lax.optimization_barrier(jnp.sum(values * values, axis=1))
    return (values * lax.rsqrt(squares + 1e-06)[:, None]).astype(jnp.bfloat16)

def reference(embeddings, assignment, block_mask, cluster_cap, adjacent):
    normed = unit_rows(embeddings)
    row_index = jnp.arange(DOCS, dtype=jnp.int32)
    active = jnp.repeat(block_mask, BLK) == 1
    device_block = row_index // DOC_DEV
    source = device_block // N_REP
    lane_index = device_block % N_REP
    cluster_ids = jnp.arange(CLUSTERS, dtype=jnp.int32)
    member = ((assignment[:, None] == cluster_ids[None, :]) & active[:, None]).astype(jnp.int32)
    blocked = member.reshape(DOCS // DOC_DEV, DOC_DEV, CLUSTERS)
    before = (jnp.cumsum(blocked, axis=1) - blocked).reshape(DOCS, CLUSTERS)
    row_rank = lax.optimization_barrier(jnp.sum(before * member, axis=1)).astype(jnp.int32)
    placed = active & (row_rank < cluster_cap[assignment])
    slot_index = lane_index * SLOTS + source * CAPS + row_rank
    position = jnp.where(placed, assignment * GROUP + slot_index, CLUSTERS * GROUP).astype(jnp.int32)
    slot_table = jnp.zeros((CLUSTERS * GROUP, D), jnp.bfloat16).at[position].set(normed, mode='drop').reshape(CLUSTERS, GROUP, D)
    filled = jnp.zeros((CLUSTERS * GROUP,), jnp.float32).at[position].set(1.0, mode='drop').reshape(CLUSTERS, GROUP)
    group_ids = jnp.arange(GROUP, dtype=jnp.int32)
    distinct = (group_ids[:, None] != group_ids[None, :]).astype(jnp.float32)

    def cluster_score(cluster):
        members = slot_table[cluster].astype(jnp.float32)
        valid_cols = filled[cluster]
        gram_tile = jnp.dot(members, members.T, precision=lax.Precision.HIGHEST)
        weights = jax.nn.sigmoid(slope_gain * (gram_tile - inner_cut)) * valid_cols[None, :] * distinct
        inner_sum = lax.optimization_barrier(jnp.sum(weights, axis=1))
        neighbour = adjacent[cluster]
        edge_rows = slot_table[neighbour].reshape(N_REP, N_DP, CAPS, D)[:, :, 0].astype(jnp.float32)
        edge_valid = filled[neighbour].reshape(N_REP, N_DP, CAPS)[:, :, 0]
        edge_gram = jnp.einsum('rsd,rkd->rsk', members.reshape(N_REP, SLOTS, D), edge_rows, precision=lax.Precision.HIGHEST)
        edge_weights = jax.nn.sigmoid(slope_gain * (edge_gram - edge_cut)) * edge_valid[:, None, :]
        return inner_sum + lax.optimization_barrier(jnp.sum(edge_weights, axis=2)).reshape(GROUP)
    scores = lax.map(cluster_score, cluster_ids)
    keep_slots = (1.0 / (1.0 + scores)).reshape(CLUSTERS * GROUP)
    safe_index = jnp.where(placed, position, 0).astype(jnp.int32)
    return jnp.where(placed, keep_slots[safe_index], 1.0).astype(jnp.float32)
```

```python
import functools

import jax
import jax.numpy as jnp
from jax import lax
from jax.experimental import pallas as pl
from jax.experimental.pallas import tpu as pltpu
from jax.sharding import PartitionSpec as P

CAPS = 24
LANES = 128
ALL = ("dp", "rep")
FEATURE_STEP = 512
EMPTY_MARK = 4.0
PENALTY = -1000.0
VMEM_BYTES = 60 * 1024 * 1024

slope_gain = 64.0
inner_cut = 0.12
edge_cut = 0.06


def each(count, body, limit=8):
    if count <= limit:
        for index in range(count):
            body(index)
    else:

        def step(index, carry):
            body(index)
            return carry

        lax.fori_loop(0, count, step, 0)


def iota(shape, dim):
    return lax.broadcasted_iota(jnp.int32, shape, dim)


def select_kernel(
    clusters, reps, cap, adjacent, mask, assign, rows, out, slots, pick, filled, chosen, squares
):
    step = pl.program_id(0)
    blocks = assign.shape[0]
    depth = chosen.shape[1]
    wide = rows.shape[1]
    count = pick.shape[0]
    base = clusters * CAPS

    @pl.when(step == 0)
    def _():
        table = assign[...]
        sub = iota(table.shape, 0)
        active = jnp.zeros(table.shape, jnp.int32)
        for block in range(blocks):
            active = jnp.where(sub == block, mask[block], active)
        live = jnp.where(active == 1, table, -1)
        members = jnp.concatenate(
            [(live == c).astype(jnp.float32) for c in range(clusters)], axis=0
        ).astype(jnp.bfloat16)
        total = clusters * blocks
        earlier = (iota((LANES, LANES), 0) < iota((LANES, LANES), 1)).astype(jnp.bfloat16)
        within = jnp.dot(members, earlier, preferred_element_type=jnp.float32)
        left, right = iota((total, total), 0), iota((total, total), 1)
        same = (left // blocks == right // blocks) & (right < left)
        sums = jnp.dot(
            same.astype(jnp.bfloat16), members, preferred_element_type=jnp.float32
        ).astype(jnp.bfloat16)
        before = jnp.dot(
            sums, jnp.ones((LANES, LANES), jnp.bfloat16), preferred_element_type=jnp.float32
        )
        rank = (within + before).astype(jnp.int32)
        slot = jnp.full(table.shape, -1, jnp.int32)
        for c in range(clusters):
            own = rank[c * blocks : (c + 1) * blocks]
            slot = jnp.where((live == c) & (own < cap[c]), c * CAPS + own, slot)
        slots[...] = slot
        place = iota((count, LANES), 0)
        target = jnp.where(place < base, place, -7)
        for c in range(clusters):
            target = jnp.where(place == base + c, adjacent[c] * CAPS, target)
        seen = jnp.zeros((count, LANES), jnp.float32)
        for block in range(blocks):
            hit = (target == slot[block : block + 1]).astype(jnp.float32)
            pick[:, block * LANES : (block + 1) * LANES] = hit.astype(jnp.bfloat16)
            seen += hit
        filled[...] = seen
        squares[...] = jnp.zeros_like(squares)

    part = jnp.dot(pick[...], rows[...], preferred_element_type=jnp.float32)
    chosen[:, pl.ds(pl.multiple_of(step * wide, wide), wide)] = part
    power = squares[...]
    for k in range(wide // LANES):
        piece = part[:, k * LANES : (k + 1) * LANES]
        power += piece * piece
    squares[...] = power

    @pl.when(step == pl.num_programs(0) - 1)
    def _():
        scale = lax.rsqrt(jnp.sum(squares[...], axis=1, keepdims=True) + 1e-06)
        squares[...] = jnp.broadcast_to(scale, squares.shape)
        mark = jnp.sum(filled[...], axis=1, keepdims=True) < 0.5
        mark = mark & (iota(filled.shape, 1) == 0)
        filled[...] = jnp.where(mark, EMPTY_MARK, 0.0)
        quarter = depth // reps
        tiles = quarter // LANES
        sub = iota((tiles, LANES), 0)

        def eight(group):
            near = pl.ds(pl.multiple_of(base + group * 8, 8), 8)
            near_gain, near_flag = squares[near, :], filled[near, :]
            for k in range(8):
                at = pl.ds(pl.multiple_of((group * 8 + k) * CAPS, 8), CAPS)
                gain, flag = squares[at, :], filled[at, :]
                for q in range(reps):
                    pieces = []
                    edge = jnp.zeros((tiles, LANES), jnp.float32)
                    for t in range(tiles):
                        cols = slice(q * quarter + t * LANES, q * quarter + (t + 1) * LANES)
                        piece = chosen[at, cols] * gain
                        line = chosen[near, cols] * near_gain
                        if t == 0:
                            piece += flag
                            line += near_flag
                        pieces.append(piece)
                        line = jnp.broadcast_to(line[k : k + 1], edge.shape)
                        edge = jnp.where(sub == t, line, edge)
                    pieces.append(edge)
                    chunk = jnp.concatenate(pieces, axis=0).astype(jnp.bfloat16)
                    out[(group * 8 + k) * reps + q] = chunk

        each(clusters // 8, eight, 1)


def gram_kernel(
    ranks, per_set, got, send_far, send_near, keep_far, keep_near, x, edge_rows, edge_x, hold, sem
):
    sources = got.shape[0]
    count, quarter = x.shape
    tiles = quarter // LANES
    blocks = count // LANES
    reps = 4
    main = tiles * CAPS
    me = lax.axis_index("rep")
    my_core, my_y = me % 2, me // 2

    def gather(pair):
        values = [got[2 * pair + k].astype(jnp.float32) for k in range(2)]
        for k in range(2):
            edge_rows[pl.ds((2 * pair + k) * tiles, tiles), :] = values[k][main:]
        for k in range(tiles):
            rows = slice(k * CAPS, (k + 1) * CAPS)
            both = jnp.concatenate([v[rows] for v in values], axis=0)
            x[pl.ds(pair * 2 * CAPS, 2 * CAPS), k * LANES : (k + 1) * LANES] = both.astype(
                jnp.bfloat16
            )

    each(sources // 2, gather, 16)

    for lane in range(reps):
        edge_x[lane * ranks : (lane + 1) * ranks, :] = jnp.concatenate(
            [
                edge_rows[pl.ds(lane * tiles + k, ranks, stride=reps * tiles), :]
                for k in range(tiles)
            ],
            axis=1,
        ).astype(jnp.bfloat16)

    first = (iota((8, LANES), 1) == 0).astype(jnp.bfloat16)
    contract = (((1,), (1,)), ((), ()))
    marks = lax.dot_general(first, x[:, :LANES], contract, preferred_element_type=jnp.float32)
    col_pen = jnp.where(marks[:1] > 2.0, PENALTY, 0.0)

    def put(index, value):
        owner, place = index % reps, index // reps
        slot = 2 * (my_core == owner % 2).astype(jnp.int32) + (my_y == owner // 2).astype(jnp.int32)
        hold[slot, place * LANES : place * LANES + value.shape[0], :] = value

    index = 0
    step = 2 * LANES
    for start in range(0, count, step):
        rows = x[start : start + step, :]
        gram = lax.dot_general(rows, x[start:, :], contract, preferred_element_type=jnp.float32)
        row_pen = jnp.where(rows[:, :1].astype(jnp.float32) > 2.0, PENALTY, 0.0)
        gram = gram + row_pen + col_pen[:, start:]
        shape = (LANES, LANES)
        for half in range(2):
            for tile in range(half, (count - start) // LANES):
                value = gram[
                    half * LANES : (half + 1) * LANES, tile * LANES : (tile + 1) * LANES
                ]
                if tile == half:
                    value = jnp.where(iota(shape, 0) == iota(shape, 1), PENALTY, value)
                put(index, value)
                index += 1

    near = edge_x[...]
    edge = lax.dot_general(near, x[...], contract, preferred_element_type=jnp.float32)
    edge = edge + jnp.where(near[:, :1].astype(jnp.float32) > 2.0, PENALTY, 0.0)
    lane_of = lax.rem(lax.div(iota((ranks, count), 1), CAPS), reps)
    small = edge[:ranks]
    for lane in range(1, reps):
        small = jnp.where(lane_of == lane, edge[lane * ranks : (lane + 1) * ranks], small)
    per_tile = LANES // ranks
    for first_block in range(0, blocks, per_tile):
        stop = min(blocks, first_block + per_tile)
        put(
            index,
            jnp.concatenate(
                [small[:, b * LANES : (b + 1) * LANES] for b in range(first_block, stop)], axis=0
            ),
        )
        index += 1

    copies = [
        pltpu.make_async_copy(hold.at[k], ref, sem.at[k])
        for k, ref in enumerate((send_far, send_near, keep_far, keep_near))
    ]
    for copy in copies:
        copy.start()
    for copy in copies:
        copy.wait()


def score_kernel(ranks, sources, keep, core, far, out, total):
    count = sources * CAPS
    blocks = count // LANES
    reps = 4
    me = lax.axis_index("rep")
    pairs = [(i, j) for i in range(blocks) for j in range(i, blocks)]
    total[...] = jnp.zeros_like(total)

    def value(place, size):
        at = slice(place * LANES, place * LANES + size)
        return keep[at, :] + core[at, :] + far[at, :]

    def by_rep(values):
        picked = jnp.int32(values[0])
        for k in range(1, len(values)):
            picked = jnp.where(me == k, jnp.int32(values[k]), picked)
        return picked

    def tile(place):
        options = [pairs[min(place * reps + k, len(pairs) - 1)] for k in range(reps)]
        i, j = by_rep([p[0] for p in options]), by_rep([p[1] for p in options])
        weight = jax.nn.sigmoid(slope_gain * (value(place, LANES) - inner_cut))
        total[pl.ds(i, 1), :] += jnp.sum(weight.T, axis=0, keepdims=True)
        other = (i != j).astype(jnp.float32)
        total[pl.ds(j, 1), :] += jnp.sum(weight, axis=0, keepdims=True) * other

    per_set = -(-len(pairs) // reps)
    for place in range(per_set):
        if (place + 1) * reps <= len(pairs):
            tile(place)
        else:
            pl.when(place * reps + me < len(pairs))(functools.partial(tile, place))

    per_tile = LANES // ranks
    for e, first_block in enumerate(range(0, blocks, per_tile)):
        owner, place = (len(pairs) + e) % reps, (len(pairs) + e) // reps
        stop = min(blocks, first_block + per_tile)

        @pl.when(me == owner)
        def _(place=place, first_block=first_block, stop=stop):
            edge = value(place, (stop - first_block) * ranks)
            edge = jax.nn.sigmoid(slope_gain * (edge - edge_cut))
            for b in range(first_block, stop):
                at = (b - first_block) * ranks
                total[b : b + 1, :] += jnp.sum(edge[at : at + ranks], axis=0, keepdims=True)

    result = jnp.zeros((sources, LANES), jnp.float32)
    for b in range(blocks):
        where = iota((sources, LANES), 1) + b * LANES
        mine = lax.div(where, CAPS) == iota((sources, LANES), 0)
        spread = jnp.where(mine, total[b : b + 1, :], 0.0)
        move = lax.rem(iota((LANES, LANES), 0) + b * LANES, CAPS) == iota((LANES, LANES), 1)
        result += jnp.dot(
            spread,
            move.astype(jnp.float32),
            precision=lax.Precision.HIGHEST,
            preferred_element_type=jnp.float32,
        )
    out[...] = result


def final_kernel(clusters, reps, slots, sums, out):
    slot = slots[...]
    result = jnp.ones(slot.shape, jnp.float32)
    for c in range(clusters):
        inner = jnp.sum(sums[c * reps : (c + 1) * reps, :], axis=0, keepdims=True)
        keep = jnp.broadcast_to(1.0 / (1.0 + inner), slot.shape)
        rank = slot - c * CAPS
        mine = (rank >= 0) & (rank < CAPS)
        found = jnp.take_along_axis(keep, jnp.where(mine, rank, 0), axis=1)
        result = jnp.where(mine, found, result)
    out[...] = result


def local(embeddings, assignment, block_mask, cluster_cap, adjacent):
    dp_count, reps = lax.axis_size("dp"), lax.axis_size("rep")
    devices = dp_count * reps
    rows_dev, depth = embeddings.shape
    blocks = block_mask.shape[0]
    clusters = cluster_cap.shape[0]
    quarter = depth // reps
    tiles = quarter // LANES
    chunk = tiles * CAPS + tiles
    picks = -(-(clusters * (CAPS + 1)) // 16) * 16
    params = pltpu.CompilerParams(vmem_limit_bytes=VMEM_BYTES)
    smem = pl.BlockSpec(memory_space=pltpu.SMEM)
    vmem = pl.BlockSpec(memory_space=pltpu.VMEM)
    anywhere = pl.BlockSpec(memory_space=pl.ANY)

    send, slots = pl.pallas_call(
        functools.partial(select_kernel, clusters, reps),
        grid=(depth // FEATURE_STEP,),
        in_specs=[
            smem,
            smem,
            smem,
            pl.BlockSpec((blocks, LANES), lambda i: (0, 0)),
            pl.BlockSpec((rows_dev, FEATURE_STEP), lambda i: (0, i)),
        ],
        out_specs=[
            pl.BlockSpec((devices, chunk, LANES), lambda i: (0, 0, 0)),
            pl.BlockSpec((blocks, LANES), lambda i: (0, 0)),
        ],
        out_shape=[
            jax.ShapeDtypeStruct((devices, chunk, LANES), jnp.bfloat16),
            jax.ShapeDtypeStruct((blocks, LANES), jnp.int32),
        ],
        scratch_shapes=[
            pltpu.VMEM((picks, rows_dev), jnp.bfloat16),
            pltpu.VMEM((picks, LANES), jnp.float32),
            pltpu.VMEM((picks, depth), jnp.float32),
            pltpu.VMEM((picks, LANES), jnp.float32),
        ],
        compiler_params=params,
        name="select_rows",
    )(cluster_cap, adjacent, block_mask, assignment.reshape(blocks, LANES), embeddings)

    got = lax.all_to_all(send, ALL, split_axis=0, concat_axis=0, tiled=True)

    count = devices * CAPS
    group = count // LANES
    pairs = group * (group + 1) // 2
    edge_tiles = -(-group // (LANES // dp_count))
    per_set = -(-(pairs + edge_tiles) // reps)
    part = jax.ShapeDtypeStruct((per_set * LANES, LANES), jnp.float32)
    send_far, send_near, keep_far, keep_near = pl.pallas_call(
        functools.partial(gram_kernel, dp_count, per_set),
        in_specs=[vmem],
        out_specs=[anywhere] * 4,
        out_shape=[part] * 4,
        scratch_shapes=[
            pltpu.VMEM((count, quarter), jnp.bfloat16),
            pltpu.VMEM((devices * tiles, LANES), jnp.float32),
            pltpu.VMEM((reps * dp_count, quarter), jnp.bfloat16),
            pltpu.VMEM((4, per_set * LANES, LANES), jnp.float32),
            pltpu.SemaphoreType.DMA((4,)),
        ],
        compiler_params=params,
        name="gram_tiles",
    )(got)

    cores = [(0, 1), (1, 0), (2, 3), (3, 2)]
    across = [(0, 2), (2, 0), (1, 3), (3, 1)]
    core_far = lax.ppermute(send_far, "rep", cores)
    far = lax.ppermute(keep_far + core_far, "rep", across)
    core_near = lax.ppermute(send_near, "rep", cores)

    sums = pl.pallas_call(
        functools.partial(score_kernel, dp_count, devices),
        in_specs=[vmem] * 3,
        out_specs=vmem,
        out_shape=jax.ShapeDtypeStruct((devices, LANES), jnp.float32),
        scratch_shapes=[pltpu.VMEM((-(-group // 8) * 8, LANES), jnp.float32)],
        compiler_params=params,
        name="score_tiles",
    )(keep_near, core_near, far)

    back = lax.all_to_all(sums, ALL, split_axis=0, concat_axis=0, tiled=True)
    keep = pl.pallas_call(
        functools.partial(final_kernel, clusters, reps),
        in_specs=[vmem] * 2,
        out_specs=vmem,
        out_shape=jax.ShapeDtypeStruct((blocks, LANES), jnp.float32),
        compiler_params=params,
        name="final_keep",
    )(slots, back)
    return keep.reshape(rows_dev)


def solution(mesh):
    placed = (P(ALL, None), P(ALL), P(ALL), P(), P())
    return jax.shard_map(local, mesh=mesh, in_specs=placed, out_specs=P(ALL), check_vma=False)
```

```python
import functools

import jax
import jax.numpy as jnp
from jax import lax
from jax.experimental import pallas as pl
from jax.experimental.pallas import tpu as pltpu
from jax.sharding import PartitionSpec as P

CAPS = 24
LANES = 128
ALL = ("dp", "rep")
FEATURE_STEP = 512
EMPTY_MARK = 4.0
PENALTY = -1000.0
SPARE_BYTES = 6 * 1024 * 1024
SELECT_BYTES = 57 * 1024 * 1024

slope_gain = 64.0
inner_cut = 0.12
edge_cut = 0.06


def each(count, body, limit=8):
    if count <= limit:
        for index in range(count):
            body(index)
    else:

        def step(index, carry):
            body(index)
            return carry

        lax.fori_loop(0, count, step, 0)


def grant(size):
    return pltpu.CompilerParams(vmem_limit_bytes=size + SPARE_BYTES)


def iota(shape, dim):
    return lax.broadcasted_iota(jnp.int32, shape, dim)


def select_kernel(
    clusters,
    reps,
    cap,
    adjacent,
    mask,
    assign,
    rows,
    out,
    slots,
    data,
    pick,
    filled,
    chosen,
    squares,
    staged,
    in_sem,
    out_sem,
):
    steps, _, wide = data.shape
    reads = [
        pltpu.make_async_copy(rows.at[:, i * wide : (i + 1) * wide], data.at[i], in_sem.at[i])
        for i in range(steps)
    ]
    for read in reads:
        read.start()

    blocks = assign.shape[0]
    depth = chosen.shape[1]
    count = pick.shape[0]
    base = clusters * CAPS
    table = assign[...]
    sub = iota(table.shape, 0)
    active = jnp.zeros(table.shape, jnp.int32)
    for block in range(blocks):
        active = jnp.where(sub == block, mask[block], active)
    live = jnp.where(active == 1, table, -1)
    members = jnp.concatenate(
        [(live == c).astype(jnp.float32) for c in range(clusters)], axis=0
    ).astype(jnp.bfloat16)
    total = clusters * blocks
    earlier = (iota((LANES, LANES), 0) < iota((LANES, LANES), 1)).astype(jnp.bfloat16)
    within = jnp.dot(members, earlier, preferred_element_type=jnp.float32)
    left, right = iota((total, total), 0), iota((total, total), 1)
    same = (left // blocks == right // blocks) & (right < left)
    sums = jnp.dot(
        same.astype(jnp.bfloat16), members, preferred_element_type=jnp.float32
    ).astype(jnp.bfloat16)
    before = jnp.dot(
        sums, jnp.ones((LANES, LANES), jnp.bfloat16), preferred_element_type=jnp.float32
    )
    rank = (within + before).astype(jnp.int32)
    slot = jnp.full(table.shape, -1, jnp.int32)
    for c in range(clusters):
        own = rank[c * blocks : (c + 1) * blocks]
        slot = jnp.where((live == c) & (own < cap[c]), c * CAPS + own, slot)
    slots[...] = slot
    place = iota((count, LANES), 0)
    target = jnp.where(place < base, place, -7)
    for c in range(clusters):
        target = jnp.where(place == base + c, adjacent[c] * CAPS, target)
    seen = jnp.zeros((count, LANES), jnp.float32)
    for block in range(blocks):
        hit = (target == slot[block : block + 1]).astype(jnp.float32)
        pick[:, block * LANES : (block + 1) * LANES] = hit.astype(jnp.bfloat16)
        seen += hit
    mark = jnp.sum(seen, axis=1, keepdims=True) < 0.5
    mark = mark & (iota(filled.shape, 1) == 0)
    filled[...] = jnp.where(mark, EMPTY_MARK, 0.0)

    power = jnp.zeros(squares.shape, jnp.float32)
    for i, read in enumerate(reads):
        read.wait()
        part = jnp.dot(pick[...], data[i], preferred_element_type=jnp.float32)
        chosen[:, i * wide : (i + 1) * wide] = part
        for k in range(wide // LANES):
            piece = part[:, k * LANES : (k + 1) * LANES]
            power += piece * piece

    scale = lax.rsqrt(jnp.sum(power, axis=1, keepdims=True) + 1e-06)
    squares[...] = jnp.broadcast_to(scale, squares.shape)
    quarter = depth // reps
    tiles = quarter // LANES
    sub = iota((tiles, LANES), 0)

    def write(c):
        at = pl.ds(c * reps, reps)
        return pltpu.make_async_copy(staged.at[at], out.at[at], out_sem.at[c])

    def eight(group):
        near = pl.ds(pl.multiple_of(base + group * 8, 8), 8)
        near_gain, near_flag = squares[near, :], filled[near, :]
        for k in range(8):
            c = group * 8 + k
            at = pl.ds(pl.multiple_of(c * CAPS, 8), CAPS)
            gain, flag = squares[at, :], filled[at, :]
            for q in range(reps):
                pieces = []
                edge = jnp.zeros((tiles, LANES), jnp.float32)
                for t in range(tiles):
                    cols = slice(q * quarter + t * LANES, q * quarter + (t + 1) * LANES)
                    piece = chosen[at, cols] * gain
                    line = chosen[near, cols] * near_gain
                    if t == 0:
                        piece += flag
                        line += near_flag
                    pieces.append(piece)
                    line = jnp.broadcast_to(line[k : k + 1], edge.shape)
                    edge = jnp.where(sub == t, line, edge)
                pieces.append(edge)
                chunk = jnp.concatenate(pieces, axis=0).astype(jnp.bfloat16)
                staged[c * reps + q] = chunk
            write(c).start()

    each(clusters // 8, eight, 1)
    for c in range(clusters):
        write(c).wait()


def gram_kernel(
    ranks, per_set, got, send_far, send_near, keep_far, keep_near, x, edge_rows, edge_x, hold, sem
):
    sources = got.shape[0]
    count, quarter = x.shape
    tiles = quarter // LANES
    blocks = count // LANES
    reps = 4
    main = tiles * CAPS
    me = lax.axis_index("rep")
    my_core, my_y = me % 2, me // 2

    def gather(pair):
        values = [got[2 * pair + k].astype(jnp.float32) for k in range(2)]
        for k in range(2):
            edge_rows[pl.ds((2 * pair + k) * tiles, tiles), :] = values[k][main:]
        for k in range(tiles):
            rows = slice(k * CAPS, (k + 1) * CAPS)
            both = jnp.concatenate([v[rows] for v in values], axis=0)
            x[pl.ds(pair * 2 * CAPS, 2 * CAPS), k * LANES : (k + 1) * LANES] = both.astype(
                jnp.bfloat16
            )

    each(sources // 2, gather, 16)

    for lane in range(reps):
        edge_x[lane * ranks : (lane + 1) * ranks, :] = jnp.concatenate(
            [
                edge_rows[pl.ds(lane * tiles + k, ranks, stride=reps * tiles), :]
                for k in range(tiles)
            ],
            axis=1,
        ).astype(jnp.bfloat16)

    first = (iota((8, LANES), 1) == 0).astype(jnp.bfloat16)
    contract = (((1,), (1,)), ((), ()))
    marks = lax.dot_general(first, x[:, :LANES], contract, preferred_element_type=jnp.float32)
    col_pen = jnp.where(marks[:1] > 2.0, PENALTY, 0.0)

    def put(index, value):
        owner, place = index % reps, index // reps
        slot = 2 * (my_core == owner % 2).astype(jnp.int32) + (my_y == owner // 2).astype(jnp.int32)
        hold[slot, place * LANES : place * LANES + value.shape[0], :] = value

    index = 0
    step = 2 * LANES
    for start in range(0, count, step):
        rows = x[start : start + step, :]
        gram = lax.dot_general(rows, x[start:, :], contract, preferred_element_type=jnp.float32)
        row_pen = jnp.where(rows[:, :1].astype(jnp.float32) > 2.0, PENALTY, 0.0)
        gram = gram + row_pen + col_pen[:, start:]
        shape = (LANES, LANES)
        for half in range(2):
            for tile in range(half, (count - start) // LANES):
                value = gram[
                    half * LANES : (half + 1) * LANES, tile * LANES : (tile + 1) * LANES
                ]
                if tile == half:
                    value = jnp.where(iota(shape, 0) == iota(shape, 1), PENALTY, value)
                put(index, value)
                index += 1

    near = edge_x[...]
    edge = lax.dot_general(near, x[...], contract, preferred_element_type=jnp.float32)
    edge = edge + jnp.where(near[:, :1].astype(jnp.float32) > 2.0, PENALTY, 0.0)
    lane_of = lax.rem(lax.div(iota((ranks, count), 1), CAPS), reps)
    small = edge[:ranks]
    for lane in range(1, reps):
        small = jnp.where(lane_of == lane, edge[lane * ranks : (lane + 1) * ranks], small)
    per_tile = LANES // ranks
    for first_block in range(0, blocks, per_tile):
        stop = min(blocks, first_block + per_tile)
        put(
            index,
            jnp.concatenate(
                [small[:, b * LANES : (b + 1) * LANES] for b in range(first_block, stop)], axis=0
            ),
        )
        index += 1

    copies = [
        pltpu.make_async_copy(hold.at[k], ref, sem.at[k])
        for k, ref in enumerate((send_far, send_near, keep_far, keep_near))
    ]
    for copy in copies:
        copy.start()
    for copy in copies:
        copy.wait()


def score_kernel(ranks, sources, keep, core, far, out, total):
    count = sources * CAPS
    blocks = count // LANES
    reps = 4
    me = lax.axis_index("rep")
    pairs = [(i, j) for i in range(blocks) for j in range(i, blocks)]
    total[...] = jnp.zeros_like(total)

    def value(place, size):
        at = slice(place * LANES, place * LANES + size)
        return keep[at, :] + core[at, :] + far[at, :]

    def by_rep(values):
        picked = jnp.int32(values[0])
        for k in range(1, len(values)):
            picked = jnp.where(me == k, jnp.int32(values[k]), picked)
        return picked

    def tile(place):
        options = [pairs[min(place * reps + k, len(pairs) - 1)] for k in range(reps)]
        i, j = by_rep([p[0] for p in options]), by_rep([p[1] for p in options])
        weight = jax.nn.sigmoid(slope_gain * (value(place, LANES) - inner_cut))
        total[pl.ds(i, 1), :] += jnp.sum(weight.T, axis=0, keepdims=True)
        other = (i != j).astype(jnp.float32)
        total[pl.ds(j, 1), :] += jnp.sum(weight, axis=0, keepdims=True) * other

    per_set = -(-len(pairs) // reps)
    for place in range(per_set):
        if (place + 1) * reps <= len(pairs):
            tile(place)
        else:
            pl.when(place * reps + me < len(pairs))(functools.partial(tile, place))

    per_tile = LANES // ranks
    for e, first_block in enumerate(range(0, blocks, per_tile)):
        owner, place = (len(pairs) + e) % reps, (len(pairs) + e) // reps
        stop = min(blocks, first_block + per_tile)

        @pl.when(me == owner)
        def _(place=place, first_block=first_block, stop=stop):
            edge = value(place, (stop - first_block) * ranks)
            edge = jax.nn.sigmoid(slope_gain * (edge - edge_cut))
            for b in range(first_block, stop):
                at = (b - first_block) * ranks
                total[b : b + 1, :] += jnp.sum(edge[at : at + ranks], axis=0, keepdims=True)

    result = jnp.zeros((sources, LANES), jnp.float32)
    for b in range(blocks):
        where = iota((sources, LANES), 1) + b * LANES
        mine = lax.div(where, CAPS) == iota((sources, LANES), 0)
        spread = jnp.where(mine, total[b : b + 1, :], 0.0)
        move = lax.rem(iota((LANES, LANES), 0) + b * LANES, CAPS) == iota((LANES, LANES), 1)
        result += jnp.dot(
            spread,
            move.astype(jnp.float32),
            precision=lax.Precision.HIGHEST,
            preferred_element_type=jnp.float32,
        )
    out[...] = result


def final_kernel(clusters, reps, slots, sums, out):
    slot = slots[...]
    result = jnp.ones(slot.shape, jnp.float32)
    for c in range(clusters):
        inner = jnp.sum(sums[c * reps : (c + 1) * reps, :], axis=0, keepdims=True)
        keep = jnp.broadcast_to(1.0 / (1.0 + inner), slot.shape)
        rank = slot - c * CAPS
        mine = (rank >= 0) & (rank < CAPS)
        found = jnp.take_along_axis(keep, jnp.where(mine, rank, 0), axis=1)
        result = jnp.where(mine, found, result)
    out[...] = result


def local(embeddings, assignment, block_mask, cluster_cap, adjacent):
    dp_count, reps = lax.axis_size("dp"), lax.axis_size("rep")
    devices = dp_count * reps
    rows_dev, depth = embeddings.shape
    blocks = block_mask.shape[0]
    clusters = cluster_cap.shape[0]
    quarter = depth // reps
    tiles = quarter // LANES
    chunk = tiles * CAPS + tiles
    picks = -(-(clusters * (CAPS + 1)) // 16) * 16
    steps = depth // FEATURE_STEP
    smem = pl.BlockSpec(memory_space=pltpu.SMEM)
    vmem = pl.BlockSpec(memory_space=pltpu.VMEM)
    anywhere = pl.BlockSpec(memory_space=pl.ANY)

    send, slots = pl.pallas_call(
        functools.partial(select_kernel, clusters, reps),
        in_specs=[smem, smem, smem, vmem, anywhere],
        out_specs=[anywhere, vmem],
        out_shape=[
            jax.ShapeDtypeStruct((devices, chunk, LANES), jnp.bfloat16),
            jax.ShapeDtypeStruct((blocks, LANES), jnp.int32),
        ],
        scratch_shapes=[
            pltpu.VMEM((steps, rows_dev, FEATURE_STEP), jnp.bfloat16),
            pltpu.VMEM((picks, rows_dev), jnp.bfloat16),
            pltpu.VMEM((picks, LANES), jnp.float32),
            pltpu.VMEM((picks, depth), jnp.float32),
            pltpu.VMEM((picks, LANES), jnp.float32),
            pltpu.VMEM((devices, chunk, LANES), jnp.bfloat16),
            pltpu.SemaphoreType.DMA((steps,)),
            pltpu.SemaphoreType.DMA((clusters,)),
        ],
        compiler_params=pltpu.CompilerParams(vmem_limit_bytes=SELECT_BYTES),
        name="select_rows",
    )(cluster_cap, adjacent, block_mask, assignment.reshape(blocks, LANES), embeddings)

    got = lax.all_to_all(send, ALL, split_axis=0, concat_axis=0, tiled=True)

    count = devices * CAPS
    group = count // LANES
    pairs = group * (group + 1) // 2
    edge_tiles = -(-group // (LANES // dp_count))
    per_set = -(-(pairs + edge_tiles) // reps)
    part = jax.ShapeDtypeStruct((per_set * LANES, LANES), jnp.float32)
    send_far, send_near, keep_far, keep_near = pl.pallas_call(
        functools.partial(gram_kernel, dp_count, per_set),
        in_specs=[vmem],
        out_specs=[anywhere] * 4,
        out_shape=[part] * 4,
        scratch_shapes=[
            pltpu.VMEM((count, quarter), jnp.bfloat16),
            pltpu.VMEM((devices * tiles, LANES), jnp.float32),
            pltpu.VMEM((reps * dp_count, quarter), jnp.bfloat16),
            pltpu.VMEM((4, per_set * LANES, LANES), jnp.float32),
            pltpu.SemaphoreType.DMA((4,)),
        ],
        compiler_params=grant(6 * count * quarter + 4 * per_set * LANES * LANES * 4),
        name="gram_tiles",
    )(got)

    cores = [(0, 1), (1, 0), (2, 3), (3, 2)]
    across = [(0, 2), (2, 0), (1, 3), (3, 1)]
    core_far = lax.ppermute(send_far, "rep", cores)
    far = lax.ppermute((keep_far + core_far).astype(jnp.float16), "rep", across)
    core_near = lax.ppermute(send_near, "rep", cores)

    sums = pl.pallas_call(
        functools.partial(score_kernel, dp_count, devices),
        in_specs=[vmem] * 3,
        out_specs=vmem,
        out_shape=jax.ShapeDtypeStruct((devices, LANES), jnp.float32),
        scratch_shapes=[pltpu.VMEM((-(-group // 8) * 8, LANES), jnp.float32)],
        compiler_params=grant(3 * per_set * LANES * LANES * 4),
        name="score_tiles",
    )(keep_near, core_near, far.astype(jnp.float32))

    back = lax.all_to_all(sums, ALL, split_axis=0, concat_axis=0, tiled=True)
    keep = pl.pallas_call(
        functools.partial(final_kernel, clusters, reps),
        in_specs=[vmem] * 2,
        out_specs=vmem,
        out_shape=jax.ShapeDtypeStruct((blocks, LANES), jnp.float32),
        compiler_params=grant(0),
        name="final_keep",
    )(slots, back)
    return keep.reshape(rows_dev)


def solution(mesh):
    placed = (P(ALL, None), P(ALL), P(ALL), P(), P())
    return jax.shard_map(local, mesh=mesh, in_specs=placed, out_specs=P(ALL), check_vma=False)
```

```python
import functools

import jax
import jax.numpy as jnp
from jax import lax
from jax.experimental import pallas as pl
from jax.experimental.pallas import tpu as pltpu
from jax.sharding import PartitionSpec as P

CAPS = 24
LANES = 128
ALL = ("dp", "rep")
FEATURE_STEP = 512
ROW_STEP = 256
EMPTY_MARK = 4.0
PENALTY = -1000.0
SPARE_BYTES = 6 * 1024 * 1024
SELECT_BYTES = 48 * 1024 * 1024

slope_gain = 64.0
inner_cut = 0.12
edge_cut = 0.06


def each(count, body, limit=8):
    if count <= limit:
        for index in range(count):
            body(index)
    else:

        def step(index, carry):
            body(index)
            return carry

        lax.fori_loop(0, count, step, 0)


def grant(size):
    return pltpu.CompilerParams(vmem_limit_bytes=size + SPARE_BYTES)


def iota(shape, dim):
    return lax.broadcasted_iota(jnp.int32, shape, dim)


def select_kernel(
    clusters,
    reps,
    cap,
    adjacent,
    mask,
    assign,
    rows,
    out,
    slots,
    data,
    pick,
    filled,
    chosen,
    squares,
    in_sem,
):
    steps, deep, _ = data.shape
    reads = [
        pltpu.make_async_copy(rows.at[i * deep : (i + 1) * deep, :], data.at[i], in_sem.at[i])
        for i in range(steps)
    ]
    for read in reads:
        read.start()

    blocks = assign.shape[0]
    depth = chosen.shape[1]
    count = pick.shape[0]
    base = clusters * CAPS
    table = assign[...]
    sub = iota(table.shape, 0)
    active = jnp.zeros(table.shape, jnp.int32)
    for block in range(blocks):
        active = jnp.where(sub == block, mask[block], active)
    live = jnp.where(active == 1, table, -1)
    members = jnp.concatenate(
        [(live == c).astype(jnp.float32) for c in range(clusters)], axis=0
    ).astype(jnp.bfloat16)
    total = clusters * blocks
    earlier = (iota((LANES, LANES), 0) < iota((LANES, LANES), 1)).astype(jnp.bfloat16)
    within = jnp.dot(members, earlier, preferred_element_type=jnp.float32)
    left, right = iota((total, total), 0), iota((total, total), 1)
    same = (left // blocks == right // blocks) & (right < left)
    sums = jnp.dot(
        same.astype(jnp.bfloat16), members, preferred_element_type=jnp.float32
    ).astype(jnp.bfloat16)
    before = jnp.dot(
        sums, jnp.ones((LANES, LANES), jnp.bfloat16), preferred_element_type=jnp.float32
    )
    rank = (within + before).astype(jnp.int32)
    slot = jnp.full(table.shape, -1, jnp.int32)
    for c in range(clusters):
        own = rank[c * blocks : (c + 1) * blocks]
        slot = jnp.where((live == c) & (own < cap[c]), c * CAPS + own, slot)
    slots[...] = slot
    place = iota((count, LANES), 0)
    target = jnp.where(place < base, place, -7)
    for c in range(clusters):
        target = jnp.where(place == base + c, adjacent[c] * CAPS, target)
    seen = jnp.zeros((count, LANES), jnp.float32)
    for block in range(blocks):
        hit = (target == slot[block : block + 1]).astype(jnp.float32)
        pick[:, block * LANES : (block + 1) * LANES] = hit.astype(jnp.bfloat16)
        seen += hit
    mark = jnp.sum(seen, axis=1, keepdims=True) < 0.5
    mark = mark & (iota(filled.shape, 1) == 0)
    filled[...] = jnp.where(mark, EMPTY_MARK, 0.0)

    power = jnp.zeros(squares.shape, jnp.float32)
    for i, read in enumerate(reads):
        read.wait()
        chunk_pick = pick[:, i * deep : (i + 1) * deep]
        for start in range(0, depth, FEATURE_STEP):
            cols = slice(start, start + FEATURE_STEP)
            part = jnp.dot(chunk_pick, data[i, :, cols], preferred_element_type=jnp.float32)
            if i:
                part += chosen[:, cols]
            chosen[:, cols] = part
            if i == steps - 1:
                for k in range(FEATURE_STEP // LANES):
                    piece = part[:, k * LANES : (k + 1) * LANES]
                    power += piece * piece

    scale = lax.rsqrt(jnp.sum(power, axis=1, keepdims=True) + 1e-06)
    squares[...] = jnp.broadcast_to(scale, squares.shape)
    quarter = depth // reps
    tiles = quarter // LANES
    sub = iota((tiles, LANES), 0)

    def eight(group):
        near = pl.ds(pl.multiple_of(base + group * 8, 8), 8)
        near_gain, near_flag = squares[near, :], filled[near, :]
        for k in range(8):
            c = group * 8 + k
            at = pl.ds(pl.multiple_of(c * CAPS, 8), CAPS)
            gain, flag = squares[at, :], filled[at, :]
            for q in range(reps):
                pieces = []
                edge = jnp.zeros((tiles, LANES), jnp.float32)
                for t in range(tiles):
                    cols = slice(q * quarter + t * LANES, q * quarter + (t + 1) * LANES)
                    piece = chosen[at, cols] * gain
                    line = chosen[near, cols] * near_gain
                    if t == 0:
                        piece += flag
                        line += near_flag
                    pieces.append(piece)
                    line = jnp.broadcast_to(line[k : k + 1], edge.shape)
                    edge = jnp.where(sub == t, line, edge)
                pieces.append(edge)
                chunk = jnp.concatenate(pieces, axis=0).astype(jnp.bfloat16)
                out[c * reps + q] = chunk

    each(clusters // 8, eight, 1)


def gram_kernel(
    ranks, per_set, got, send_far, send_near, keep_far, keep_near, x, edge_rows, edge_x, hold, sem
):
    sources = got.shape[0]
    count, quarter = x.shape
    tiles = quarter // LANES
    blocks = count // LANES
    reps = 4
    main = tiles * CAPS
    me = lax.axis_index("rep")
    my_core, my_y = me % 2, me // 2

    def gather(pair):
        values = [got[2 * pair + k].astype(jnp.float32) for k in range(2)]
        for k in range(2):
            edge_rows[pl.ds((2 * pair + k) * tiles, tiles), :] = values[k][main:]
        for k in range(tiles):
            rows = slice(k * CAPS, (k + 1) * CAPS)
            both = jnp.concatenate([v[rows] for v in values], axis=0)
            x[pl.ds(pair * 2 * CAPS, 2 * CAPS), k * LANES : (k + 1) * LANES] = both.astype(
                jnp.bfloat16
            )

    each(sources // 2, gather, 16)

    for lane in range(reps):
        edge_x[lane * ranks : (lane + 1) * ranks, :] = jnp.concatenate(
            [
                edge_rows[pl.ds(lane * tiles + k, ranks, stride=reps * tiles), :]
                for k in range(tiles)
            ],
            axis=1,
        ).astype(jnp.bfloat16)

    first = (iota((8, LANES), 1) == 0).astype(jnp.bfloat16)
    contract = (((1,), (1,)), ((), ()))
    marks = lax.dot_general(first, x[:, :LANES], contract, preferred_element_type=jnp.float32)
    col_pen = jnp.where(marks[:1] > 2.0, PENALTY, 0.0)

    def put(index, value):
        owner, place = index % reps, index // reps
        slot = 2 * (my_core == owner % 2).astype(jnp.int32) + (my_y == owner // 2).astype(jnp.int32)
        hold[slot, place * LANES : place * LANES + value.shape[0], :] = value

    index = 0
    step = 2 * LANES
    for start in range(0, count, step):
        rows = x[start : start + step, :]
        gram = lax.dot_general(rows, x[start:, :], contract, preferred_element_type=jnp.float32)
        row_pen = jnp.where(rows[:, :1].astype(jnp.float32) > 2.0, PENALTY, 0.0)
        gram = gram + row_pen + col_pen[:, start:]
        shape = (LANES, LANES)
        for half in range(2):
            for tile in range(half, (count - start) // LANES):
                value = gram[
                    half * LANES : (half + 1) * LANES, tile * LANES : (tile + 1) * LANES
                ]
                if tile == half:
                    value = jnp.where(iota(shape, 0) == iota(shape, 1), PENALTY, value)
                put(index, value)
                index += 1

    near = edge_x[...]
    edge = lax.dot_general(near, x[...], contract, preferred_element_type=jnp.float32)
    edge = edge + jnp.where(near[:, :1].astype(jnp.float32) > 2.0, PENALTY, 0.0)
    lane_of = lax.rem(lax.div(iota((ranks, count), 1), CAPS), reps)
    small = edge[:ranks]
    for lane in range(1, reps):
        small = jnp.where(lane_of == lane, edge[lane * ranks : (lane + 1) * ranks], small)
    per_tile = LANES // ranks
    for first_block in range(0, blocks, per_tile):
        stop = min(blocks, first_block + per_tile)
        put(
            index,
            jnp.concatenate(
                [small[:, b * LANES : (b + 1) * LANES] for b in range(first_block, stop)], axis=0
            ),
        )
        index += 1

    copies = [
        pltpu.make_async_copy(hold.at[k], ref, sem.at[k])
        for k, ref in enumerate((send_far, send_near, keep_far, keep_near))
    ]
    for copy in copies:
        copy.start()
    for copy in copies:
        copy.wait()


def score_kernel(ranks, sources, keep, core, far, out, total):
    count = sources * CAPS
    blocks = count // LANES
    reps = 4
    me = lax.axis_index("rep")
    pairs = [(i, j) for i in range(blocks) for j in range(i, blocks)]
    total[...] = jnp.zeros_like(total)

    def value(place, size):
        at = slice(place * LANES, place * LANES + size)
        return keep[at, :] + core[at, :] + far[at, :]

    def by_rep(values):
        picked = jnp.int32(values[0])
        for k in range(1, len(values)):
            picked = jnp.where(me == k, jnp.int32(values[k]), picked)
        return picked

    def tile(place):
        options = [pairs[min(place * reps + k, len(pairs) - 1)] for k in range(reps)]
        i, j = by_rep([p[0] for p in options]), by_rep([p[1] for p in options])
        weight = jax.nn.sigmoid(slope_gain * (value(place, LANES) - inner_cut))
        total[pl.ds(i, 1), :] += jnp.sum(weight.T, axis=0, keepdims=True)
        other = (i != j).astype(jnp.float32)
        total[pl.ds(j, 1), :] += jnp.sum(weight, axis=0, keepdims=True) * other

    per_set = -(-len(pairs) // reps)
    for place in range(per_set):
        if (place + 1) * reps <= len(pairs):
            tile(place)
        else:
            pl.when(place * reps + me < len(pairs))(functools.partial(tile, place))

    per_tile = LANES // ranks
    for e, first_block in enumerate(range(0, blocks, per_tile)):
        owner, place = (len(pairs) + e) % reps, (len(pairs) + e) // reps
        stop = min(blocks, first_block + per_tile)

        @pl.when(me == owner)
        def _(place=place, first_block=first_block, stop=stop):
            edge = value(place, (stop - first_block) * ranks)
            edge = jax.nn.sigmoid(slope_gain * (edge - edge_cut))
            for b in range(first_block, stop):
                at = (b - first_block) * ranks
                total[b : b + 1, :] += jnp.sum(edge[at : at + ranks], axis=0, keepdims=True)

    result = jnp.zeros((sources, LANES), jnp.float32)
    for b in range(blocks):
        where = iota((sources, LANES), 1) + b * LANES
        mine = lax.div(where, CAPS) == iota((sources, LANES), 0)
        spread = jnp.where(mine, total[b : b + 1, :], 0.0)
        move = lax.rem(iota((LANES, LANES), 0) + b * LANES, CAPS) == iota((LANES, LANES), 1)
        result += jnp.dot(
            spread,
            move.astype(jnp.float32),
            precision=lax.Precision.HIGHEST,
            preferred_element_type=jnp.float32,
        )
    out[...] = result


def final_kernel(clusters, reps, slots, sums, out):
    slot = slots[...]
    result = jnp.ones(slot.shape, jnp.float32)
    for c in range(clusters):
        inner = jnp.sum(sums[c * reps : (c + 1) * reps, :], axis=0, keepdims=True)
        keep = jnp.broadcast_to(1.0 / (1.0 + inner), slot.shape)
        rank = slot - c * CAPS
        mine = (rank >= 0) & (rank < CAPS)
        found = jnp.take_along_axis(keep, jnp.where(mine, rank, 0), axis=1)
        result = jnp.where(mine, found, result)
    out[...] = result


def local(embeddings, assignment, block_mask, cluster_cap, adjacent):
    dp_count, reps = lax.axis_size("dp"), lax.axis_size("rep")
    devices = dp_count * reps
    rows_dev, depth = embeddings.shape
    blocks = block_mask.shape[0]
    clusters = cluster_cap.shape[0]
    quarter = depth // reps
    tiles = quarter // LANES
    chunk = tiles * CAPS + tiles
    picks = -(-(clusters * (CAPS + 1)) // 16) * 16
    steps = rows_dev // ROW_STEP
    smem = pl.BlockSpec(memory_space=pltpu.SMEM)
    vmem = pl.BlockSpec(memory_space=pltpu.VMEM)
    anywhere = pl.BlockSpec(memory_space=pl.ANY)

    inputs = (
        cluster_cap, adjacent, block_mask, assignment.reshape(blocks, LANES), embeddings
    )
    send, slots = pl.pallas_call(
        functools.partial(select_kernel, clusters, reps),
        in_specs=[smem, smem, smem, vmem, anywhere],
        out_specs=[vmem, vmem],
        out_shape=[
            jax.ShapeDtypeStruct((devices, chunk, LANES), jnp.bfloat16),
            jax.ShapeDtypeStruct((blocks, LANES), jnp.int32),
        ],
        scratch_shapes=[
            pltpu.VMEM((steps, ROW_STEP, depth), jnp.bfloat16),
            pltpu.VMEM((picks, rows_dev), jnp.bfloat16),
            pltpu.VMEM((picks, LANES), jnp.float32),
            pltpu.VMEM((picks, depth), jnp.float32),
            pltpu.VMEM((picks, LANES), jnp.float32),
            pltpu.SemaphoreType.DMA((steps,)),
        ],
        compiler_params=pltpu.CompilerParams(vmem_limit_bytes=SELECT_BYTES),
        name="select_rows",
    )(*[pltpu.with_memory_space_constraint(x, pltpu.HBM) for x in inputs])

    got = lax.all_to_all(send, ALL, split_axis=0, concat_axis=0, tiled=True)

    count = devices * CAPS
    group = count // LANES
    pairs = group * (group + 1) // 2
    edge_tiles = -(-group // (LANES // dp_count))
    per_set = -(-(pairs + edge_tiles) // reps)
    part = jax.ShapeDtypeStruct((per_set * LANES, LANES), jnp.float32)
    send_far, send_near, keep_far, keep_near = pl.pallas_call(
        functools.partial(gram_kernel, dp_count, per_set),
        in_specs=[vmem],
        out_specs=[anywhere] * 4,
        out_shape=[part] * 4,
        scratch_shapes=[
            pltpu.VMEM((count, quarter), jnp.bfloat16),
            pltpu.VMEM((devices * tiles, LANES), jnp.float32),
            pltpu.VMEM((reps * dp_count, quarter), jnp.bfloat16),
            pltpu.VMEM((4, per_set * LANES, LANES), jnp.float32),
            pltpu.SemaphoreType.DMA((4,)),
        ],
        compiler_params=grant(6 * count * quarter + 4 * per_set * LANES * LANES * 4),
        name="gram_tiles",
    )(got)

    cores = [(0, 1), (1, 0), (2, 3), (3, 2)]
    across = [(0, 2), (2, 0), (1, 3), (3, 1)]
    core_far = lax.ppermute(send_far, "rep", cores)
    far = lax.ppermute((keep_far + core_far).astype(jnp.float16), "rep", across)
    core_near = lax.ppermute(send_near, "rep", cores)

    sums = pl.pallas_call(
        functools.partial(score_kernel, dp_count, devices),
        in_specs=[vmem] * 3,
        out_specs=vmem,
        out_shape=jax.ShapeDtypeStruct((devices, LANES), jnp.float32),
        scratch_shapes=[pltpu.VMEM((-(-group // 8) * 8, LANES), jnp.float32)],
        compiler_params=grant(3 * per_set * LANES * LANES * 4),
        name="score_tiles",
    )(keep_near, core_near, far.astype(jnp.float32))

    back = lax.all_to_all(sums, ALL, split_axis=0, concat_axis=0, tiled=True)
    keep = pl.pallas_call(
        functools.partial(final_kernel, clusters, reps),
        in_specs=[vmem] * 2,
        out_specs=vmem,
        out_shape=jax.ShapeDtypeStruct((blocks, LANES), jnp.float32),
        compiler_params=grant(0),
        name="final_keep",
    )(slots, back)
    return keep.reshape(rows_dev)


def solution(mesh):
    placed = (P(ALL, None), P(ALL), P(ALL), P(), P())
    return jax.shard_map(local, mesh=mesh, in_specs=placed, out_specs=P(ALL), check_vma=False)
```

```python
import functools

import jax
import jax.numpy as jnp
from jax import lax
from jax.experimental import pallas as pl
from jax.experimental.pallas import tpu as pltpu
from jax.sharding import PartitionSpec as P

CAPS = 24
LANES = 128
ALL = ("dp", "rep")
FEATURE_STEP = 512
ROW_STEP = 256
EMPTY_MARK = 4.0
PENALTY = -1000.0
SPARE_BYTES = 6 * 1024 * 1024
SELECT_BYTES = 48 * 1024 * 1024

slope_gain = 64.0
inner_cut = 0.12
edge_cut = 0.06


def each(count, body, limit=8):
    if count <= limit:
        for index in range(count):
            body(index)
    else:

        def step(index, carry):
            body(index)
            return carry

        lax.fori_loop(0, count, step, 0)


def grant(size):
    return pltpu.CompilerParams(vmem_limit_bytes=size + SPARE_BYTES)


def iota(shape, dim):
    return lax.broadcasted_iota(jnp.int32, shape, dim)


def select_kernel(
    clusters,
    reps,
    cap,
    adjacent,
    mask,
    assign,
    rows,
    out,
    slots,
    data,
    pick,
    filled,
    chosen,
    squares,
    in_sem,
):
    steps, deep, _ = data.shape
    reads = [
        pltpu.make_async_copy(rows.at[i * deep : (i + 1) * deep, :], data.at[i], in_sem.at[i])
        for i in range(steps)
    ]
    for read in reads:
        read.start()

    blocks = assign.shape[0]
    depth = chosen.shape[1]
    count = pick.shape[0]
    base = clusters * CAPS
    table = assign[...]
    sub = iota(table.shape, 0)
    active = jnp.zeros(table.shape, jnp.int32)
    for block in range(blocks):
        active = jnp.where(sub == block, mask[block], active)
    live = jnp.where(active == 1, table, -1)
    members = jnp.concatenate(
        [(live == c).astype(jnp.float32) for c in range(clusters)], axis=0
    ).astype(jnp.bfloat16)
    total = clusters * blocks
    earlier = (iota((LANES, LANES), 0) < iota((LANES, LANES), 1)).astype(jnp.bfloat16)
    within = jnp.dot(members, earlier, preferred_element_type=jnp.float32)
    left, right = iota((total, total), 0), iota((total, total), 1)
    same = (left // blocks == right // blocks) & (right < left)
    sums = jnp.dot(
        same.astype(jnp.bfloat16), members, preferred_element_type=jnp.float32
    ).astype(jnp.bfloat16)
    before = jnp.dot(
        sums, jnp.ones((LANES, LANES), jnp.bfloat16), preferred_element_type=jnp.float32
    )
    rank = (within + before).astype(jnp.int32)
    slot = jnp.full(table.shape, -1, jnp.int32)
    for c in range(clusters):
        own = rank[c * blocks : (c + 1) * blocks]
        slot = jnp.where((live == c) & (own < cap[c]), c * CAPS + own, slot)
    slots[...] = slot
    place = iota((count, LANES), 0)
    target = jnp.where(place < base, place, -7)
    for c in range(clusters):
        target = jnp.where(place == base + c, adjacent[c] * CAPS, target)
    seen = jnp.zeros((count, LANES), jnp.float32)
    for block in range(blocks):
        hit = (target == slot[block : block + 1]).astype(jnp.float32)
        pick[:, block * LANES : (block + 1) * LANES] = hit.astype(jnp.bfloat16)
        seen += hit
    mark = jnp.sum(seen, axis=1, keepdims=True) < 0.5
    mark = mark & (iota(filled.shape, 1) == 0)
    filled[...] = jnp.where(mark, EMPTY_MARK, 0.0)

    power = jnp.zeros(squares.shape, jnp.float32)
    for i, read in enumerate(reads):
        read.wait()
        chunk_pick = pick[:, i * deep : (i + 1) * deep]
        for start in range(0, depth, FEATURE_STEP):
            cols = slice(start, start + FEATURE_STEP)
            part = jnp.dot(chunk_pick, data[i, :, cols], preferred_element_type=jnp.float32)
            if i:
                part += chosen[:, cols]
            chosen[:, cols] = part
            if i == steps - 1:
                for k in range(FEATURE_STEP // LANES):
                    piece = part[:, k * LANES : (k + 1) * LANES]
                    power += piece * piece

    scale = lax.rsqrt(jnp.sum(power, axis=1, keepdims=True) + 1e-06)
    squares[...] = jnp.broadcast_to(scale, squares.shape)
    quarter = depth // reps
    tiles = quarter // LANES
    sub = iota((tiles, LANES), 0)

    def eight(group):
        near = pl.ds(pl.multiple_of(base + group * 8, 8), 8)
        near_gain, near_flag = squares[near, :], filled[near, :]
        for k in range(8):
            c = group * 8 + k
            at = pl.ds(pl.multiple_of(c * CAPS, 8), CAPS)
            gain, flag = squares[at, :], filled[at, :]
            for q in range(reps):
                pieces = []
                edge = jnp.zeros((tiles, LANES), jnp.float32)
                for t in range(tiles):
                    cols = slice(q * quarter + t * LANES, q * quarter + (t + 1) * LANES)
                    piece = chosen[at, cols] * gain
                    line = chosen[near, cols] * near_gain
                    if t == 0:
                        piece += flag
                        line += near_flag
                    pieces.append(piece)
                    line = jnp.broadcast_to(line[k : k + 1], edge.shape)
                    edge = jnp.where(sub == t, line, edge)
                pieces.append(edge)
                chunk = jnp.concatenate(pieces, axis=0).astype(jnp.bfloat16)
                out[c * reps + q] = chunk

    each(clusters // 8, eight, 1)


def tile_sets(blocks):
    tiles = []
    for p in range(0, blocks, 2):
        tiles.append((p, p + 1, True))
        tiles += [(i, j, False) for i in (p, p + 1) for j in range(i + 1, blocks)]
    half = len(tiles) // 2
    return tiles[:half], tiles[half:]


def set_rows(blocks, ranks):
    size = len(tile_sets(blocks)[0])
    edge = size // 2 * LANES + size % 2 * (LANES // 2)
    return edge, edge + -(-(blocks // 2) // 2) * ranks


def emit_tiles(y, core, ranks, x, small, out):
    count = x.shape[0]
    blocks = count // LANES
    contract = (((1,), (1,)), ((), ()))
    first = (iota((8, LANES), 1) == 0).astype(jnp.bfloat16)
    marks = lax.dot_general(first, x[:, :LANES], contract, preferred_element_type=jnp.float32)
    col_pen = jnp.where(marks[:1] > 2.0, PENALTY, 0.0)
    tiles = tile_sets(blocks)[y]
    edge_base, _ = set_rows(blocks, ranks)

    def put(owner, start, value):
        slot = (core == owner).astype(jnp.int32)
        out[slot, start : start + value.shape[0], :] = value

    for p in range(0, blocks, 2):
        mine = [(e, t) for e, t in enumerate(tiles) if t[0] // 2 == p // 2]
        if not mine:
            continue
        row0 = min(t[0] for _, t in mine)
        row1 = max(t[1] if t[2] else t[0] for _, t in mine) + 1
        col0 = min(t[0] if t[2] else t[1] for _, t in mine)
        col1 = max(t[1] for _, t in mine) + 1
        rows = x[row0 * LANES : row1 * LANES, :]
        cols = slice(col0 * LANES, col1 * LANES)
        gram = lax.dot_general(rows, x[cols, :], contract, preferred_element_type=jnp.float32)
        row_pen = jnp.where(rows[:, :1].astype(jnp.float32) > 2.0, PENALTY, 0.0)
        gram = gram + row_pen + col_pen[:, cols]

        def tile(i, j, gram=gram, row0=row0, col0=col0):
            i, j = (i - row0) * LANES, (j - col0) * LANES
            return gram[i : i + LANES, j : j + LANES]

        for e, (i, j, diagonal) in mine:
            if diagonal:
                upper = iota((LANES, LANES), 0) < iota((LANES, LANES), 1)
                value = jnp.where(upper, tile(i, i), tile(j, j))
            else:
                value = tile(i, j)
            if e == len(tiles) - 1 and len(tiles) % 2:
                half = LANES // 2
                for owner in range(2):
                    put(owner, e // 2 * LANES, value[owner * half : (owner + 1) * half])
            else:
                put(e % 2, e // 2 * LANES, value)

    for k in range(blocks // 2):
        at = (y * (blocks // 2) + k) * LANES
        put(k % 2, edge_base + k // 2 * ranks, small[:, at : at + LANES])


def gather_kernel(ranks, got, x, small, out, edge_rows, edge_x):
    sources = got.shape[0]
    count, quarter = x.shape
    tiles = quarter // LANES
    reps = 4
    main = tiles * CAPS
    me = lax.axis_index("rep")

    def gather(pair):
        values = [got[2 * pair + k].astype(jnp.float32) for k in range(2)]
        for k in range(2):
            edge_rows[pl.ds((2 * pair + k) * tiles, tiles), :] = values[k][main:]
        for k in range(tiles):
            rows = slice(k * CAPS, (k + 1) * CAPS)
            both = jnp.concatenate([v[rows] for v in values], axis=0)
            x[pl.ds(pair * 2 * CAPS, 2 * CAPS), k * LANES : (k + 1) * LANES] = both.astype(
                jnp.bfloat16
            )

    each(sources // 2, gather, 16)

    for lane in range(reps):
        edge_x[lane * ranks : (lane + 1) * ranks, :] = jnp.concatenate(
            [
                edge_rows[pl.ds(lane * tiles + k, ranks, stride=reps * tiles), :]
                for k in range(tiles)
            ],
            axis=1,
        ).astype(jnp.bfloat16)

    near = edge_x[...]
    contract = (((1,), (1,)), ((), ()))
    edge = lax.dot_general(near, x[...], contract, preferred_element_type=jnp.float32)
    edge = edge + jnp.where(near[:, :1].astype(jnp.float32) > 2.0, PENALTY, 0.0)
    lane_of = lax.rem(lax.div(iota((ranks, count), 1), CAPS), reps)
    picked = edge[:ranks]
    for lane in range(1, reps):
        picked = jnp.where(lane_of == lane, edge[lane * ranks : (lane + 1) * ranks], picked)
    small[...] = picked

    for y in range(2):
        pl.when(me // 2 != y)(
            functools.partial(emit_tiles, y, me % 2, ranks, x, small, out)
        )


def near_kernel(ranks, x, small, out):
    me = lax.axis_index("rep")
    for y in range(2):
        pl.when(me // 2 == y)(
            functools.partial(emit_tiles, y, me % 2, ranks, x, small, out)
        )


def score_kernel(ranks, sources, sums, out, total):
    count = sources * CAPS
    blocks = count // LANES
    me = lax.axis_index("rep")
    core, my_y = me % 2, me // 2
    sets = tile_sets(blocks)
    size = len(sets[0])
    edge_base, _ = set_rows(blocks, ranks)
    total[...] = jnp.zeros_like(total)
    shape = (LANES, LANES)

    def by_rep(values):
        picked = jnp.int32(values[0])
        for k in range(1, len(values)):
            picked = jnp.where(me == k, jnp.int32(values[k]), picked)
        return picked

    def weigh(value, cut):
        return jax.nn.sigmoid(slope_gain * (value - cut))

    def rows_of(weight):
        return jnp.sum(weight.T, axis=0, keepdims=True)

    def cols_of(weight):
        return jnp.sum(weight, axis=0, keepdims=True)

    def plain(i, j, weight):
        total[pl.ds(i, 1), :] += rows_of(weight)
        total[pl.ds(j, 1), :] += cols_of(weight)

    def packed(i, j, weight):
        upper = jnp.where(iota(shape, 0) < iota(shape, 1), weight, 0.0)
        lower = jnp.where(iota(shape, 0) > iota(shape, 1), weight, 0.0)
        total[pl.ds(i, 1), :] += rows_of(upper) + cols_of(upper)
        total[pl.ds(j, 1), :] += rows_of(lower) + cols_of(lower)

    for place in range(size // 2):
        options = [sets[r // 2][2 * place + r % 2] for r in range(4)]
        i, j = by_rep([t[0] for t in options]), by_rep([t[1] for t in options])
        kinds = [t[2] for t in options]
        weight = weigh(sums[place * LANES : (place + 1) * LANES, :], inner_cut)
        if not any(kinds):
            plain(i, j, weight)
        else:
            kind = by_rep([int(k) for k in kinds])
            pl.when(kind == 1)(functools.partial(packed, i, j, weight))
            pl.when(kind == 0)(functools.partial(plain, i, j, weight))
    if size % 2:
        options = [sets[r // 2][size - 1] for r in range(4)]
        i, j = by_rep([t[0] for t in options]), by_rep([t[1] for t in options])
        start = size // 2 * LANES
        weight = weigh(sums[start : start + LANES // 2, :], inner_cut)
        halves = [jnp.where(core == k, weight, 0.0) for k in range(2)]
        plain(i, j, jnp.concatenate(halves, axis=0))

    for k in range(blocks // 2):

        @pl.when(core == k % 2)
        def _(k=k):
            at = edge_base + k // 2 * ranks
            edge = weigh(sums[at : at + ranks, :], edge_cut)
            total[pl.ds(my_y * (blocks // 2) + k, 1), :] += cols_of(edge)

    result = jnp.zeros((sources, LANES), jnp.float32)
    for b in range(blocks):
        where = iota((sources, LANES), 1) + b * LANES
        mine = lax.div(where, CAPS) == iota((sources, LANES), 0)
        spread = jnp.where(mine, total[b : b + 1, :], 0.0)
        move = lax.rem(iota((LANES, LANES), 0) + b * LANES, CAPS) == iota((LANES, LANES), 1)
        result += jnp.dot(
            spread,
            move.astype(jnp.float32),
            precision=lax.Precision.HIGHEST,
            preferred_element_type=jnp.float32,
        )
    out[...] = result


def final_kernel(clusters, reps, slots, sums, out):
    slot = slots[...]
    result = jnp.ones(slot.shape, jnp.float32)
    for c in range(clusters):
        inner = jnp.sum(sums[c * reps : (c + 1) * reps, :], axis=0, keepdims=True)
        keep = jnp.broadcast_to(1.0 / (1.0 + inner), slot.shape)
        rank = slot - c * CAPS
        mine = (rank >= 0) & (rank < CAPS)
        found = jnp.take_along_axis(keep, jnp.where(mine, rank, 0), axis=1)
        result = jnp.where(mine, found, result)
    out[...] = result


def local(embeddings, assignment, block_mask, cluster_cap, adjacent):
    dp_count, reps = lax.axis_size("dp"), lax.axis_size("rep")
    devices = dp_count * reps
    rows_dev, depth = embeddings.shape
    blocks = block_mask.shape[0]
    clusters = cluster_cap.shape[0]
    quarter = depth // reps
    tiles = quarter // LANES
    chunk = tiles * CAPS + tiles
    picks = -(-(clusters * (CAPS + 1)) // 16) * 16
    steps = rows_dev // ROW_STEP
    smem = pl.BlockSpec(memory_space=pltpu.SMEM)
    vmem = pl.BlockSpec(memory_space=pltpu.VMEM)
    anywhere = pl.BlockSpec(memory_space=pl.ANY)

    inputs = (
        cluster_cap, adjacent, block_mask, assignment.reshape(blocks, LANES), embeddings
    )
    send, slots = pl.pallas_call(
        functools.partial(select_kernel, clusters, reps),
        in_specs=[smem, smem, smem, vmem, anywhere],
        out_specs=[vmem, vmem],
        out_shape=[
            jax.ShapeDtypeStruct((devices, chunk, LANES), jnp.bfloat16),
            jax.ShapeDtypeStruct((blocks, LANES), jnp.int32),
        ],
        scratch_shapes=[
            pltpu.VMEM((steps, ROW_STEP, depth), jnp.bfloat16),
            pltpu.VMEM((picks, rows_dev), jnp.bfloat16),
            pltpu.VMEM((picks, LANES), jnp.float32),
            pltpu.VMEM((picks, depth), jnp.float32),
            pltpu.VMEM((picks, LANES), jnp.float32),
            pltpu.SemaphoreType.DMA((steps,)),
        ],
        compiler_params=pltpu.CompilerParams(vmem_limit_bytes=SELECT_BYTES),
        name="select_rows",
    )(*[pltpu.with_memory_space_constraint(x, pltpu.HBM) for x in inputs])

    got = lax.all_to_all(send, ALL, split_axis=0, concat_axis=0, tiled=True)

    count = devices * CAPS
    group = count // LANES
    _, part_rows = set_rows(group, dp_count)
    part = jax.ShapeDtypeStruct((2, part_rows, LANES), jnp.float32)
    part_bytes = 2 * part_rows * LANES * 4
    x, small, far_parts = pl.pallas_call(
        functools.partial(gather_kernel, dp_count),
        in_specs=[vmem],
        out_specs=[vmem] * 3,
        out_shape=[
            jax.ShapeDtypeStruct((count, quarter), jnp.bfloat16),
            jax.ShapeDtypeStruct((dp_count, count), jnp.float32),
            part,
        ],
        scratch_shapes=[
            pltpu.VMEM((devices * tiles, LANES), jnp.float32),
            pltpu.VMEM((reps * dp_count, quarter), jnp.bfloat16),
        ],
        compiler_params=grant(6 * count * quarter + part_bytes),
        name="gather_far_tiles",
    )(got)

    wire = jnp.float16
    cores = [(0, 1), (1, 0), (2, 3), (3, 2)]
    across = [(0, 2), (2, 0), (1, 3), (3, 1)]
    far = lax.ppermute(far_parts[0].astype(wire), "rep", cores)
    far = (far_parts[1] + far.astype(jnp.float32)).astype(wire)
    far, x, small = lax.optimization_barrier((far, x, small))
    far = lax.ppermute(far, "rep", across)
    near_parts = pl.pallas_call(
        functools.partial(near_kernel, dp_count),
        in_specs=[vmem] * 2,
        out_specs=vmem,
        out_shape=part,
        compiler_params=grant(4 * count * quarter + part_bytes),
        cost_estimate=pl.CostEstimate(
            flops=count * count * quarter, bytes_accessed=2 * count * quarter, transcendentals=0
        ),
        name="near_tiles",
    )(x, small)
    near = near_parts[0].astype(wire)
    middle = part_rows // 32 * 16
    near = [lax.ppermute(n, "rep", cores) for n in (near[:middle], near[middle:])]
    near = jnp.concatenate(near)
    both = near_parts[1] + near.astype(jnp.float32) + far.astype(jnp.float32)

    sums = pl.pallas_call(
        functools.partial(score_kernel, dp_count, devices),
        in_specs=[vmem],
        out_specs=vmem,
        out_shape=jax.ShapeDtypeStruct((devices, LANES), jnp.float32),
        scratch_shapes=[pltpu.VMEM((-(-group // 8) * 8, LANES), jnp.float32)],
        compiler_params=grant(part_bytes),
        name="score_tiles",
    )(both)

    back = lax.all_to_all(sums, ALL, split_axis=0, concat_axis=0, tiled=True)
    keep = pl.pallas_call(
        functools.partial(final_kernel, clusters, reps),
        in_specs=[vmem] * 2,
        out_specs=vmem,
        out_shape=jax.ShapeDtypeStruct((blocks, LANES), jnp.float32),
        compiler_params=grant(0),
        name="final_keep",
    )(slots, back)
    return keep.reshape(rows_dev)


def solution(mesh):
    placed = (P(ALL, None), P(ALL), P(ALL), P(), P())
    return jax.shard_map(local, mesh=mesh, in_specs=placed, out_specs=P(ALL), check_vma=False)
```

```python
import functools

import jax
import jax.numpy as jnp
from jax import lax
from jax.experimental import pallas as pl
from jax.experimental.pallas import tpu as pltpu
from jax.sharding import PartitionSpec as P

CAPS = 24
LANES = 128
ALL = ("dp", "rep")
FEATURE_STEP = 512
ROW_STEP = 256
EMPTY_MARK = 4.0
PENALTY = -1000.0
SPARE_BYTES = 6 * 1024 * 1024
SELECT_BYTES = 48 * 1024 * 1024

slope_gain = 64.0
inner_cut = 0.12
edge_cut = 0.06


def each(count, body, limit=8):
    if count <= limit:
        for index in range(count):
            body(index)
    else:

        def step(index, carry):
            body(index)
            return carry

        lax.fori_loop(0, count, step, 0)


def grant(size):
    return pltpu.CompilerParams(vmem_limit_bytes=size + SPARE_BYTES)


def iota(shape, dim):
    return lax.broadcasted_iota(jnp.int32, shape, dim)


def select_kernel(
    clusters,
    reps,
    cap_in,
    adjacent_in,
    mask_in,
    assign_in,
    rows,
    out,
    slots,
    cap,
    adjacent,
    mask,
    assign,
    data,
    pick,
    filled,
    chosen,
    squares,
    in_sem,
    small_sem,
):
    steps, deep, _ = data.shape
    reads = [
        pltpu.make_async_copy(rows.at[i * deep : (i + 1) * deep, :], data.at[i], in_sem.at[i])
        for i in range(steps)
    ]
    for read in reads:
        read.start()
    wanted = ((assign_in, assign), (mask_in, mask), (cap_in, cap), (adjacent_in, adjacent))
    smalls = [
        pltpu.make_async_copy(here, there, small_sem.at[k]) for k, (here, there) in enumerate(wanted)
    ]
    for small in smalls:
        small.start()
    for small in smalls:
        small.wait()

    blocks = assign.shape[0]
    depth = chosen.shape[1]
    count = pick.shape[0]
    base = clusters * CAPS
    table = assign[...]
    sub = iota(table.shape, 0)
    active = jnp.zeros(table.shape, jnp.int32)
    for block in range(blocks):
        active = jnp.where(sub == block, mask[block], active)
    live = jnp.where(active == 1, table, -1)
    members = jnp.concatenate(
        [(live == c).astype(jnp.float32) for c in range(clusters)], axis=0
    ).astype(jnp.bfloat16)
    total = clusters * blocks
    earlier = (iota((LANES, LANES), 0) < iota((LANES, LANES), 1)).astype(jnp.bfloat16)
    within = jnp.dot(members, earlier, preferred_element_type=jnp.float32)
    left, right = iota((total, total), 0), iota((total, total), 1)
    same = (left // blocks == right // blocks) & (right < left)
    sums = jnp.dot(
        same.astype(jnp.bfloat16), members, preferred_element_type=jnp.float32
    ).astype(jnp.bfloat16)
    before = jnp.dot(
        sums, jnp.ones((LANES, LANES), jnp.bfloat16), preferred_element_type=jnp.float32
    )
    rank = (within + before).astype(jnp.int32)
    slot = jnp.full(table.shape, -1, jnp.int32)
    for c in range(clusters):
        own = rank[c * blocks : (c + 1) * blocks]
        slot = jnp.where((live == c) & (own < cap[c]), c * CAPS + own, slot)
    slots[...] = slot
    place = iota((count, LANES), 0)
    target = jnp.where(place < base, place, -7)
    for c in range(clusters):
        target = jnp.where(place == base + c, adjacent[c] * CAPS, target)
    seen = jnp.zeros((count, LANES), jnp.float32)
    for block in range(blocks):
        hit = (target == slot[block : block + 1]).astype(jnp.float32)
        pick[:, block * LANES : (block + 1) * LANES] = hit.astype(jnp.bfloat16)
        seen += hit
    mark = jnp.sum(seen, axis=1, keepdims=True) < 0.5
    mark = mark & (iota(filled.shape, 1) == 0)
    filled[...] = jnp.where(mark, EMPTY_MARK, 0.0)

    power = jnp.zeros(squares.shape, jnp.float32)
    for i, read in enumerate(reads):
        read.wait()
        chunk_pick = pick[:, i * deep : (i + 1) * deep]
        for start in range(0, depth, FEATURE_STEP):
            cols = slice(start, start + FEATURE_STEP)
            part = jnp.dot(chunk_pick, data[i, :, cols], preferred_element_type=jnp.float32)
            if i:
                part += chosen[:, cols]
            chosen[:, cols] = part
            if i == steps - 1:
                for k in range(FEATURE_STEP // LANES):
                    piece = part[:, k * LANES : (k + 1) * LANES]
                    power += piece * piece

    scale = lax.rsqrt(jnp.sum(power, axis=1, keepdims=True) + 1e-06)
    squares[...] = jnp.broadcast_to(scale, squares.shape)
    quarter = depth // reps
    tiles = quarter // LANES
    sub = iota((tiles, LANES), 0)

    def eight(group):
        near = pl.ds(pl.multiple_of(base + group * 8, 8), 8)
        near_gain, near_flag = squares[near, :], filled[near, :]
        for k in range(8):
            c = group * 8 + k
            at = pl.ds(pl.multiple_of(c * CAPS, 8), CAPS)
            gain, flag = squares[at, :], filled[at, :]
            for q in range(reps):
                pieces = []
                edge = jnp.zeros((tiles, LANES), jnp.float32)
                for t in range(tiles):
                    cols = slice(q * quarter + t * LANES, q * quarter + (t + 1) * LANES)
                    piece = chosen[at, cols] * gain
                    line = chosen[near, cols] * near_gain
                    if t == 0:
                        piece += flag
                        line += near_flag
                    pieces.append(piece)
                    line = jnp.broadcast_to(line[k : k + 1], edge.shape)
                    edge = jnp.where(sub == t, line, edge)
                pieces.append(edge)
                chunk = jnp.concatenate(pieces, axis=0).astype(jnp.bfloat16)
                out[c * reps + q] = chunk

    each(clusters // 8, eight, 1)


def tile_sets(blocks):
    tiles = []
    for p in range(0, blocks, 2):
        tiles.append((p, p + 1, True))
        tiles += [(i, j, False) for i in (p, p + 1) for j in range(i + 1, blocks)]
    half = len(tiles) // 2
    return tiles[:half], tiles[half:]


def set_rows(blocks, ranks):
    size = len(tile_sets(blocks)[0])
    edge = size // 2 * LANES + size % 2 * (LANES // 2)
    return edge, edge + -(-(blocks // 2) // 2) * ranks


def emit_tiles(y, core, ranks, x, small, out):
    count = x.shape[0]
    blocks = count // LANES
    contract = (((1,), (1,)), ((), ()))
    first = (iota((8, LANES), 1) == 0).astype(jnp.bfloat16)
    marks = lax.dot_general(first, x[:, :LANES], contract, preferred_element_type=jnp.float32)
    col_pen = jnp.where(marks[:1] > 2.0, PENALTY, 0.0)
    tiles = tile_sets(blocks)[y]
    edge_base, _ = set_rows(blocks, ranks)

    def put(owner, start, value):
        slot = (core == owner).astype(jnp.int32)
        out[slot, start : start + value.shape[0], :] = value

    for p in range(0, blocks, 2):
        mine = [(e, t) for e, t in enumerate(tiles) if t[0] // 2 == p // 2]
        if not mine:
            continue
        row0 = min(t[0] for _, t in mine)
        row1 = max(t[1] if t[2] else t[0] for _, t in mine) + 1
        col0 = min(t[0] if t[2] else t[1] for _, t in mine)
        col1 = max(t[1] for _, t in mine) + 1
        rows = x[row0 * LANES : row1 * LANES, :]
        cols = slice(col0 * LANES, col1 * LANES)
        gram = lax.dot_general(rows, x[cols, :], contract, preferred_element_type=jnp.float32)
        row_pen = jnp.where(rows[:, :1].astype(jnp.float32) > 2.0, PENALTY, 0.0)
        gram = gram + row_pen + col_pen[:, cols]

        def tile(i, j, gram=gram, row0=row0, col0=col0):
            i, j = (i - row0) * LANES, (j - col0) * LANES
            return gram[i : i + LANES, j : j + LANES]

        for e, (i, j, diagonal) in mine:
            if diagonal:
                upper = iota((LANES, LANES), 0) < iota((LANES, LANES), 1)
                value = jnp.where(upper, tile(i, i), tile(j, j))
            else:
                value = tile(i, j)
            if e == len(tiles) - 1 and len(tiles) % 2:
                half = LANES // 2
                for owner in range(2):
                    put(owner, e // 2 * LANES, value[owner * half : (owner + 1) * half])
            else:
                put(e % 2, e // 2 * LANES, value)

    for k in range(blocks // 2):
        at = (y * (blocks // 2) + k) * LANES
        put(k % 2, edge_base + k // 2 * ranks, small[:, at : at + LANES])


def gather_kernel(ranks, got, x, small, out, edge_rows, edge_x):
    sources = got.shape[0]
    count, quarter = x.shape
    tiles = quarter // LANES
    reps = 4
    main = tiles * CAPS
    me = lax.axis_index("rep")

    def gather(pair):
        values = [got[2 * pair + k].astype(jnp.float32) for k in range(2)]
        for k in range(2):
            edge_rows[pl.ds((2 * pair + k) * tiles, tiles), :] = values[k][main:]
        for k in range(tiles):
            rows = slice(k * CAPS, (k + 1) * CAPS)
            both = jnp.concatenate([v[rows] for v in values], axis=0)
            x[pl.ds(pair * 2 * CAPS, 2 * CAPS), k * LANES : (k + 1) * LANES] = both.astype(
                jnp.bfloat16
            )

    each(sources // 2, gather, 16)

    for lane in range(reps):
        edge_x[lane * ranks : (lane + 1) * ranks, :] = jnp.concatenate(
            [
                edge_rows[pl.ds(lane * tiles + k, ranks, stride=reps * tiles), :]
                for k in range(tiles)
            ],
            axis=1,
        ).astype(jnp.bfloat16)

    near = edge_x[...]
    contract = (((1,), (1,)), ((), ()))
    edge = lax.dot_general(near, x[...], contract, preferred_element_type=jnp.float32)
    edge = edge + jnp.where(near[:, :1].astype(jnp.float32) > 2.0, PENALTY, 0.0)
    lane_of = lax.rem(lax.div(iota((ranks, count), 1), CAPS), reps)
    picked = edge[:ranks]
    for lane in range(1, reps):
        picked = jnp.where(lane_of == lane, edge[lane * ranks : (lane + 1) * ranks], picked)
    small[...] = picked

    for y in range(2):
        pl.when(me // 2 != y)(
            functools.partial(emit_tiles, y, me % 2, ranks, x, small, out)
        )


def near_kernel(ranks, x, small, out):
    me = lax.axis_index("rep")
    for y in range(2):
        pl.when(me // 2 == y)(
            functools.partial(emit_tiles, y, me % 2, ranks, x, small, out)
        )


def score_kernel(ranks, sources, sums, out, total):
    count = sources * CAPS
    blocks = count // LANES
    me = lax.axis_index("rep")
    core, my_y = me % 2, me // 2
    sets = tile_sets(blocks)
    size = len(sets[0])
    edge_base, _ = set_rows(blocks, ranks)
    total[...] = jnp.zeros_like(total)
    shape = (LANES, LANES)

    def by_rep(values):
        picked = jnp.int32(values[0])
        for k in range(1, len(values)):
            picked = jnp.where(me == k, jnp.int32(values[k]), picked)
        return picked

    def weigh(value, cut):
        return jax.nn.sigmoid(slope_gain * (value - cut))

    def rows_of(weight):
        return jnp.sum(weight.T, axis=0, keepdims=True)

    def cols_of(weight):
        return jnp.sum(weight, axis=0, keepdims=True)

    def plain(i, j, weight):
        total[pl.ds(i, 1), :] += rows_of(weight)
        total[pl.ds(j, 1), :] += cols_of(weight)

    def packed(i, j, weight):
        upper = jnp.where(iota(shape, 0) < iota(shape, 1), weight, 0.0)
        lower = jnp.where(iota(shape, 0) > iota(shape, 1), weight, 0.0)
        total[pl.ds(i, 1), :] += rows_of(upper) + cols_of(upper)
        total[pl.ds(j, 1), :] += rows_of(lower) + cols_of(lower)

    for place in range(size // 2):
        options = [sets[r // 2][2 * place + r % 2] for r in range(4)]
        i, j = by_rep([t[0] for t in options]), by_rep([t[1] for t in options])
        kinds = [t[2] for t in options]
        weight = weigh(sums[place * LANES : (place + 1) * LANES, :], inner_cut)
        if not any(kinds):
            plain(i, j, weight)
        else:
            kind = by_rep([int(k) for k in kinds])
            pl.when(kind == 1)(functools.partial(packed, i, j, weight))
            pl.when(kind == 0)(functools.partial(plain, i, j, weight))
    if size % 2:
        options = [sets[r // 2][size - 1] for r in range(4)]
        i, j = by_rep([t[0] for t in options]), by_rep([t[1] for t in options])
        start = size // 2 * LANES
        weight = weigh(sums[start : start + LANES // 2, :], inner_cut)
        halves = [jnp.where(core == k, weight, 0.0) for k in range(2)]
        plain(i, j, jnp.concatenate(halves, axis=0))

    for k in range(blocks // 2):

        @pl.when(core == k % 2)
        def _(k=k):
            at = edge_base + k // 2 * ranks
            edge = weigh(sums[at : at + ranks, :], edge_cut)
            total[pl.ds(my_y * (blocks // 2) + k, 1), :] += cols_of(edge)

    board = total[...]
    lane = iota((1, LANES), 1)
    for shift in range(0, LANES, 8):
        turned = pltpu.roll(board, (LANES - shift) % LANES, 1)
        for source in range(sources):
            block, offset = divmod(source * CAPS, LANES)
            if offset == shift:
                line = turned[block : block + 1, :]
                if offset + CAPS > LANES:
                    line = jnp.where(lane < LANES - offset, line, turned[block + 1 : block + 2, :])
                out[source : source + 1, :] = line


def final_kernel(clusters, reps, slots, sums, out):
    slot = slots[...]
    result = jnp.ones(slot.shape, jnp.float32)
    for c in range(clusters):
        inner = jnp.sum(sums[c * reps : (c + 1) * reps, :], axis=0, keepdims=True)
        keep = jnp.broadcast_to(1.0 / (1.0 + inner), slot.shape)
        rank = slot - c * CAPS
        mine = (rank >= 0) & (rank < CAPS)
        found = jnp.take_along_axis(keep, jnp.where(mine, rank, 0), axis=1)
        result = jnp.where(mine, found, result)
    out[...] = result


def local(embeddings, assignment, block_mask, cluster_cap, adjacent):
    dp_count, reps = lax.axis_size("dp"), lax.axis_size("rep")
    devices = dp_count * reps
    rows_dev, depth = embeddings.shape
    blocks = block_mask.shape[0]
    clusters = cluster_cap.shape[0]
    quarter = depth // reps
    tiles = quarter // LANES
    chunk = tiles * CAPS + tiles
    picks = -(-(clusters * (CAPS + 1)) // 16) * 16
    steps = rows_dev // ROW_STEP
    smem = pl.BlockSpec(memory_space=pltpu.SMEM)
    vmem = pl.BlockSpec(memory_space=pltpu.VMEM)
    anywhere = pl.BlockSpec(memory_space=pl.ANY)

    inputs = (
        cluster_cap, adjacent, block_mask, assignment.reshape(blocks, LANES), embeddings
    )
    send, slots = pl.pallas_call(
        functools.partial(select_kernel, clusters, reps),
        in_specs=[anywhere] * 5,
        out_specs=[vmem, vmem],
        out_shape=[
            jax.ShapeDtypeStruct((devices, chunk, LANES), jnp.bfloat16),
            jax.ShapeDtypeStruct((blocks, LANES), jnp.int32),
        ],
        scratch_shapes=[
            pltpu.SMEM((clusters,), jnp.int32),
            pltpu.SMEM((clusters,), jnp.int32),
            pltpu.SMEM((blocks,), jnp.int32),
            pltpu.VMEM((blocks, LANES), jnp.int32),
            pltpu.VMEM((steps, ROW_STEP, depth), jnp.bfloat16),
            pltpu.VMEM((picks, rows_dev), jnp.bfloat16),
            pltpu.VMEM((picks, LANES), jnp.float32),
            pltpu.VMEM((picks, depth), jnp.float32),
            pltpu.VMEM((picks, LANES), jnp.float32),
            pltpu.SemaphoreType.DMA((steps,)),
            pltpu.SemaphoreType.DMA((4,)),
        ],
        compiler_params=pltpu.CompilerParams(vmem_limit_bytes=SELECT_BYTES),
        name="select_rows",
    )(*[pltpu.with_memory_space_constraint(x, pltpu.HBM) for x in inputs])

    got = lax.all_to_all(send, ALL, split_axis=0, concat_axis=0, tiled=True)

    count = devices * CAPS
    group = count // LANES
    _, part_rows = set_rows(group, dp_count)
    part = jax.ShapeDtypeStruct((2, part_rows, LANES), jnp.float32)
    part_bytes = 2 * part_rows * LANES * 4
    x, small, far_parts = pl.pallas_call(
        functools.partial(gather_kernel, dp_count),
        in_specs=[vmem],
        out_specs=[vmem] * 3,
        out_shape=[
            jax.ShapeDtypeStruct((count, quarter), jnp.bfloat16),
            jax.ShapeDtypeStruct((dp_count, count), jnp.float32),
            part,
        ],
        scratch_shapes=[
            pltpu.VMEM((devices * tiles, LANES), jnp.float32),
            pltpu.VMEM((reps * dp_count, quarter), jnp.bfloat16),
        ],
        compiler_params=grant(6 * count * quarter + part_bytes),
        name="gather_far_tiles",
    )(got)

    wire = jnp.float16
    cores = [(0, 1), (1, 0), (2, 3), (3, 2)]
    across = [(0, 2), (2, 0), (1, 3), (3, 1)]
    far = lax.ppermute(far_parts[0].astype(wire), "rep", cores)
    far = (far_parts[1] + far.astype(jnp.float32)).astype(wire)
    far, x, small = lax.optimization_barrier((far, x, small))
    far = lax.ppermute(far, "rep", across)
    near_parts = pl.pallas_call(
        functools.partial(near_kernel, dp_count),
        in_specs=[vmem] * 2,
        out_specs=vmem,
        out_shape=part,
        compiler_params=grant(4 * count * quarter + part_bytes),
        cost_estimate=pl.CostEstimate(
            flops=count * count * quarter, bytes_accessed=2 * count * quarter, transcendentals=0
        ),
        name="near_tiles",
    )(x, small)
    near = near_parts[0].astype(wire)
    middle = part_rows // 32 * 16
    near = [lax.ppermute(n, "rep", cores) for n in (near[:middle], near[middle:])]
    near = jnp.concatenate(near)
    both = near_parts[1] + near.astype(jnp.float32) + far.astype(jnp.float32)

    sums = pl.pallas_call(
        functools.partial(score_kernel, dp_count, devices),
        in_specs=[vmem],
        out_specs=vmem,
        out_shape=jax.ShapeDtypeStruct((devices, LANES), jnp.float32),
        scratch_shapes=[pltpu.VMEM((-(-group // 8) * 8, LANES), jnp.float32)],
        compiler_params=grant(part_bytes),
        name="score_tiles",
    )(both)

    back = lax.all_to_all(sums, ALL, split_axis=0, concat_axis=0, tiled=True)
    keep = pl.pallas_call(
        functools.partial(final_kernel, clusters, reps),
        in_specs=[vmem] * 2,
        out_specs=vmem,
        out_shape=jax.ShapeDtypeStruct((blocks, LANES), jnp.float32),
        compiler_params=grant(0),
        name="final_keep",
    )(slots, back)
    return keep.reshape(rows_dev)


def solution(mesh):
    placed = (P(ALL, None), P(ALL), P(ALL), P(), P())
    return jax.shard_map(local, mesh=mesh, in_specs=placed, out_specs=P(ALL), check_vma=False)
```

```python
import functools

import jax
import jax.numpy as jnp
from jax import lax
from jax.experimental import pallas as pl
from jax.experimental.pallas import tpu as pltpu
from jax.sharding import PartitionSpec as P

CAPS = 24
LANES = 128
ALL = ("dp", "rep")
FEATURE_STEP = 512
ROW_STEP = 256
EMPTY_MARK = 4.0
PENALTY = -1000.0
SPARE_BYTES = 6 * 1024 * 1024
SELECT_BYTES = 48 * 1024 * 1024

slope_gain = 64.0
inner_cut = 0.12
edge_cut = 0.06


def each(count, body, limit=8):
    if count <= limit:
        for index in range(count):
            body(index)
    else:

        def step(index, carry):
            body(index)
            return carry

        lax.fori_loop(0, count, step, 0)


def grant(size):
    return pltpu.CompilerParams(vmem_limit_bytes=size + SPARE_BYTES)


def iota(shape, dim):
    return lax.broadcasted_iota(jnp.int32, shape, dim)


def select_kernel(
    clusters,
    reps,
    cap_in,
    adjacent_in,
    mask_in,
    assign_in,
    rows,
    out,
    slots,
    cap,
    adjacent,
    mask,
    assign,
    data,
    pick,
    filled,
    chosen,
    squares,
    in_sem,
    small_sem,
):
    steps, deep, _ = data.shape
    reads = [
        pltpu.make_async_copy(rows.at[i * deep : (i + 1) * deep, :], data.at[i], in_sem.at[i])
        for i in range(steps)
    ]
    for read in reads:
        read.start()
    wanted = ((assign_in, assign), (mask_in, mask), (cap_in, cap), (adjacent_in, adjacent))
    smalls = [
        pltpu.make_async_copy(here, there, small_sem.at[k]) for k, (here, there) in enumerate(wanted)
    ]
    for small in smalls:
        small.start()
    for small in smalls:
        small.wait()

    blocks = assign.shape[0]
    depth = chosen.shape[1]
    count = pick.shape[0]
    base = clusters * CAPS
    table = assign[...]
    sub = iota(table.shape, 0)
    active = jnp.zeros(table.shape, jnp.int32)
    for block in range(blocks):
        active = jnp.where(sub == block, mask[block], active)
    live = jnp.where(active == 1, table, -1)
    members = jnp.concatenate(
        [(live == c).astype(jnp.float32) for c in range(clusters)], axis=0
    ).astype(jnp.bfloat16)
    total = clusters * blocks
    earlier = (iota((LANES, LANES), 0) < iota((LANES, LANES), 1)).astype(jnp.bfloat16)
    within = jnp.dot(members, earlier, preferred_element_type=jnp.float32)
    left, right = iota((total, total), 0), iota((total, total), 1)
    same = (left // blocks == right // blocks) & (right < left)
    sums = jnp.dot(
        same.astype(jnp.bfloat16), members, preferred_element_type=jnp.float32
    ).astype(jnp.bfloat16)
    before = jnp.dot(
        sums, jnp.ones((LANES, LANES), jnp.bfloat16), preferred_element_type=jnp.float32
    )
    rank = (within + before).astype(jnp.int32)
    slot = jnp.full(table.shape, -1, jnp.int32)
    for c in range(clusters):
        own = rank[c * blocks : (c + 1) * blocks]
        slot = jnp.where((live == c) & (own < cap[c]), c * CAPS + own, slot)
    slots[...] = slot
    place = iota((count, LANES), 0)
    target = jnp.where(place < base, place, -7)
    for c in range(clusters):
        target = jnp.where(place == base + c, adjacent[c] * CAPS, target)
    seen = jnp.zeros((count, LANES), jnp.float32)
    for block in range(blocks):
        hit = (target == slot[block : block + 1]).astype(jnp.float32)
        pick[:, block * LANES : (block + 1) * LANES] = hit.astype(jnp.bfloat16)
        seen += hit
    mark = jnp.sum(seen, axis=1, keepdims=True) < 0.5
    mark = mark & (iota(filled.shape, 1) == 0)
    filled[...] = jnp.where(mark, EMPTY_MARK, 0.0)

    power = jnp.zeros(squares.shape, jnp.float32)
    for i, read in enumerate(reads):
        read.wait()
        chunk_pick = pick[:, i * deep : (i + 1) * deep]
        for start in range(0, depth, FEATURE_STEP):
            cols = slice(start, start + FEATURE_STEP)
            part = jnp.dot(chunk_pick, data[i, :, cols], preferred_element_type=jnp.float32)
            if i:
                part += chosen[:, cols]
            chosen[:, cols] = part
            if i == steps - 1:
                for k in range(FEATURE_STEP // LANES):
                    piece = part[:, k * LANES : (k + 1) * LANES]
                    power += piece * piece

    scale = lax.rsqrt(jnp.sum(power, axis=1, keepdims=True) + 1e-06)
    squares[...] = jnp.broadcast_to(scale, squares.shape)
    quarter = depth // reps
    tiles = quarter // LANES
    sub = iota((tiles, LANES), 0)

    def eight(group):
        near = pl.ds(pl.multiple_of(base + group * 8, 8), 8)
        near_gain, near_flag = squares[near, :], filled[near, :]
        for k in range(8):
            c = group * 8 + k
            at = pl.ds(pl.multiple_of(c * CAPS, 8), CAPS)
            gain, flag = squares[at, :], filled[at, :]
            for q in range(reps):
                pieces = []
                edge = jnp.zeros((tiles, LANES), jnp.float32)
                for t in range(tiles):
                    cols = slice(q * quarter + t * LANES, q * quarter + (t + 1) * LANES)
                    piece = chosen[at, cols] * gain
                    line = chosen[near, cols] * near_gain
                    if t == 0:
                        piece += flag
                        line += near_flag
                    pieces.append(piece)
                    line = jnp.broadcast_to(line[k : k + 1], edge.shape)
                    edge = jnp.where(sub == t, line, edge)
                pieces.append(edge)
                chunk = jnp.concatenate(pieces, axis=0).astype(jnp.bfloat16)
                out[c * reps + q] = chunk

    each(clusters // 8, eight, 1)


def tile_sets(blocks):
    tiles = []
    for p in range(0, blocks, 2):
        tiles.append((p, p + 1, True))
        tiles += [(i, j, False) for i in (p, p + 1) for j in range(i + 1, blocks)]
    half = len(tiles) // 2
    return tiles[:half], tiles[half:]


def set_rows(blocks, ranks):
    size = len(tile_sets(blocks)[0])
    edge = size // 2 * LANES + size % 2 * (LANES // 2)
    return edge, edge + -(-(blocks // 2) // 2) * ranks


def emit_tiles(y, core, ranks, x, edge_x, out):
    count, quarter = x.shape
    blocks = count // LANES
    half = blocks // 2
    reps = edge_x.shape[0] // ranks
    contract = (((1,), (1,)), ((), ()))
    tiles = tile_sets(blocks)[y]
    edge_base, _ = set_rows(blocks, ranks)
    marker = (iota((16, quarter), 1) == 0).astype(jnp.bfloat16)
    edges_left = True

    def put(owner, start, value):
        slot = (core == owner).astype(jnp.int32)
        out[slot, start : start + value.shape[0], :] = value

    def penalty(marks):
        return jnp.where(marks > 2.0, PENALTY, 0.0)

    for p in range(0, blocks, 2):
        mine = [(e, t) for e, t in enumerate(tiles) if t[0] // 2 == p // 2]
        if not mine:
            continue
        row0 = min(t[0] for _, t in mine)
        row1 = max(t[1] if t[2] else t[0] for _, t in mine) + 1
        col0 = min(t[0] if t[2] else t[1] for _, t in mine)
        col1 = max(t[1] for _, t in mine) + 1
        rows = x[row0 * LANES : row1 * LANES, :]
        edges_here = edges_left and col0 <= y * half and col1 >= (y + 1) * half
        near = [edge_x[...]] if edges_here else []
        left = jnp.concatenate([rows, *near, marker], axis=0)
        right = x[col0 * LANES : col1 * LANES, :]
        gram = lax.dot_general(left, right, contract, preferred_element_type=jnp.float32)
        col_pen = penalty(gram[left.shape[0] - 16 : left.shape[0] - 15])
        main = rows.shape[0]
        pairs = gram[:main] + penalty(rows[:, :1].astype(jnp.float32)) + col_pen

        def tile(i, j, pairs=pairs, row0=row0, col0=col0):
            i, j = (i - row0) * LANES, (j - col0) * LANES
            return pairs[i : i + LANES, j : j + LANES]

        for e, (i, j, diagonal) in mine:
            if diagonal:
                upper = iota((LANES, LANES), 0) < iota((LANES, LANES), 1)
                value = jnp.where(upper, tile(i, i), tile(j, j))
            else:
                value = tile(i, j)
            if e == len(tiles) - 1 and len(tiles) % 2:
                cut = LANES // 2
                for owner in range(2):
                    put(owner, e // 2 * LANES, value[owner * cut : (owner + 1) * cut])
            else:
                put(e % 2, e // 2 * LANES, value)

        if edges_here:
            edges_left = False
            edge = gram[main : main + reps * ranks] + penalty(near[0][:, :1].astype(jnp.float32))
            shape = (ranks, LANES)
            for k in range(half):
                block = y * half + k
                at = (block - col0) * LANES
                spot = iota(shape, 1) + block * LANES
                lane_of = lax.rem(lax.div(spot, CAPS), reps)
                value = edge[:ranks, at : at + LANES]
                for lane in range(1, reps):
                    other = edge[lane * ranks : (lane + 1) * ranks, at : at + LANES]
                    value = jnp.where(lane_of == lane, other, value)
                put(k % 2, edge_base + k // 2 * ranks, value)
    assert not edges_left


def gather_kernel(ranks, got, x, edge_x, out, edge_rows):
    sources = got.shape[0]
    quarter = x.shape[1]
    tiles = quarter // LANES
    reps = edge_x.shape[0] // ranks
    main = tiles * CAPS
    me = lax.axis_index("rep")

    def gather(pair):
        values = [got[2 * pair + k].astype(jnp.float32) for k in range(2)]
        for k in range(2):
            edge_rows[pl.ds((2 * pair + k) * tiles, tiles), :] = values[k][main:]
        for k in range(tiles):
            rows = slice(k * CAPS, (k + 1) * CAPS)
            both = jnp.concatenate([v[rows] for v in values], axis=0)
            x[pl.ds(pair * 2 * CAPS, 2 * CAPS), k * LANES : (k + 1) * LANES] = both.astype(
                jnp.bfloat16
            )

    each(sources // 2, gather, 16)

    for k in range(tiles):
        lines = [
            edge_rows[pl.ds(lane * tiles + k, ranks, stride=reps * tiles), :]
            for lane in range(reps)
        ]
        edge_x[:, k * LANES : (k + 1) * LANES] = jnp.concatenate(lines, axis=0).astype(jnp.bfloat16)

    for y in range(2):
        pl.when(me // 2 != y)(
            functools.partial(emit_tiles, y, me % 2, ranks, x, edge_x, out)
        )


def near_kernel(ranks, x, edge_x, out):
    me = lax.axis_index("rep")
    for y in range(2):
        pl.when(me // 2 == y)(
            functools.partial(emit_tiles, y, me % 2, ranks, x, edge_x, out)
        )


def score_kernel(ranks, sources, sums, out, total):
    count = sources * CAPS
    blocks = count // LANES
    me = lax.axis_index("rep")
    core, my_y = me % 2, me // 2
    sets = tile_sets(blocks)
    size = len(sets[0])
    edge_base, _ = set_rows(blocks, ranks)
    total[...] = jnp.zeros_like(total)
    shape = (LANES, LANES)

    def by_rep(values):
        picked = jnp.int32(values[0])
        for k in range(1, len(values)):
            picked = jnp.where(me == k, jnp.int32(values[k]), picked)
        return picked

    def weigh(value, cut):
        return jax.nn.sigmoid(slope_gain * (value - cut))

    def rows_of(weight):
        return jnp.sum(weight.T, axis=0, keepdims=True)

    def cols_of(weight):
        return jnp.sum(weight, axis=0, keepdims=True)

    def plain(i, j, weight):
        total[pl.ds(i, 1), :] += rows_of(weight)
        total[pl.ds(j, 1), :] += cols_of(weight)

    def packed(i, j, weight):
        upper = jnp.where(iota(shape, 0) < iota(shape, 1), weight, 0.0)
        lower = jnp.where(iota(shape, 0) > iota(shape, 1), weight, 0.0)
        total[pl.ds(i, 1), :] += rows_of(upper) + cols_of(upper)
        total[pl.ds(j, 1), :] += rows_of(lower) + cols_of(lower)

    for place in range(size // 2):
        options = [sets[r // 2][2 * place + r % 2] for r in range(4)]
        i, j = by_rep([t[0] for t in options]), by_rep([t[1] for t in options])
        kinds = [t[2] for t in options]
        weight = weigh(sums[place * LANES : (place + 1) * LANES, :], inner_cut)
        if not any(kinds):
            plain(i, j, weight)
        else:
            kind = by_rep([int(k) for k in kinds])
            pl.when(kind == 1)(functools.partial(packed, i, j, weight))
            pl.when(kind == 0)(functools.partial(plain, i, j, weight))
    if size % 2:
        options = [sets[r // 2][size - 1] for r in range(4)]
        i, j = by_rep([t[0] for t in options]), by_rep([t[1] for t in options])
        start = size // 2 * LANES
        weight = weigh(sums[start : start + LANES // 2, :], inner_cut)
        halves = [jnp.where(core == k, weight, 0.0) for k in range(2)]
        plain(i, j, jnp.concatenate(halves, axis=0))

    for k in range(blocks // 2):

        @pl.when(core == k % 2)
        def _(k=k):
            at = edge_base + k // 2 * ranks
            edge = weigh(sums[at : at + ranks, :], edge_cut)
            total[pl.ds(my_y * (blocks // 2) + k, 1), :] += cols_of(edge)

    board = total[...]
    lane = iota((1, LANES), 1)
    for shift in range(0, LANES, 8):
        turned = pltpu.roll(board, (LANES - shift) % LANES, 1)
        for source in range(sources):
            block, offset = divmod(source * CAPS, LANES)
            if offset == shift:
                line = turned[block : block + 1, :]
                if offset + CAPS > LANES:
                    line = jnp.where(lane < LANES - offset, line, turned[block + 1 : block + 2, :])
                out[source : source + 1, :] = line


def final_kernel(clusters, reps, slots, sums, out):
    slot = slots[...]
    result = jnp.ones(slot.shape, jnp.float32)
    for c in range(clusters):
        inner = jnp.sum(sums[c * reps : (c + 1) * reps, :], axis=0, keepdims=True)
        keep = jnp.broadcast_to(1.0 / (1.0 + inner), slot.shape)
        rank = slot - c * CAPS
        mine = (rank >= 0) & (rank < CAPS)
        found = jnp.take_along_axis(keep, jnp.where(mine, rank, 0), axis=1)
        result = jnp.where(mine, found, result)
    out[...] = result


def local(embeddings, assignment, block_mask, cluster_cap, adjacent):
    dp_count, reps = lax.axis_size("dp"), lax.axis_size("rep")
    devices = dp_count * reps
    rows_dev, depth = embeddings.shape
    blocks = block_mask.shape[0]
    clusters = cluster_cap.shape[0]
    quarter = depth // reps
    tiles = quarter // LANES
    chunk = tiles * CAPS + tiles
    picks = -(-(clusters * (CAPS + 1)) // 16) * 16
    steps = rows_dev // ROW_STEP
    smem = pl.BlockSpec(memory_space=pltpu.SMEM)
    vmem = pl.BlockSpec(memory_space=pltpu.VMEM)
    anywhere = pl.BlockSpec(memory_space=pl.ANY)

    inputs = (
        cluster_cap, adjacent, block_mask, assignment.reshape(blocks, LANES), embeddings
    )
    send, slots = pl.pallas_call(
        functools.partial(select_kernel, clusters, reps),
        in_specs=[anywhere] * 5,
        out_specs=[vmem, vmem],
        out_shape=[
            jax.ShapeDtypeStruct((devices, chunk, LANES), jnp.bfloat16),
            jax.ShapeDtypeStruct((blocks, LANES), jnp.int32),
        ],
        scratch_shapes=[
            pltpu.SMEM((clusters,), jnp.int32),
            pltpu.SMEM((clusters,), jnp.int32),
            pltpu.SMEM((blocks,), jnp.int32),
            pltpu.VMEM((blocks, LANES), jnp.int32),
            pltpu.VMEM((steps, ROW_STEP, depth), jnp.bfloat16),
            pltpu.VMEM((picks, rows_dev), jnp.bfloat16),
            pltpu.VMEM((picks, LANES), jnp.float32),
            pltpu.VMEM((picks, depth), jnp.float32),
            pltpu.VMEM((picks, LANES), jnp.float32),
            pltpu.SemaphoreType.DMA((steps,)),
            pltpu.SemaphoreType.DMA((4,)),
        ],
        compiler_params=pltpu.CompilerParams(vmem_limit_bytes=SELECT_BYTES),
        name="select_rows",
    )(*[pltpu.with_memory_space_constraint(x, pltpu.HBM) for x in inputs])

    got = lax.all_to_all(send, ALL, split_axis=0, concat_axis=0, tiled=True)

    count = devices * CAPS
    group = count // LANES
    _, part_rows = set_rows(group, dp_count)
    part = jax.ShapeDtypeStruct((2, part_rows, LANES), jnp.float32)
    part_bytes = 2 * part_rows * LANES * 4
    x, edge_x, far_parts = pl.pallas_call(
        functools.partial(gather_kernel, dp_count),
        in_specs=[vmem],
        out_specs=[vmem] * 3,
        out_shape=[
            jax.ShapeDtypeStruct((count, quarter), jnp.bfloat16),
            jax.ShapeDtypeStruct((reps * dp_count, quarter), jnp.bfloat16),
            part,
        ],
        scratch_shapes=[
            pltpu.VMEM((devices * tiles, LANES), jnp.float32),
        ],
        compiler_params=grant(6 * count * quarter + part_bytes),
        name="gather_far_tiles",
    )(got)

    wire = jnp.float16
    cores = [(0, 1), (1, 0), (2, 3), (3, 2)]
    across = [(0, 2), (2, 0), (1, 3), (3, 1)]
    far = lax.ppermute(far_parts[0].astype(wire), "rep", cores)
    far = (far_parts[1] + far.astype(jnp.float32)).astype(wire)
    far, x, edge_x = lax.optimization_barrier((far, x, edge_x))
    far = lax.ppermute(far, "rep", across)
    near_parts = pl.pallas_call(
        functools.partial(near_kernel, dp_count),
        in_specs=[vmem] * 2,
        out_specs=vmem,
        out_shape=part,
        compiler_params=grant(4 * count * quarter + part_bytes),
        cost_estimate=pl.CostEstimate(
            flops=count * count * quarter, bytes_accessed=2 * count * quarter, transcendentals=0
        ),
        name="near_tiles",
    )(x, edge_x)
    near = near_parts[0].astype(wire)
    middle = part_rows // 32 * 16
    near = [lax.ppermute(n, "rep", cores) for n in (near[:middle], near[middle:])]
    near = jnp.concatenate(near)
    both = near_parts[1] + near.astype(jnp.float32) + far.astype(jnp.float32)

    sums = pl.pallas_call(
        functools.partial(score_kernel, dp_count, devices),
        in_specs=[vmem],
        out_specs=vmem,
        out_shape=jax.ShapeDtypeStruct((devices, LANES), jnp.float32),
        scratch_shapes=[pltpu.VMEM((-(-group // 8) * 8, LANES), jnp.float32)],
        compiler_params=grant(part_bytes),
        name="score_tiles",
    )(both)

    back = lax.all_to_all(sums, ALL, split_axis=0, concat_axis=0, tiled=True)
    keep = pl.pallas_call(
        functools.partial(final_kernel, clusters, reps),
        in_specs=[vmem] * 2,
        out_specs=vmem,
        out_shape=jax.ShapeDtypeStruct((blocks, LANES), jnp.float32),
        compiler_params=grant(0),
        name="final_keep",
    )(slots, back)
    return keep.reshape(rows_dev)


def solution(mesh):
    placed = (P(ALL, None), P(ALL), P(ALL), P(), P())
    return jax.shard_map(local, mesh=mesh, in_specs=placed, out_specs=P(ALL), check_vma=False)
```

```python
import functools

import jax
import jax.numpy as jnp
from jax import lax
from jax.experimental import pallas as pl
from jax.experimental.pallas import tpu as pltpu
from jax.sharding import PartitionSpec as P

CAPS = 24
LANES = 128
ALL = ("dp", "rep")
FEATURE_STEP = 512
ROW_STEP = 256
EMPTY_MARK = 4.0
PENALTY = -1000.0
SPARE_BYTES = 6 * 1024 * 1024
SELECT_BYTES = 48 * 1024 * 1024

slope_gain = 64.0
inner_cut = 0.12
edge_cut = 0.06


def each(count, body, limit=8):
    if count <= limit:
        for index in range(count):
            body(index)
    else:

        def step(index, carry):
            body(index)
            return carry

        lax.fori_loop(0, count, step, 0)


def grant(size):
    return pltpu.CompilerParams(vmem_limit_bytes=size + SPARE_BYTES)


def iota(shape, dim):
    return lax.broadcasted_iota(jnp.int32, shape, dim)


def select_kernel(
    clusters,
    reps,
    cap_in,
    adjacent_in,
    mask_in,
    assign_in,
    rows,
    out,
    slots,
    cap,
    adjacent,
    mask,
    assign,
    data,
    pick,
    filled,
    chosen,
    squares,
    edges,
    in_sem,
    small_sem,
):
    steps, deep, _ = data.shape
    reads = [
        pltpu.make_async_copy(rows.at[i * deep : (i + 1) * deep, :], data.at[i], in_sem.at[i])
        for i in range(steps)
    ]
    for read in reads:
        read.start()
    wanted = ((assign_in, assign), (mask_in, mask), (cap_in, cap), (adjacent_in, adjacent))
    smalls = [
        pltpu.make_async_copy(here, there, small_sem.at[k]) for k, (here, there) in enumerate(wanted)
    ]
    for small in smalls:
        small.start()
    for small in smalls:
        small.wait()

    blocks = assign.shape[0]
    depth = chosen.shape[1]
    count = pick.shape[0]
    base = clusters * CAPS
    table = assign[...]
    sub = iota(table.shape, 0)
    active = jnp.zeros(table.shape, jnp.int32)
    for block in range(blocks):
        active = jnp.where(sub == block, mask[block], active)
    live = jnp.where(active == 1, table, -1)
    members = jnp.concatenate(
        [(live == c).astype(jnp.float32) for c in range(clusters)], axis=0
    ).astype(jnp.bfloat16)
    total = clusters * blocks
    earlier = (iota((LANES, LANES), 0) < iota((LANES, LANES), 1)).astype(jnp.bfloat16)
    within = jnp.dot(members, earlier, preferred_element_type=jnp.float32)
    left, right = iota((total, total), 0), iota((total, total), 1)
    same = (left // blocks == right // blocks) & (right < left)
    sums = jnp.dot(
        same.astype(jnp.bfloat16), members, preferred_element_type=jnp.float32
    ).astype(jnp.bfloat16)
    before = jnp.dot(
        sums, jnp.ones((LANES, LANES), jnp.bfloat16), preferred_element_type=jnp.float32
    )
    rank = (within + before).astype(jnp.int32)
    slot = jnp.full(table.shape, -1, jnp.int32)
    for c in range(clusters):
        own = rank[c * blocks : (c + 1) * blocks]
        slot = jnp.where((live == c) & (own < cap[c]), c * CAPS + own, slot)
    slots[...] = slot
    place = iota((count, LANES), 0)
    target = jnp.where(place < base, place, -7)
    for c in range(clusters):
        target = jnp.where(place == base + c, adjacent[c] * CAPS, target)
    seen = jnp.zeros((count, LANES), jnp.float32)
    for block in range(blocks):
        hit = (target == slot[block : block + 1]).astype(jnp.float32)
        pick[:, block * LANES : (block + 1) * LANES] = hit.astype(jnp.bfloat16)
        seen += hit
    mark = jnp.sum(seen, axis=1, keepdims=True) < 0.5
    mark = mark & (iota(filled.shape, 1) == 0)
    filled[...] = jnp.where(mark, EMPTY_MARK, 0.0)

    power = jnp.zeros(squares.shape, jnp.float32)
    for i, read in enumerate(reads):
        read.wait()
        chunk_pick = pick[:, i * deep : (i + 1) * deep]
        for start in range(0, depth, FEATURE_STEP):
            cols = slice(start, start + FEATURE_STEP)
            part = jnp.dot(chunk_pick, data[i, :, cols], preferred_element_type=jnp.float32)
            if i:
                part += chosen[:, cols]
            chosen[:, cols] = part
            if i == steps - 1:
                for k in range(FEATURE_STEP // LANES):
                    piece = part[:, k * LANES : (k + 1) * LANES]
                    power += piece * piece

    scale = lax.rsqrt(jnp.sum(power, axis=1, keepdims=True) + 1e-06)
    squares[...] = jnp.broadcast_to(scale, squares.shape)
    quarter = depth // reps
    tiles = quarter // LANES

    def eight(group):
        near = pl.ds(pl.multiple_of(base + group * 8, 8), 8)
        near_gain, near_flag = squares[near, :], filled[near, :]
        for q in range(reps):
            for t in range(tiles):
                col = q * quarter + t * LANES
                line = chosen[near, col : col + LANES] * near_gain
                if t == 0:
                    line += near_flag
                edges[pl.ds(q * 8 * tiles + t, 8, stride=tiles), :] = line
        for k in range(8):
            at = pl.ds(pl.multiple_of((group * 8 + k) * CAPS, 8), CAPS)
            gain, flag = squares[at, :], filled[at, :]
            for q in range(reps):
                pieces = []
                for t in range(tiles):
                    cols = slice(q * quarter + t * LANES, q * quarter + (t + 1) * LANES)
                    pieces.append(chosen[at, cols] * gain)
                pieces[0] += flag
                pieces.append(edges[(q * 8 + k) * tiles : (q * 8 + k + 1) * tiles, :])
                chunk = jnp.concatenate(pieces, axis=0).astype(jnp.bfloat16)
                out[(group * 8 + k) * reps + q] = chunk

    each(clusters // 8, eight, 1)


def tile_sets(blocks):
    tiles = []
    for p in range(0, blocks, 2):
        tiles.append((p, p + 1, True))
        tiles += [(i, j, False) for i in (p, p + 1) for j in range(i + 1, blocks)]
    half = len(tiles) // 2
    return tiles[:half], tiles[half:]


def set_rows(blocks, ranks):
    size = len(tile_sets(blocks)[0])
    edge = size // 2 * LANES + size % 2 * (LANES // 2)
    return edge, edge + -(-(blocks // 2) // 2) * ranks


def emit_tiles(y, core, ranks, x, edge_x, out):
    count, quarter = x.shape
    blocks = count // LANES
    half = blocks // 2
    reps = edge_x.shape[0] // ranks
    contract = (((1,), (1,)), ((), ()))
    tiles = tile_sets(blocks)[y]
    edge_base, _ = set_rows(blocks, ranks)
    marker = (iota((16, quarter), 1) == 0).astype(jnp.bfloat16)
    edges_left = True

    def put(owner, start, value):
        slot = (core == owner).astype(jnp.int32)
        out[slot, start : start + value.shape[0], :] = value

    def penalty(marks):
        return jnp.where(marks > 2.0, PENALTY, 0.0)

    for p in range(0, blocks, 2):
        mine = [(e, t) for e, t in enumerate(tiles) if t[0] // 2 == p // 2]
        if not mine:
            continue
        row0 = min(t[0] for _, t in mine)
        row1 = max(t[1] if t[2] else t[0] for _, t in mine) + 1
        col0 = min(t[0] if t[2] else t[1] for _, t in mine)
        col1 = max(t[1] for _, t in mine) + 1
        rows = x[row0 * LANES : row1 * LANES, :]
        edges_here = edges_left and col0 <= y * half and col1 >= (y + 1) * half
        near = [edge_x[...]] if edges_here else []
        left = jnp.concatenate([rows, *near, marker], axis=0)
        right = x[col0 * LANES : col1 * LANES, :]
        gram = lax.dot_general(left, right, contract, preferred_element_type=jnp.float32)
        col_pen = penalty(gram[left.shape[0] - 16 : left.shape[0] - 15])
        main = rows.shape[0]
        pairs = gram[:main] + penalty(rows[:, :1].astype(jnp.float32)) + col_pen

        def tile(i, j, pairs=pairs, row0=row0, col0=col0):
            i, j = (i - row0) * LANES, (j - col0) * LANES
            return pairs[i : i + LANES, j : j + LANES]

        for e, (i, j, diagonal) in mine:
            if diagonal:
                upper = iota((LANES, LANES), 0) < iota((LANES, LANES), 1)
                value = jnp.where(upper, tile(i, i), tile(j, j))
            else:
                value = tile(i, j)
            if e == len(tiles) - 1 and len(tiles) % 2:
                cut = LANES // 2
                for owner in range(2):
                    put(owner, e // 2 * LANES, value[owner * cut : (owner + 1) * cut])
            else:
                put(e % 2, e // 2 * LANES, value)

        if edges_here:
            edges_left = False
            edge = gram[main : main + reps * ranks] + penalty(near[0][:, :1].astype(jnp.float32))
            shape = (ranks, LANES)
            for k in range(half):
                block = y * half + k
                at = (block - col0) * LANES
                spot = iota(shape, 1) + block * LANES
                lane_of = lax.rem(lax.div(spot, CAPS), reps)
                value = edge[:ranks, at : at + LANES]
                for lane in range(1, reps):
                    other = edge[lane * ranks : (lane + 1) * ranks, at : at + LANES]
                    value = jnp.where(lane_of == lane, other, value)
                put(k % 2, edge_base + k // 2 * ranks, value)
    assert not edges_left


def gather_kernel(ranks, got, x, edge_x, out, edge_rows):
    sources = got.shape[0]
    quarter = x.shape[1]
    tiles = quarter // LANES
    reps = edge_x.shape[0] // ranks
    main = tiles * CAPS
    me = lax.axis_index("rep")

    def gather(pair):
        values = [got[2 * pair + k].astype(jnp.float32) for k in range(2)]
        for k in range(2):
            edge_rows[pl.ds((2 * pair + k) * tiles, tiles), :] = values[k][main:]
        for k in range(tiles):
            rows = slice(k * CAPS, (k + 1) * CAPS)
            both = jnp.concatenate([v[rows] for v in values], axis=0)
            x[pl.ds(pair * 2 * CAPS, 2 * CAPS), k * LANES : (k + 1) * LANES] = both.astype(
                jnp.bfloat16
            )

    each(sources // 2, gather, 16)

    for k in range(tiles):
        lines = [
            edge_rows[pl.ds(lane * tiles + k, ranks, stride=reps * tiles), :]
            for lane in range(reps)
        ]
        edge_x[:, k * LANES : (k + 1) * LANES] = jnp.concatenate(lines, axis=0).astype(jnp.bfloat16)

    for y in range(2):
        pl.when(me // 2 != y)(
            functools.partial(emit_tiles, y, me % 2, ranks, x, edge_x, out)
        )


def near_kernel(ranks, x, edge_x, out):
    me = lax.axis_index("rep")
    for y in range(2):
        pl.when(me // 2 == y)(
            functools.partial(emit_tiles, y, me % 2, ranks, x, edge_x, out)
        )


def score_kernel(ranks, sources, sums, out, total):
    count = sources * CAPS
    blocks = count // LANES
    me = lax.axis_index("rep")
    core, my_y = me % 2, me // 2
    sets = tile_sets(blocks)
    size = len(sets[0])
    edge_base, _ = set_rows(blocks, ranks)
    total[...] = jnp.zeros_like(total)
    shape = (LANES, LANES)

    def by_rep(values):
        picked = jnp.int32(values[0])
        for k in range(1, len(values)):
            picked = jnp.where(me == k, jnp.int32(values[k]), picked)
        return picked

    def weigh(value, cut):
        return jax.nn.sigmoid(slope_gain * (value - cut))

    def rows_of(weight):
        return jnp.sum(weight.T, axis=0, keepdims=True)

    def cols_of(weight):
        return jnp.sum(weight, axis=0, keepdims=True)

    def plain(i, j, weight):
        total[pl.ds(i, 1), :] += rows_of(weight)
        total[pl.ds(j, 1), :] += cols_of(weight)

    def packed(i, j, weight):
        upper = jnp.where(iota(shape, 0) < iota(shape, 1), weight, 0.0)
        lower = jnp.where(iota(shape, 0) > iota(shape, 1), weight, 0.0)
        total[pl.ds(i, 1), :] += rows_of(upper) + cols_of(upper)
        total[pl.ds(j, 1), :] += rows_of(lower) + cols_of(lower)

    for place in range(size // 2):
        options = [sets[r // 2][2 * place + r % 2] for r in range(4)]
        i, j = by_rep([t[0] for t in options]), by_rep([t[1] for t in options])
        kinds = [t[2] for t in options]
        weight = weigh(sums[place * LANES : (place + 1) * LANES, :], inner_cut)
        if not any(kinds):
            plain(i, j, weight)
        else:
            kind = by_rep([int(k) for k in kinds])
            pl.when(kind == 1)(functools.partial(packed, i, j, weight))
            pl.when(kind == 0)(functools.partial(plain, i, j, weight))
    if size % 2:
        options = [sets[r // 2][size - 1] for r in range(4)]
        i, j = by_rep([t[0] for t in options]), by_rep([t[1] for t in options])
        start = size // 2 * LANES
        weight = weigh(sums[start : start + LANES // 2, :], inner_cut)
        halves = [jnp.where(core == k, weight, 0.0) for k in range(2)]
        plain(i, j, jnp.concatenate(halves, axis=0))

    for k in range(blocks // 2):

        @pl.when(core == k % 2)
        def _(k=k):
            at = edge_base + k // 2 * ranks
            edge = weigh(sums[at : at + ranks, :], edge_cut)
            total[pl.ds(my_y * (blocks // 2) + k, 1), :] += cols_of(edge)

    board = total[...]
    lane = iota((1, LANES), 1)
    for shift in range(0, LANES, 8):
        turned = pltpu.roll(board, (LANES - shift) % LANES, 1)
        for source in range(sources):
            block, offset = divmod(source * CAPS, LANES)
            if offset == shift:
                line = turned[block : block + 1, :]
                if offset + CAPS > LANES:
                    line = jnp.where(lane < LANES - offset, line, turned[block + 1 : block + 2, :])
                out[source : source + 1, :] = line


def final_kernel(clusters, reps, slots, sums, out):
    slot = slots[...]
    result = jnp.ones(slot.shape, jnp.float32)
    for c in range(clusters):
        inner = jnp.sum(sums[c * reps : (c + 1) * reps, :], axis=0, keepdims=True)
        keep = jnp.broadcast_to(1.0 / (1.0 + inner), slot.shape)
        rank = slot - c * CAPS
        mine = (rank >= 0) & (rank < CAPS)
        found = jnp.take_along_axis(keep, jnp.where(mine, rank, 0), axis=1)
        result = jnp.where(mine, found, result)
    out[...] = result


def local(embeddings, assignment, block_mask, cluster_cap, adjacent):
    dp_count, reps = lax.axis_size("dp"), lax.axis_size("rep")
    devices = dp_count * reps
    rows_dev, depth = embeddings.shape
    blocks = block_mask.shape[0]
    clusters = cluster_cap.shape[0]
    quarter = depth // reps
    tiles = quarter // LANES
    chunk = tiles * CAPS + tiles
    picks = -(-(clusters * (CAPS + 1)) // 16) * 16
    steps = rows_dev // ROW_STEP
    smem = pl.BlockSpec(memory_space=pltpu.SMEM)
    vmem = pl.BlockSpec(memory_space=pltpu.VMEM)
    anywhere = pl.BlockSpec(memory_space=pl.ANY)

    inputs = (
        cluster_cap, adjacent, block_mask, assignment.reshape(blocks, LANES), embeddings
    )
    send, slots = pl.pallas_call(
        functools.partial(select_kernel, clusters, reps),
        in_specs=[anywhere] * 5,
        out_specs=[vmem, vmem],
        out_shape=[
            jax.ShapeDtypeStruct((devices, chunk, LANES), jnp.bfloat16),
            jax.ShapeDtypeStruct((blocks, LANES), jnp.int32),
        ],
        scratch_shapes=[
            pltpu.SMEM((clusters,), jnp.int32),
            pltpu.SMEM((clusters,), jnp.int32),
            pltpu.SMEM((blocks,), jnp.int32),
            pltpu.VMEM((blocks, LANES), jnp.int32),
            pltpu.VMEM((steps, ROW_STEP, depth), jnp.bfloat16),
            pltpu.VMEM((picks, rows_dev), jnp.bfloat16),
            pltpu.VMEM((picks, LANES), jnp.float32),
            pltpu.VMEM((picks, depth), jnp.float32),
            pltpu.VMEM((picks, LANES), jnp.float32),
            pltpu.VMEM((8 * reps * tiles, LANES), jnp.float32),
            pltpu.SemaphoreType.DMA((steps,)),
            pltpu.SemaphoreType.DMA((4,)),
        ],
        compiler_params=pltpu.CompilerParams(vmem_limit_bytes=SELECT_BYTES),
        name="select_rows",
    )(*[pltpu.with_memory_space_constraint(x, pltpu.HBM) for x in inputs])

    got = lax.all_to_all(send, ALL, split_axis=0, concat_axis=0, tiled=True)

    count = devices * CAPS
    group = count // LANES
    _, part_rows = set_rows(group, dp_count)
    part = jax.ShapeDtypeStruct((2, part_rows, LANES), jnp.float32)
    part_bytes = 2 * part_rows * LANES * 4
    x, edge_x, far_parts = pl.pallas_call(
        functools.partial(gather_kernel, dp_count),
        in_specs=[vmem],
        out_specs=[vmem] * 3,
        out_shape=[
            jax.ShapeDtypeStruct((count, quarter), jnp.bfloat16),
            jax.ShapeDtypeStruct((reps * dp_count, quarter), jnp.bfloat16),
            part,
        ],
        scratch_shapes=[
            pltpu.VMEM((devices * tiles, LANES), jnp.float32),
        ],
        compiler_params=grant(6 * count * quarter + part_bytes),
        name="gather_far_tiles",
    )(got)

    wire = jnp.float16
    cores = [(0, 1), (1, 0), (2, 3), (3, 2)]
    across = [(0, 2), (2, 0), (1, 3), (3, 1)]
    far = lax.ppermute(far_parts[0].astype(wire), "rep", cores)
    far = (far_parts[1] + far.astype(jnp.float32)).astype(wire)
    far, x, edge_x = lax.optimization_barrier((far, x, edge_x))
    far = lax.ppermute(far, "rep", across)
    near_parts = pl.pallas_call(
        functools.partial(near_kernel, dp_count),
        in_specs=[vmem] * 2,
        out_specs=vmem,
        out_shape=part,
        compiler_params=grant(4 * count * quarter + part_bytes),
        cost_estimate=pl.CostEstimate(
            flops=count * count * quarter, bytes_accessed=2 * count * quarter, transcendentals=0
        ),
        name="near_tiles",
    )(x, edge_x)
    near = lax.ppermute(near_parts[0].astype(wire), "rep", cores)
    both = near_parts[1] + far.astype(jnp.float32)
    both = lax.optimization_barrier(both) + near.astype(jnp.float32)

    sums = pl.pallas_call(
        functools.partial(score_kernel, dp_count, devices),
        in_specs=[vmem],
        out_specs=vmem,
        out_shape=jax.ShapeDtypeStruct((devices, LANES), jnp.float32),
        scratch_shapes=[pltpu.VMEM((-(-group // 8) * 8, LANES), jnp.float32)],
        compiler_params=grant(part_bytes),
        name="score_tiles",
    )(both)

    back = lax.all_to_all(sums, ALL, split_axis=0, concat_axis=0, tiled=True)
    keep = pl.pallas_call(
        functools.partial(final_kernel, clusters, reps),
        in_specs=[vmem] * 2,
        out_specs=vmem,
        out_shape=jax.ShapeDtypeStruct((blocks, LANES), jnp.float32),
        compiler_params=grant(0),
        name="final_keep",
    )(slots, back)
    return keep.reshape(rows_dev)


def solution(mesh):
    placed = (P(ALL, None), P(ALL), P(ALL), P(), P())
    return jax.shard_map(local, mesh=mesh, in_specs=placed, out_specs=P(ALL), check_vma=False)
```

```python
import functools

import jax
import jax.numpy as jnp
from jax import lax
from jax.experimental import pallas as pl
from jax.experimental.pallas import tpu as pltpu
from jax.sharding import PartitionSpec as P

CAPS = 24
LANES = 128
GROUPS = LANES // CAPS
ALL = ("dp", "rep")
FEATURE_STEP = 512
ROW_STEP = 256
EMPTY_MARK = 4.0
PENALTY = -1000.0
SPARE_BYTES = 6 * 1024 * 1024
SELECT_BYTES = 48 * 1024 * 1024

slope_gain = 64.0
inner_cut = 0.12
edge_cut = 0.06


def each(count, body, limit=8):
    if count <= limit:
        for index in range(count):
            body(index)
    else:

        def step(index, carry):
            body(index)
            return carry

        lax.fori_loop(0, count, step, 0)


def grant(size):
    return pltpu.CompilerParams(vmem_limit_bytes=size + SPARE_BYTES)


def iota(shape, dim):
    return lax.broadcasted_iota(jnp.int32, shape, dim)


def ring(count):
    return [*range(0, count, 2), *range(count - 1, 0, -2)]


def select_kernel(
    clusters,
    reps,
    cap_in,
    adjacent_in,
    mask_in,
    assign_in,
    rows,
    out,
    slots,
    cap,
    adjacent,
    mask,
    assign,
    data,
    pick,
    filled,
    chosen,
    squares,
    in_sem,
    small_sem,
):
    steps, deep, _ = data.shape
    reads = [
        pltpu.make_async_copy(rows.at[i * deep : (i + 1) * deep, :], data.at[i], in_sem.at[i])
        for i in range(steps)
    ]
    for read in reads:
        read.start()
    wanted = ((assign_in, assign), (mask_in, mask), (cap_in, cap), (adjacent_in, adjacent))
    smalls = [
        pltpu.make_async_copy(here, there, small_sem.at[k]) for k, (here, there) in enumerate(wanted)
    ]
    for small in smalls:
        small.start()
    for small in smalls:
        small.wait()

    blocks = assign.shape[0]
    depth = chosen.shape[1]
    count = pick.shape[0]
    table = assign[...]
    sub = iota(table.shape, 0)
    active = jnp.zeros(table.shape, jnp.int32)
    for block in range(blocks):
        active = jnp.where(sub == block, mask[block], active)
    owner = jnp.full(table.shape, -1, jnp.int32)
    caps = [None] * clusters
    current = jnp.int32(0)
    for place in ring(clusters):
        owner = jnp.where(table == current, place, owner)
        caps[place] = cap[current]
        current = adjacent[current]
    live = jnp.where(active == 1, owner, -1)
    members = jnp.concatenate(
        [(live == c).astype(jnp.float32) for c in range(clusters)], axis=0
    ).astype(jnp.bfloat16)
    total = clusters * blocks
    earlier = (iota((LANES, LANES), 0) < iota((LANES, LANES), 1)).astype(jnp.bfloat16)
    within = jnp.dot(members, earlier, preferred_element_type=jnp.float32)
    left, right = iota((total, total), 0), iota((total, total), 1)
    same = (left // blocks == right // blocks) & (right < left)
    sums = jnp.dot(
        same.astype(jnp.bfloat16), members, preferred_element_type=jnp.float32
    ).astype(jnp.bfloat16)
    before = jnp.dot(
        sums, jnp.ones((LANES, LANES), jnp.bfloat16), preferred_element_type=jnp.float32
    )
    rank = (within + before).astype(jnp.int32)
    slot = jnp.full(table.shape, -1, jnp.int32)
    for c in range(clusters):
        own = rank[c * blocks : (c + 1) * blocks]
        slot = jnp.where((live == c) & (own < caps[c]), c * CAPS + own, slot)
    slots[...] = slot
    target = iota((count, LANES), 0)
    seen = jnp.zeros((count, LANES), jnp.float32)
    for block in range(blocks):
        hit = (target == slot[block : block + 1]).astype(jnp.float32)
        pick[:, block * LANES : (block + 1) * LANES] = hit.astype(jnp.bfloat16)
        seen += hit
    mark = jnp.sum(seen, axis=1, keepdims=True) < 0.5
    mark = mark & (iota(filled.shape, 1) == 0)
    filled[...] = jnp.where(mark, EMPTY_MARK, 0.0)

    power = jnp.zeros(squares.shape, jnp.float32)
    for i, read in enumerate(reads):
        read.wait()
        chunk_pick = pick[:, i * deep : (i + 1) * deep]
        for start in range(0, depth, FEATURE_STEP):
            cols = slice(start, start + FEATURE_STEP)
            part = jnp.dot(chunk_pick, data[i, :, cols], preferred_element_type=jnp.float32)
            if i:
                part += chosen[:, cols]
            chosen[:, cols] = part
            if i == steps - 1:
                for k in range(FEATURE_STEP // LANES):
                    piece = part[:, k * LANES : (k + 1) * LANES]
                    power += piece * piece

    scale = lax.rsqrt(jnp.sum(power, axis=1, keepdims=True) + 1e-06)
    squares[...] = jnp.broadcast_to(scale, squares.shape)
    quarter = depth // reps
    tiles = quarter // LANES

    def eight(group):
        for k in range(8):
            at = pl.ds(pl.multiple_of((group * 8 + k) * CAPS, 8), CAPS)
            gain, flag = squares[at, :], filled[at, :]
            for q in range(reps):
                pieces = []
                for t in range(tiles):
                    cols = slice(q * quarter + t * LANES, q * quarter + (t + 1) * LANES)
                    pieces.append(chosen[at, cols] * gain)
                pieces[0] += flag
                chunk = jnp.concatenate(pieces, axis=0).astype(jnp.bfloat16)
                out[(group * 8 + k) * reps + q] = chunk

    each(clusters // 8, eight, 1)


def tile_sets(blocks):
    tiles = []
    for p in range(0, blocks, 2):
        tiles.append((p, p + 1, True))
        tiles += [(i, j, False) for i in (p, p + 1) for j in range(i + 1, blocks)]
    half = len(tiles) // 2
    return tiles[:half], tiles[half:]


def set_rows(blocks):
    size = len(tile_sets(blocks)[0])
    return size // 2 * LANES + size % 2 * (LANES // 2)


def back_rows(ranks):
    return -(-(1 + ranks) // GROUPS)


def emit_tiles(y, core, x, edge_x, out, packed):
    count, quarter = x.shape
    blocks = count // LANES
    contract = (((1,), (1,)), ((), ()))
    tiles = tile_sets(blocks)[y]
    marker = (iota((16, quarter), 1) == 0).astype(jnp.bfloat16)
    extra = [marker] if edge_x is None else [edge_x[...], marker]
    size = sum(e.shape[0] for e in extra)
    edges = {}

    def put(owner, start, value):
        slot = (core == owner).astype(jnp.int32)
        out[slot, start : start + value.shape[0], :] = value

    def penalty(marks):
        return jnp.where(marks > 2.0, PENALTY, 0.0)

    def note(gram, main, col0):
        for k in range(gram.shape[1] // LANES):
            edges.setdefault(col0 + k, gram[main : main + size - 16, k * LANES : (k + 1) * LANES])

    for p in range(0, blocks, 2):
        mine = [(e, t) for e, t in enumerate(tiles) if t[0] // 2 == p // 2]
        if not mine:
            continue
        row0 = min(t[0] for _, t in mine)
        row1 = max(t[1] if t[2] else t[0] for _, t in mine) + 1
        col0 = min(t[0] if t[2] else t[1] for _, t in mine)
        col1 = max(t[1] for _, t in mine) + 1
        rows = x[row0 * LANES : row1 * LANES, :]
        left = jnp.concatenate([rows, *extra], axis=0)
        right = x[col0 * LANES : col1 * LANES, :]
        gram = lax.dot_general(left, right, contract, preferred_element_type=jnp.float32)
        main = rows.shape[0]
        col_pen = penalty(gram[main + size - 16 : main + size - 15])
        pairs = gram[:main] + penalty(rows[:, :1].astype(jnp.float32)) + col_pen
        note(gram, main, col0)

        def tile(i, j, pairs=pairs, row0=row0, col0=col0):
            i, j = (i - row0) * LANES, (j - col0) * LANES
            return pairs[i : i + LANES, j : j + LANES]

        for e, (i, j, diagonal) in mine:
            if diagonal:
                upper = iota((LANES, LANES), 0) < iota((LANES, LANES), 1)
                value = jnp.where(upper, tile(i, i), tile(j, j))
            else:
                value = tile(i, j)
            if e == len(tiles) - 1 and len(tiles) % 2:
                cut = LANES // 2
                for owner in range(2):
                    put(owner, e // 2 * LANES, value[owner * cut : (owner + 1) * cut])
            else:
                put(e % 2, e // 2 * LANES, value)

    if edge_x is None:
        return
    first = min(edges)
    if first:
        near = edge_x[...]
        note(
            lax.dot_general(
                near, x[: first * LANES, :], contract, preferred_element_type=jnp.float32
            ),
            0,
            0,
        )
    reps = 4
    ranks = edge_x.shape[0] // reps
    row_pen = penalty(edge_x[:, :1].astype(jnp.float32))
    shape = (ranks, LANES)
    lines = []
    for block in range(blocks):
        edge = edges[block] + row_pen
        lane_of = lax.rem(lax.div(iota(shape, 1) + block * LANES, CAPS), reps)
        value = edge[:ranks]
        for lane in range(1, reps):
            value = jnp.where(lane_of == lane, edge[lane * ranks : (lane + 1) * ranks], value)
        lines.append(value)

    height = back_rows(ranks)
    spot = iota((1, LANES), 1)
    for source in range(count // CAPS):
        block, offset = divmod(source * CAPS, LANES)
        value = lines[block]
        if offset + CAPS > LANES:
            value = jnp.where(iota(shape, 1) >= offset, value, lines[block + 1])
        turned = [pltpu.roll(value, (k * CAPS - offset) % LANES, 1) for k in range(GROUPS)]
        for row in range(height):
            line = jnp.zeros((1, LANES), jnp.float32)
            for k in range(GROUPS):
                j = row * GROUPS + k - 1
                if 0 <= j < ranks:
                    line = jnp.where(spot >= k * CAPS, turned[k][j : j + 1, :], line)
            at = source * height + row
            packed[at : at + 1, :] = line


def gather_kernel(ranks, got, x, edge_x, out, edge_rows):
    sources = got.shape[0]
    quarter = x.shape[1]
    tiles = quarter // LANES
    reps = edge_x.shape[0] // ranks
    me = lax.axis_index("rep")
    sub = iota((tiles, LANES), 0)

    def gather(pair):
        values = [got[2 * pair + k].astype(jnp.float32) for k in range(2)]
        for k in range(2):
            lines = jnp.zeros((tiles, LANES), jnp.float32)
            for t in range(tiles):
                line = jnp.broadcast_to(values[k][t * CAPS : t * CAPS + 1], lines.shape)
                lines = jnp.where(sub == t, line, lines)
            edge_rows[pl.ds((2 * pair + k) * tiles, tiles), :] = lines
        for t in range(tiles):
            rows = slice(t * CAPS, (t + 1) * CAPS)
            both = jnp.concatenate([v[rows] for v in values], axis=0)
            x[pl.ds(pair * 2 * CAPS, 2 * CAPS), t * LANES : (t + 1) * LANES] = both.astype(
                jnp.bfloat16
            )

    each(sources // 2, gather, 16)

    for k in range(tiles):
        lines = [
            edge_rows[pl.ds(lane * tiles + k, ranks, stride=reps * tiles), :]
            for lane in range(reps)
        ]
        edge_x[:, k * LANES : (k + 1) * LANES] = jnp.concatenate(lines, axis=0).astype(jnp.bfloat16)

    for y in range(2):
        pl.when(me // 2 != y)(functools.partial(emit_tiles, y, me % 2, x, None, out, None))


def near_kernel(x, edge_x, out, packed):
    me = lax.axis_index("rep")
    for y in range(2):
        pl.when(me // 2 == y)(functools.partial(emit_tiles, y, me % 2, x, edge_x, out, packed))


def score_kernel(sources, sums, logits, out, total):
    count = sources * CAPS
    blocks = count // LANES
    me = lax.axis_index("rep")
    core = me % 2
    sets = tile_sets(blocks)
    size = len(sets[0])
    total[...] = jnp.zeros_like(total)
    shape = (LANES, LANES)

    def by_rep(values):
        picked = jnp.int32(values[0])
        for k in range(1, len(values)):
            picked = jnp.where(me == k, jnp.int32(values[k]), picked)
        return picked

    def weigh(value, cut):
        return jax.nn.sigmoid(slope_gain * (value - cut))

    def rows_of(weight):
        return jnp.sum(weight.T, axis=0, keepdims=True)

    def cols_of(weight):
        return jnp.sum(weight, axis=0, keepdims=True)

    def plain(i, j, weight):
        total[pl.ds(i, 1), :] += rows_of(weight)
        total[pl.ds(j, 1), :] += cols_of(weight)

    def packed(i, j, weight):
        upper = jnp.where(iota(shape, 0) < iota(shape, 1), weight, 0.0)
        lower = jnp.where(iota(shape, 0) > iota(shape, 1), weight, 0.0)
        total[pl.ds(i, 1), :] += rows_of(upper) + cols_of(upper)
        total[pl.ds(j, 1), :] += rows_of(lower) + cols_of(lower)

    for place in range(size // 2):
        options = [sets[r // 2][2 * place + r % 2] for r in range(4)]
        i, j = by_rep([t[0] for t in options]), by_rep([t[1] for t in options])
        kinds = [t[2] for t in options]
        weight = weigh(sums[place * LANES : (place + 1) * LANES, :], inner_cut)
        if not any(kinds):
            plain(i, j, weight)
        else:
            kind = by_rep([int(k) for k in kinds])
            pl.when(kind == 1)(functools.partial(packed, i, j, weight))
            pl.when(kind == 0)(functools.partial(plain, i, j, weight))
    if size % 2:
        options = [sets[r // 2][size - 1] for r in range(4)]
        i, j = by_rep([t[0] for t in options]), by_rep([t[1] for t in options])
        start = size // 2 * LANES
        weight = weigh(sums[start : start + LANES // 2, :], inner_cut)
        halves = [jnp.where(core == k, weight, 0.0) for k in range(2)]
        plain(i, j, jnp.concatenate(halves, axis=0))

    height = logits.shape[0] // sources
    out[...] = logits[...]
    board = total[...]
    lane = iota((1, LANES), 1)
    for shift in range(0, LANES, 8):
        turned = pltpu.roll(board, (LANES - shift) % LANES, 1)
        for source in range(sources):
            block, offset = divmod(source * CAPS, LANES)
            if offset == shift:
                line = turned[block : block + 1, :]
                if offset + CAPS > LANES:
                    line = jnp.where(lane < LANES - offset, line, turned[block + 1 : block + 2, :])
                at = slice(source * height, source * height + 1)
                out[at, :] = jnp.where(lane < CAPS, line, logits[at, :])


def final_kernel(clusters, reps, slots, sums, out):
    height = sums.shape[0] // (clusters * reps)
    ranks = clusters
    slot = slots[...]

    def gathered(row):
        lines = []
        for c in range(clusters):
            starts = [(c * reps + q) * height + row for q in range(reps)]
            lines.append(sum(sums[at : at + 1, :] for at in starts))
        return jnp.concatenate(lines, axis=0)

    rows = [gathered(row) for row in range(height)]
    edges = [jax.nn.sigmoid(slope_gain * (r - edge_cut)) for r in rows]
    inner = rows[0]
    for k in range(GROUPS):
        mine = [r for r in range(height) if 1 <= r * GROUPS + k <= ranks]
        inner += pltpu.roll(sum(edges[r] for r in mine), (-k * CAPS) % LANES, 1)
    board = 1.0 / (1.0 + inner)
    result = jnp.ones(slot.shape, jnp.float32)
    for c in range(clusters):
        keep = jnp.broadcast_to(board[c : c + 1, :], slot.shape)
        rank = slot - c * CAPS
        mine = (rank >= 0) & (rank < CAPS)
        found = jnp.take_along_axis(keep, jnp.where(mine, rank, 0), axis=1)
        result = jnp.where(mine, found, result)
    out[...] = result


def local(embeddings, assignment, block_mask, cluster_cap, adjacent):
    dp_count, reps = lax.axis_size("dp"), lax.axis_size("rep")
    devices = dp_count * reps
    rows_dev, depth = embeddings.shape
    blocks = block_mask.shape[0]
    clusters = cluster_cap.shape[0]
    quarter = depth // reps
    tiles = quarter // LANES
    chunk = tiles * CAPS
    picks = clusters * CAPS
    steps = rows_dev // ROW_STEP
    smem = pl.BlockSpec(memory_space=pltpu.SMEM)
    vmem = pl.BlockSpec(memory_space=pltpu.VMEM)
    anywhere = pl.BlockSpec(memory_space=pl.ANY)

    inputs = (
        cluster_cap, adjacent, block_mask, assignment.reshape(blocks, LANES), embeddings
    )
    send, slots = pl.pallas_call(
        functools.partial(select_kernel, clusters, reps),
        in_specs=[anywhere] * 5,
        out_specs=[vmem, vmem],
        out_shape=[
            jax.ShapeDtypeStruct((devices, chunk, LANES), jnp.bfloat16),
            jax.ShapeDtypeStruct((blocks, LANES), jnp.int32),
        ],
        scratch_shapes=[
            pltpu.SMEM((clusters,), jnp.int32),
            pltpu.SMEM((clusters,), jnp.int32),
            pltpu.SMEM((blocks,), jnp.int32),
            pltpu.VMEM((blocks, LANES), jnp.int32),
            pltpu.VMEM((steps, ROW_STEP, depth), jnp.bfloat16),
            pltpu.VMEM((picks, rows_dev), jnp.bfloat16),
            pltpu.VMEM((picks, LANES), jnp.float32),
            pltpu.VMEM((picks, depth), jnp.float32),
            pltpu.VMEM((picks, LANES), jnp.float32),
            pltpu.SemaphoreType.DMA((steps,)),
            pltpu.SemaphoreType.DMA((4,)),
        ],
        compiler_params=pltpu.CompilerParams(vmem_limit_bytes=SELECT_BYTES),
        name="select_rows",
    )(*[pltpu.with_memory_space_constraint(x, pltpu.HBM) for x in inputs])

    got = lax.all_to_all(send, ALL, split_axis=0, concat_axis=0, tiled=True)

    count = devices * CAPS
    group = count // LANES
    part_rows = set_rows(group)
    height = back_rows(dp_count)
    near_bytes = (2 * part_rows + devices * height) * LANES * 4
    x, edge_x, far_parts = pl.pallas_call(
        functools.partial(gather_kernel, dp_count),
        in_specs=[vmem],
        out_specs=[vmem] * 3,
        out_shape=[
            jax.ShapeDtypeStruct((count, quarter), jnp.bfloat16),
            jax.ShapeDtypeStruct((reps * dp_count, quarter), jnp.bfloat16),
            jax.ShapeDtypeStruct((2, part_rows, LANES), jnp.float32),
        ],
        scratch_shapes=[pltpu.VMEM((devices * tiles, LANES), jnp.float32)],
        compiler_params=grant(6 * count * quarter + near_bytes),
        name="gather_far_tiles",
    )(got)

    wire = jnp.float16
    cores = [(0, 1), (1, 0), (2, 3), (3, 2)]
    across = [(0, 2), (2, 0), (1, 3), (3, 1)]
    order = ring(dp_count)
    back_one = [(order[(p + 1) % dp_count], order[p]) for p in range(dp_count)]
    far = lax.ppermute(far_parts[0].astype(wire), "rep", cores)
    edge_x = lax.ppermute(edge_x, "dp", back_one)
    far = (far_parts[1] + far.astype(jnp.float32)).astype(wire)
    far, x = lax.optimization_barrier((far, x))
    far = lax.ppermute(far, "rep", across)
    near_parts, packed = pl.pallas_call(
        near_kernel,
        in_specs=[vmem] * 2,
        out_specs=[vmem] * 2,
        out_shape=[
            jax.ShapeDtypeStruct((2, part_rows, LANES), jnp.float32),
            jax.ShapeDtypeStruct((devices * height, LANES), jnp.float32),
        ],
        compiler_params=grant(4 * count * quarter + near_bytes),
        cost_estimate=pl.CostEstimate(
            flops=count * count * quarter, bytes_accessed=2 * count * quarter, transcendentals=0
        ),
        name="near_tiles",
    )(x, edge_x)
    near = lax.ppermute(near_parts[0].astype(wire), "rep", cores)
    both = near_parts[1] + far.astype(jnp.float32)
    both = lax.optimization_barrier(both) + near.astype(jnp.float32)

    sums = pl.pallas_call(
        functools.partial(score_kernel, devices),
        in_specs=[vmem] * 2,
        out_specs=vmem,
        out_shape=jax.ShapeDtypeStruct((devices * height, LANES), jnp.float32),
        scratch_shapes=[pltpu.VMEM((-(-group // 8) * 8, LANES), jnp.float32)],
        compiler_params=grant(near_bytes),
        name="score_tiles",
    )(both, packed).reshape(devices, height, LANES)

    back = lax.all_to_all(sums, ALL, split_axis=0, concat_axis=0, tiled=True)
    keep = pl.pallas_call(
        functools.partial(final_kernel, clusters, reps),
        in_specs=[vmem] * 2,
        out_specs=vmem,
        out_shape=jax.ShapeDtypeStruct((blocks, LANES), jnp.float32),
        compiler_params=grant(0),
        name="final_keep",
    )(slots, back.reshape(devices * height, LANES))
    return keep.reshape(rows_dev)


def solution(mesh):
    placed = (P(ALL, None), P(ALL), P(ALL), P(), P())
    return jax.shard_map(local, mesh=mesh, in_specs=placed, out_specs=P(ALL), check_vma=False)
```

```python
import functools

import jax
import jax.numpy as jnp
from jax import lax
from jax.experimental import pallas as pl
from jax.experimental.pallas import tpu as pltpu
from jax.sharding import PartitionSpec as P

CAPS = 24
LANES = 128
GROUPS = LANES // CAPS
ALL = ("dp", "rep")
FEATURE_STEP = 512
ROW_STEP = 256
EMPTY_MARK = 4.0
PENALTY = -1000.0
SPARE_BYTES = 6 * 1024 * 1024
SELECT_BYTES = 48 * 1024 * 1024

slope_gain = 64.0
inner_cut = 0.12
edge_cut = 0.06


def each(count, body, limit=8):
    if count <= limit:
        for index in range(count):
            body(index)
    else:

        def step(index, carry):
            body(index)
            return carry

        lax.fori_loop(0, count, step, 0)


def grant(size):
    return pltpu.CompilerParams(vmem_limit_bytes=size + SPARE_BYTES)


def iota(shape, dim):
    return lax.broadcasted_iota(jnp.int32, shape, dim)


def ring(count):
    return [*range(0, count, 2), *range(count - 1, 0, -2)]


def select_kernel(
    clusters,
    reps,
    cap_in,
    adjacent_in,
    mask_in,
    assign_in,
    rows,
    out,
    slots,
    cap,
    adjacent,
    mask,
    assign,
    data,
    pick,
    filled,
    chosen,
    squares,
    in_sem,
    small_sem,
):
    steps, deep, _ = data.shape
    reads = [
        pltpu.make_async_copy(rows.at[i * deep : (i + 1) * deep, :], data.at[i], in_sem.at[i])
        for i in range(steps)
    ]
    for read in reads:
        read.start()
    wanted = ((assign_in, assign), (mask_in, mask), (cap_in, cap), (adjacent_in, adjacent))
    smalls = [
        pltpu.make_async_copy(here, there, small_sem.at[k]) for k, (here, there) in enumerate(wanted)
    ]
    for small in smalls:
        small.start()
    for small in smalls:
        small.wait()

    blocks = assign.shape[0]
    depth = chosen.shape[1]
    count = pick.shape[0]
    table = assign[...]
    sub = iota(table.shape, 0)
    active = jnp.zeros(table.shape, jnp.int32)
    for block in range(blocks):
        active = jnp.where(sub == block, mask[block], active)
    owner = jnp.full(table.shape, -1, jnp.int32)
    caps = [None] * clusters
    current = jnp.int32(0)
    for place in ring(clusters):
        owner = jnp.where(table == current, place, owner)
        caps[place] = cap[current]
        current = adjacent[current]
    live = jnp.where(active == 1, owner, -1)
    members = jnp.concatenate(
        [(live == c).astype(jnp.float32) for c in range(clusters)], axis=0
    ).astype(jnp.bfloat16)
    total = clusters * blocks
    earlier = (iota((LANES, LANES), 0) < iota((LANES, LANES), 1)).astype(jnp.bfloat16)
    within = jnp.dot(members, earlier, preferred_element_type=jnp.float32)
    left, right = iota((total, total), 0), iota((total, total), 1)
    same = (left // blocks == right // blocks) & (right < left)
    sums = jnp.dot(
        same.astype(jnp.bfloat16), members, preferred_element_type=jnp.float32
    ).astype(jnp.bfloat16)
    before = jnp.dot(
        sums, jnp.ones((LANES, LANES), jnp.bfloat16), preferred_element_type=jnp.float32
    )
    rank = (within + before).astype(jnp.int32)
    slot = jnp.full(table.shape, -1, jnp.int32)
    for c in range(clusters):
        own = rank[c * blocks : (c + 1) * blocks]
        slot = jnp.where((live == c) & (own < caps[c]), c * CAPS + own, slot)
    slots[...] = slot
    target = iota((count, LANES), 0)
    seen = jnp.zeros((count, LANES), jnp.float32)
    for block in range(blocks):
        hit = (target == slot[block : block + 1]).astype(jnp.float32)
        pick[:, block * LANES : (block + 1) * LANES] = hit.astype(jnp.bfloat16)
        seen += hit
    mark = jnp.sum(seen, axis=1, keepdims=True) < 0.5
    mark = mark & (iota(filled.shape, 1) == 0)
    filled[...] = jnp.where(mark, EMPTY_MARK, 0.0)

    power = jnp.zeros(squares.shape, jnp.float32)
    for i, read in enumerate(reads):
        read.wait()
        chunk_pick = pick[:, i * deep : (i + 1) * deep]
        for start in range(0, depth, FEATURE_STEP):
            cols = slice(start, start + FEATURE_STEP)
            part = jnp.dot(chunk_pick, data[i, :, cols], preferred_element_type=jnp.float32)
            if i:
                part += chosen[:, cols]
            chosen[:, cols] = part
            if i == steps - 1:
                for k in range(FEATURE_STEP // LANES):
                    piece = part[:, k * LANES : (k + 1) * LANES]
                    power += piece * piece

    scale = lax.rsqrt(jnp.sum(power, axis=1, keepdims=True) + 1e-06)
    squares[...] = jnp.broadcast_to(scale, squares.shape)
    quarter = depth // reps
    tiles = quarter // LANES

    def eight(group):
        for k in range(8):
            at = pl.ds(pl.multiple_of((group * 8 + k) * CAPS, 8), CAPS)
            gain, flag = squares[at, :], filled[at, :]
            for q in range(reps):
                pieces = []
                for t in range(tiles):
                    cols = slice(q * quarter + t * LANES, q * quarter + (t + 1) * LANES)
                    pieces.append(chosen[at, cols] * gain)
                pieces[0] += flag
                chunk = jnp.concatenate(pieces, axis=0).astype(jnp.bfloat16)
                out[(group * 8 + k) * reps + q] = chunk

    each(clusters // 8, eight, 1)


def tile_sets(blocks):
    tiles = []
    for p in range(0, blocks, 2):
        tiles.append((p, p + 1, True))
        tiles += [(i, j, False) for i in (p, p + 1) for j in range(i + 1, blocks)]
    half = len(tiles) // 2
    return tiles[:half], tiles[half:]


def set_rows(blocks):
    size = len(tile_sets(blocks)[0])
    return size // 2 * LANES + size % 2 * (LANES // 2)


def back_rows(ranks):
    return -(-(1 + ranks) // GROUPS)


def penalty(marks):
    return jnp.where(marks > 2.0, PENALTY, 0.0)


def emit_tiles(y, core, x, out):
    count, quarter = x.shape
    blocks = count // LANES
    contract = (((1,), (1,)), ((), ()))
    tiles = tile_sets(blocks)[y]
    marker = (iota((16, quarter), 1) == 0).astype(jnp.bfloat16)

    def put(owner, start, value):
        slot = (core == owner).astype(jnp.int32)
        out[slot, start : start + value.shape[0], :] = value

    for p in range(0, blocks, 2):
        mine = [(e, t) for e, t in enumerate(tiles) if t[0] // 2 == p // 2]
        if not mine:
            continue
        row0 = min(t[0] for _, t in mine)
        row1 = max(t[1] if t[2] else t[0] for _, t in mine) + 1
        col0 = min(t[0] if t[2] else t[1] for _, t in mine)
        col1 = max(t[1] for _, t in mine) + 1
        rows = x[row0 * LANES : row1 * LANES, :]
        left = jnp.concatenate([rows, marker], axis=0)
        right = x[col0 * LANES : col1 * LANES, :]
        gram = lax.dot_general(left, right, contract, preferred_element_type=jnp.float32)
        main = rows.shape[0]
        col_pen = penalty(gram[main : main + 1])
        pairs = gram[:main] + penalty(rows[:, :1].astype(jnp.float32)) + col_pen

        def tile(i, j, pairs=pairs, row0=row0, col0=col0):
            i, j = (i - row0) * LANES, (j - col0) * LANES
            return pairs[i : i + LANES, j : j + LANES]

        for e, (i, j, diagonal) in mine:
            if diagonal:
                upper = iota((LANES, LANES), 0) < iota((LANES, LANES), 1)
                value = jnp.where(upper, tile(i, i), tile(j, j))
            else:
                value = tile(i, j)
            if e == len(tiles) - 1 and len(tiles) % 2:
                cut = LANES // 2
                for owner in range(2):
                    put(owner, e // 2 * LANES, value[owner * cut : (owner + 1) * cut])
            else:
                put(e % 2, e // 2 * LANES, value)


def edge_kernel(reps, x, edge_x, packed):
    count = x.shape[0]
    ranks = edge_x.shape[0] // reps
    contract = (((1,), (1,)), ((), ()))
    near = edge_x[...]
    edges = lax.dot_general(near, x[...], contract, preferred_element_type=jnp.float32)
    edges = edges + penalty(near[:, :1].astype(jnp.float32))
    shape = (ranks, LANES)
    lines = []
    for block in range(count // LANES):
        edge = edges[:, block * LANES : (block + 1) * LANES]
        lane_of = lax.rem(lax.div(iota(shape, 1) + block * LANES, CAPS), reps)
        value = edge[:ranks]
        for lane in range(1, reps):
            value = jnp.where(lane_of == lane, edge[lane * ranks : (lane + 1) * ranks], value)
        lines.append(value)

    height = back_rows(ranks)
    spot = iota((1, LANES), 1)
    for source in range(count // CAPS):
        block, offset = divmod(source * CAPS, LANES)
        value = lines[block]
        if offset + CAPS > LANES:
            value = jnp.where(iota(shape, 1) >= offset, value, lines[block + 1])
        turned = [pltpu.roll(value, (k * CAPS - offset) % LANES, 1) for k in range(GROUPS)]
        for row in range(height):
            line = jnp.zeros((1, LANES), jnp.float32)
            for k in range(GROUPS):
                j = row * GROUPS + k - 1
                if 0 <= j < ranks:
                    line = jnp.where(spot >= k * CAPS, turned[k][j : j + 1, :], line)
            at = source * height + row
            packed[at : at + 1, :] = line


def gather_kernel(got, x, out):
    sources = got.shape[0]
    tiles = x.shape[1] // LANES
    me = lax.axis_index("rep")

    def gather(pair):
        values = [got[2 * pair + k].astype(jnp.float32) for k in range(2)]
        for t in range(tiles):
            rows = slice(t * CAPS, (t + 1) * CAPS)
            both = jnp.concatenate([v[rows] for v in values], axis=0)
            x[pl.ds(pair * 2 * CAPS, 2 * CAPS), t * LANES : (t + 1) * LANES] = both.astype(
                jnp.bfloat16
            )

    each(sources // 2, gather, 16)

    for y in range(2):
        pl.when(me // 2 != y)(functools.partial(emit_tiles, y, me % 2, x, out))


def first_rows_kernel(reps, x, edge_x):
    ranks = edge_x.shape[0] // reps
    shape = (8, x.shape[1])
    sub = iota(shape, 0)
    for first in range(0, edge_x.shape[0], 16):
        halves = []
        for start in (first, first + 8):
            lines = jnp.zeros(shape, jnp.float32)
            for k in range(8):
                lane, rank = divmod(start + k, ranks)
                at = (rank * reps + lane) * CAPS
                rows = x[at // 16 * 16 : at // 16 * 16 + 16, :].astype(jnp.float32)
                line = jnp.broadcast_to(rows[at % 16 : at % 16 + 1], shape)
                lines = jnp.where(sub == k, line, lines)
            halves.append(lines)
        edge_x[first : first + 16, :] = jnp.concatenate(halves, axis=0).astype(jnp.bfloat16)


def near_kernel(x, out):
    me = lax.axis_index("rep")
    for y in range(2):
        pl.when(me // 2 == y)(functools.partial(emit_tiles, y, me % 2, x, out))


def score_kernel(sources, sums, logits, out, total):
    count = sources * CAPS
    blocks = count // LANES
    me = lax.axis_index("rep")
    core = me % 2
    sets = tile_sets(blocks)
    size = len(sets[0])
    total[...] = jnp.zeros_like(total)
    shape = (LANES, LANES)

    def by_rep(values):
        picked = jnp.int32(values[0])
        for k in range(1, len(values)):
            picked = jnp.where(me == k, jnp.int32(values[k]), picked)
        return picked

    def weigh(value, cut):
        return jax.nn.sigmoid(slope_gain * (value - cut))

    def rows_of(weight):
        return jnp.sum(weight.T, axis=0, keepdims=True)

    def cols_of(weight):
        return jnp.sum(weight, axis=0, keepdims=True)

    def plain(i, j, weight):
        total[pl.ds(i, 1), :] += rows_of(weight)
        total[pl.ds(j, 1), :] += cols_of(weight)

    def packed(i, j, weight):
        upper = jnp.where(iota(shape, 0) < iota(shape, 1), weight, 0.0)
        lower = jnp.where(iota(shape, 0) > iota(shape, 1), weight, 0.0)
        total[pl.ds(i, 1), :] += rows_of(upper) + cols_of(upper)
        total[pl.ds(j, 1), :] += rows_of(lower) + cols_of(lower)

    for place in range(size // 2):
        options = [sets[r // 2][2 * place + r % 2] for r in range(4)]
        i, j = by_rep([t[0] for t in options]), by_rep([t[1] for t in options])
        kinds = [t[2] for t in options]
        weight = weigh(sums[place * LANES : (place + 1) * LANES, :], inner_cut)
        if not any(kinds):
            plain(i, j, weight)
        else:
            kind = by_rep([int(k) for k in kinds])
            pl.when(kind == 1)(functools.partial(packed, i, j, weight))
            pl.when(kind == 0)(functools.partial(plain, i, j, weight))
    if size % 2:
        options = [sets[r // 2][size - 1] for r in range(4)]
        i, j = by_rep([t[0] for t in options]), by_rep([t[1] for t in options])
        start = size // 2 * LANES
        weight = weigh(sums[start : start + LANES // 2, :], inner_cut)
        halves = [jnp.where(core == k, weight, 0.0) for k in range(2)]
        plain(i, j, jnp.concatenate(halves, axis=0))

    height = logits.shape[0] // sources
    out[...] = logits[...]
    board = total[...]
    lane = iota((1, LANES), 1)
    for shift in range(0, LANES, 8):
        turned = pltpu.roll(board, (LANES - shift) % LANES, 1)
        for source in range(sources):
            block, offset = divmod(source * CAPS, LANES)
            if offset == shift:
                line = turned[block : block + 1, :]
                if offset + CAPS > LANES:
                    line = jnp.where(lane < LANES - offset, line, turned[block + 1 : block + 2, :])
                at = slice(source * height, source * height + 1)
                out[at, :] = jnp.where(lane < CAPS, line, logits[at, :])


def final_kernel(clusters, reps, slots, sums, out):
    height = sums.shape[0] // (clusters * reps)
    ranks = clusters
    slot = slots[...]

    def gathered(row):
        lines = []
        for c in range(clusters):
            starts = [(c * reps + q) * height + row for q in range(reps)]
            lines.append(sum(sums[at : at + 1, :] for at in starts))
        return jnp.concatenate(lines, axis=0)

    rows = [gathered(row) for row in range(height)]
    edges = [jax.nn.sigmoid(slope_gain * (r - edge_cut)) for r in rows]
    inner = rows[0]
    for k in range(GROUPS):
        mine = [r for r in range(height) if 1 <= r * GROUPS + k <= ranks]
        inner += pltpu.roll(sum(edges[r] for r in mine), (-k * CAPS) % LANES, 1)
    board = 1.0 / (1.0 + inner)
    result = jnp.ones(slot.shape, jnp.float32)
    for c in range(clusters):
        keep = jnp.broadcast_to(board[c : c + 1, :], slot.shape)
        rank = slot - c * CAPS
        mine = (rank >= 0) & (rank < CAPS)
        found = jnp.take_along_axis(keep, jnp.where(mine, rank, 0), axis=1)
        result = jnp.where(mine, found, result)
    out[...] = result


def local(embeddings, assignment, block_mask, cluster_cap, adjacent):
    dp_count, reps = lax.axis_size("dp"), lax.axis_size("rep")
    devices = dp_count * reps
    rows_dev, depth = embeddings.shape
    blocks = block_mask.shape[0]
    clusters = cluster_cap.shape[0]
    quarter = depth // reps
    tiles = quarter // LANES
    chunk = tiles * CAPS
    picks = clusters * CAPS
    steps = rows_dev // ROW_STEP
    smem = pl.BlockSpec(memory_space=pltpu.SMEM)
    vmem = pl.BlockSpec(memory_space=pltpu.VMEM)
    anywhere = pl.BlockSpec(memory_space=pl.ANY)

    inputs = (
        cluster_cap, adjacent, block_mask, assignment.reshape(blocks, LANES), embeddings
    )
    send, slots = pl.pallas_call(
        functools.partial(select_kernel, clusters, reps),
        in_specs=[anywhere] * 5,
        out_specs=[vmem, vmem],
        out_shape=[
            jax.ShapeDtypeStruct((devices, chunk, LANES), jnp.bfloat16),
            jax.ShapeDtypeStruct((blocks, LANES), jnp.int32),
        ],
        scratch_shapes=[
            pltpu.SMEM((clusters,), jnp.int32),
            pltpu.SMEM((clusters,), jnp.int32),
            pltpu.SMEM((blocks,), jnp.int32),
            pltpu.VMEM((blocks, LANES), jnp.int32),
            pltpu.VMEM((steps, ROW_STEP, depth), jnp.bfloat16),
            pltpu.VMEM((picks, rows_dev), jnp.bfloat16),
            pltpu.VMEM((picks, LANES), jnp.float32),
            pltpu.VMEM((picks, depth), jnp.float32),
            pltpu.VMEM((picks, LANES), jnp.float32),
            pltpu.SemaphoreType.DMA((steps,)),
            pltpu.SemaphoreType.DMA((4,)),
        ],
        compiler_params=pltpu.CompilerParams(vmem_limit_bytes=SELECT_BYTES),
        name="select_rows",
    )(*[pltpu.with_memory_space_constraint(x, pltpu.HBM) for x in inputs])

    got = lax.all_to_all(send, ALL, split_axis=0, concat_axis=0, tiled=True)

    count = devices * CAPS
    group = count // LANES
    part_rows = set_rows(group)
    height = back_rows(dp_count)
    near_bytes = (2 * part_rows + devices * height) * LANES * 4
    x, far_parts = pl.pallas_call(
        gather_kernel,
        in_specs=[vmem],
        out_specs=[vmem] * 2,
        out_shape=[
            jax.ShapeDtypeStruct((count, quarter), jnp.bfloat16),
            jax.ShapeDtypeStruct((2, part_rows, LANES), jnp.float32),
        ],
        compiler_params=grant(6 * count * quarter + near_bytes),
        name="gather_far_tiles",
    )(got)
    edge_x = pl.pallas_call(
        functools.partial(first_rows_kernel, reps),
        in_specs=[vmem],
        out_specs=vmem,
        out_shape=jax.ShapeDtypeStruct((reps * dp_count, quarter), jnp.bfloat16),
        compiler_params=grant(4 * count * quarter),
        name="first_rows",
    )(x)

    wire = jnp.float16
    cores = [(0, 1), (1, 0), (2, 3), (3, 2)]
    across = [(0, 2), (2, 0), (1, 3), (3, 1)]
    order = ring(dp_count)
    back_one = [(order[(p + 1) % dp_count], order[p]) for p in range(dp_count)]
    far = lax.ppermute(far_parts[0].astype(wire), "rep", cores)
    edge_x = lax.ppermute(edge_x, "dp", back_one)
    far = (far_parts[1] + far.astype(jnp.float32)).astype(wire)
    far, x = lax.optimization_barrier((far, x))
    far = lax.ppermute(far, "rep", across)
    near_parts = pl.pallas_call(
        near_kernel,
        in_specs=[vmem],
        out_specs=vmem,
        out_shape=jax.ShapeDtypeStruct((2, part_rows, LANES), jnp.float32),
        compiler_params=grant(4 * count * quarter + near_bytes),
        cost_estimate=pl.CostEstimate(
            flops=count * count * quarter, bytes_accessed=2 * count * quarter, transcendentals=0
        ),
        name="near_tiles",
    )(x)
    packed = pl.pallas_call(
        functools.partial(edge_kernel, reps),
        in_specs=[vmem] * 2,
        out_specs=vmem,
        out_shape=jax.ShapeDtypeStruct((devices * height, LANES), jnp.float32),
        compiler_params=grant(4 * count * quarter + near_bytes),
        cost_estimate=pl.CostEstimate(
            flops=count * count * quarter, bytes_accessed=2 * count * quarter, transcendentals=0
        ),
        name="edge_logits",
    )(x, edge_x)
    near = lax.ppermute(near_parts[0].astype(wire), "rep", cores)
    near_kept, packed = lax.optimization_barrier((near_parts[1], packed))
    both = near_kept + far.astype(jnp.float32)
    both = lax.optimization_barrier(both) + near.astype(jnp.float32)

    sums = pl.pallas_call(
        functools.partial(score_kernel, devices),
        in_specs=[vmem] * 2,
        out_specs=vmem,
        out_shape=jax.ShapeDtypeStruct((devices * height, LANES), jnp.float32),
        scratch_shapes=[pltpu.VMEM((-(-group // 8) * 8, LANES), jnp.float32)],
        compiler_params=grant(near_bytes),
        name="score_tiles",
    )(both, packed).reshape(devices, height, LANES)

    back = lax.all_to_all(sums, ALL, split_axis=0, concat_axis=0, tiled=True)
    keep = pl.pallas_call(
        functools.partial(final_kernel, clusters, reps),
        in_specs=[vmem] * 2,
        out_specs=vmem,
        out_shape=jax.ShapeDtypeStruct((blocks, LANES), jnp.float32),
        compiler_params=grant(0),
        name="final_keep",
    )(slots, back.reshape(devices * height, LANES))
    return keep.reshape(rows_dev)


def solution(mesh):
    placed = (P(ALL, None), P(ALL), P(ALL), P(), P())
    return jax.shard_map(local, mesh=mesh, in_specs=placed, out_specs=P(ALL), check_vma=False)
```

```python
import functools

import jax
import jax.numpy as jnp
from jax import lax
from jax.experimental import pallas as pl
from jax.experimental.pallas import tpu as pltpu
from jax.sharding import PartitionSpec as P

CAPS = 24
LANES = 128
GROUPS = LANES // CAPS
ALL = ("dp", "rep")
FEATURE_STEP = 512
ROW_STEP = 256
EMPTY_MARK = 4.0
PENALTY = -1000.0
SPARE_BYTES = 6 * 1024 * 1024
SELECT_BYTES = 48 * 1024 * 1024

slope_gain = 64.0
inner_cut = 0.12
edge_cut = 0.06


def each(count, body, limit=8):
    if count <= limit:
        for index in range(count):
            body(index)
    else:

        def step(index, carry):
            body(index)
            return carry

        lax.fori_loop(0, count, step, 0)


def grant(size):
    return pltpu.CompilerParams(vmem_limit_bytes=size + SPARE_BYTES)


def iota(shape, dim):
    return lax.broadcasted_iota(jnp.int32, shape, dim)


def ring(count):
    return [*range(0, count, 2), *range(count - 1, 0, -2)]


def select_kernel(
    clusters,
    reps,
    cap_in,
    adjacent_in,
    mask_in,
    assign_in,
    rows,
    out,
    slots,
    cap,
    adjacent,
    mask,
    assign,
    data,
    pick,
    filled,
    chosen,
    squares,
    in_sem,
    small_sem,
):
    steps, deep, _ = data.shape
    reads = [
        pltpu.make_async_copy(rows.at[i * deep : (i + 1) * deep, :], data.at[i], in_sem.at[i])
        for i in range(steps)
    ]
    for read in reads:
        read.start()
    wanted = ((assign_in, assign), (mask_in, mask), (cap_in, cap), (adjacent_in, adjacent))
    smalls = [
        pltpu.make_async_copy(here, there, small_sem.at[k]) for k, (here, there) in enumerate(wanted)
    ]
    for small in smalls:
        small.start()
    for small in smalls:
        small.wait()

    blocks = assign.shape[0]
    depth = chosen.shape[1]
    count = pick.shape[0]
    table = assign[...]
    sub = iota(table.shape, 0)
    active = jnp.zeros(table.shape, jnp.int32)
    for block in range(blocks):
        active = jnp.where(sub == block, mask[block], active)
    owner = jnp.full(table.shape, -1, jnp.int32)
    caps = [None] * clusters
    current = jnp.int32(0)
    for place in ring(clusters):
        owner = jnp.where(table == current, place, owner)
        caps[place] = cap[current]
        current = adjacent[current]
    live = jnp.where(active == 1, owner, -1)
    members = jnp.concatenate(
        [(live == c).astype(jnp.float32) for c in range(clusters)], axis=0
    ).astype(jnp.bfloat16)
    total = clusters * blocks
    earlier = (iota((LANES, LANES), 0) < iota((LANES, LANES), 1)).astype(jnp.bfloat16)
    within = jnp.dot(members, earlier, preferred_element_type=jnp.float32)
    left, right = iota((total, total), 0), iota((total, total), 1)
    same = (left // blocks == right // blocks) & (right < left)
    sums = jnp.dot(
        same.astype(jnp.bfloat16), members, preferred_element_type=jnp.float32
    ).astype(jnp.bfloat16)
    before = jnp.dot(
        sums, jnp.ones((LANES, LANES), jnp.bfloat16), preferred_element_type=jnp.float32
    )
    rank = (within + before).astype(jnp.int32)
    slot = jnp.full(table.shape, -1, jnp.int32)
    for c in range(clusters):
        own = rank[c * blocks : (c + 1) * blocks]
        slot = jnp.where((live == c) & (own < caps[c]), c * CAPS + own, slot)
    slots[...] = slot
    target = iota((count, LANES), 0)
    seen = jnp.zeros((count, LANES), jnp.float32)
    for block in range(blocks):
        hit = (target == slot[block : block + 1]).astype(jnp.float32)
        pick[:, block * LANES : (block + 1) * LANES] = hit.astype(jnp.bfloat16)
        seen += hit
    mark = jnp.sum(seen, axis=1, keepdims=True) < 0.5
    mark = mark & (iota(filled.shape, 1) == 0)
    filled[...] = jnp.where(mark, EMPTY_MARK, 0.0)

    power = jnp.zeros(squares.shape, jnp.float32)
    for i, read in enumerate(reads):
        read.wait()
        chunk_pick = pick[:, i * deep : (i + 1) * deep]
        for start in range(0, depth, FEATURE_STEP):
            cols = slice(start, start + FEATURE_STEP)
            part = jnp.dot(chunk_pick, data[i, :, cols], preferred_element_type=jnp.float32)
            if i:
                part += chosen[:, cols]
            chosen[:, cols] = part
            if i == steps - 1:
                for k in range(FEATURE_STEP // LANES):
                    piece = part[:, k * LANES : (k + 1) * LANES]
                    power += piece * piece

    scale = lax.rsqrt(jnp.sum(power, axis=1, keepdims=True) + 1e-06)
    squares[...] = jnp.broadcast_to(scale, squares.shape)
    quarter = depth // reps
    tiles = quarter // LANES

    def eight(group):
        for k in range(8):
            at = pl.ds(pl.multiple_of((group * 8 + k) * CAPS, 8), CAPS)
            gain, flag = squares[at, :], filled[at, :]
            for q in range(reps):
                pieces = []
                for t in range(tiles):
                    cols = slice(q * quarter + t * LANES, q * quarter + (t + 1) * LANES)
                    pieces.append(chosen[at, cols] * gain)
                pieces[0] += flag
                chunk = jnp.concatenate(pieces, axis=0).astype(jnp.bfloat16)
                out[(group * 8 + k) * reps + q] = chunk

    each(clusters // 8, eight, 1)


def tile_sets(blocks):
    tiles = []
    for p in range(0, blocks, 2):
        tiles.append((p, p + 1, True))
        tiles += [(i, j, False) for i in (p, p + 1) for j in range(i + 1, blocks)]
    half = len(tiles) // 2
    return tiles[:half], tiles[half:]


def set_rows(blocks):
    size = len(tile_sets(blocks)[0])
    return size // 2 * LANES + size % 2 * (LANES // 2)


def back_rows(ranks):
    return -(-(1 + ranks) // GROUPS)


def penalty(marks):
    return jnp.where(marks > 2.0, PENALTY, 0.0)


def emit_tiles(y, core, x, out):
    count, quarter = x.shape
    blocks = count // LANES
    contract = (((1,), (1,)), ((), ()))
    tiles = tile_sets(blocks)[y]
    marker = (iota((16, quarter), 1) == 0).astype(jnp.bfloat16)

    def put(owner, start, value):
        slot = (core == owner).astype(jnp.int32)
        out[slot, start : start + value.shape[0], :] = value

    for p in range(0, blocks, 2):
        mine = [(e, t) for e, t in enumerate(tiles) if t[0] // 2 == p // 2]
        if not mine:
            continue
        row0 = min(t[0] for _, t in mine)
        row1 = max(t[1] if t[2] else t[0] for _, t in mine) + 1
        col0 = min(t[0] if t[2] else t[1] for _, t in mine)
        col1 = max(t[1] for _, t in mine) + 1
        rows = x[row0 * LANES : row1 * LANES, :]
        left = jnp.concatenate([rows, marker], axis=0)
        right = x[col0 * LANES : col1 * LANES, :]
        gram = lax.dot_general(left, right, contract, preferred_element_type=jnp.float32)
        main = rows.shape[0]
        col_pen = penalty(gram[main : main + 1])
        pairs = gram[:main] + penalty(rows[:, :1].astype(jnp.float32)) + col_pen

        def tile(i, j, pairs=pairs, row0=row0, col0=col0):
            i, j = (i - row0) * LANES, (j - col0) * LANES
            return pairs[i : i + LANES, j : j + LANES]

        for e, (i, j, diagonal) in mine:
            if diagonal:
                upper = iota((LANES, LANES), 0) < iota((LANES, LANES), 1)
                value = jnp.where(upper, tile(i, i), tile(j, j))
            else:
                value = tile(i, j)
            if e == len(tiles) - 1 and len(tiles) % 2:
                cut = LANES // 2
                for owner in range(2):
                    put(owner, e // 2 * LANES, value[owner * cut : (owner + 1) * cut])
            else:
                put(e % 2, e // 2 * LANES, value)


def edge_kernel(reps, x, edge_x, packed):
    count = x.shape[0]
    ranks = edge_x.shape[0] // reps
    contract = (((1,), (1,)), ((), ()))
    near = edge_x[...]
    edges = lax.dot_general(near, x[...], contract, preferred_element_type=jnp.float32)
    edges = edges + penalty(near[:, :1].astype(jnp.float32))
    shape = (ranks, LANES)
    lines = []
    for block in range(count // LANES):
        edge = edges[:, block * LANES : (block + 1) * LANES]
        lane_of = lax.rem(lax.div(iota(shape, 1) + block * LANES, CAPS), reps)
        value = edge[:ranks]
        for lane in range(1, reps):
            value = jnp.where(lane_of == lane, edge[lane * ranks : (lane + 1) * ranks], value)
        lines.append(value)

    half = ranks // 2
    height = back_rows(half)
    spot = iota((1, LANES), 1)
    me = lax.axis_index("rep")
    for source in range(count // CAPS):
        block, offset = divmod(source * CAPS, LANES)
        value = lines[block]
        if offset + CAPS > LANES:
            value = jnp.where(iota(shape, 1) >= offset, value, lines[block + 1])
        turned = [pltpu.roll(value, (k * CAPS - offset) % LANES, 1) for k in range(GROUPS)]
        for core in range(2):
            slot = (me % 2 == core).astype(jnp.int32)
            for row in range(height):
                line = jnp.zeros((1, LANES), jnp.float32)
                for k in range(GROUPS):
                    j = row * GROUPS + k - 1
                    if 0 <= j < half:
                        picked = turned[k][core * half + j : core * half + j + 1, :]
                        line = jnp.where(spot >= k * CAPS, picked, line)
                at = source * height + row
                packed[slot, at : at + 1, :] = line


def gather_kernel(got, x, out):
    sources = got.shape[0]
    tiles = x.shape[1] // LANES
    me = lax.axis_index("rep")

    def gather(pair):
        values = [got[2 * pair + k].astype(jnp.float32) for k in range(2)]
        for t in range(tiles):
            rows = slice(t * CAPS, (t + 1) * CAPS)
            both = jnp.concatenate([v[rows] for v in values], axis=0)
            x[pl.ds(pair * 2 * CAPS, 2 * CAPS), t * LANES : (t + 1) * LANES] = both.astype(
                jnp.bfloat16
            )

    each(sources // 2, gather, 16)

    for y in range(2):
        pl.when(me // 2 != y)(functools.partial(emit_tiles, y, me % 2, x, out))


def first_rows_kernel(reps, x, edge_x):
    ranks = edge_x.shape[0] // reps
    shape = (8, x.shape[1])
    sub = iota(shape, 0)
    for first in range(0, edge_x.shape[0], 16):
        halves = []
        for start in (first, first + 8):
            lines = jnp.zeros(shape, jnp.float32)
            for k in range(8):
                lane, rank = divmod(start + k, ranks)
                at = (rank * reps + lane) * CAPS
                rows = x[at // 16 * 16 : at // 16 * 16 + 16, :].astype(jnp.float32)
                line = jnp.broadcast_to(rows[at % 16 : at % 16 + 1], shape)
                lines = jnp.where(sub == k, line, lines)
            halves.append(lines)
        edge_x[first : first + 16, :] = jnp.concatenate(halves, axis=0).astype(jnp.bfloat16)


def near_kernel(x, out):
    me = lax.axis_index("rep")
    for y in range(2):
        pl.when(me // 2 == y)(functools.partial(emit_tiles, y, me % 2, x, out))


def score_kernel(sources, sums, logits, out, total):
    count = sources * CAPS
    blocks = count // LANES
    me = lax.axis_index("rep")
    core = me % 2
    sets = tile_sets(blocks)
    size = len(sets[0])
    total[...] = jnp.zeros_like(total)
    shape = (LANES, LANES)

    def by_rep(values):
        picked = jnp.int32(values[0])
        for k in range(1, len(values)):
            picked = jnp.where(me == k, jnp.int32(values[k]), picked)
        return picked

    def weigh(value, cut):
        return jax.nn.sigmoid(slope_gain * (value - cut))

    def rows_of(weight):
        return jnp.sum(weight.T, axis=0, keepdims=True)

    def cols_of(weight):
        return jnp.sum(weight, axis=0, keepdims=True)

    def plain(i, j, weight):
        total[pl.ds(i, 1), :] += rows_of(weight)
        total[pl.ds(j, 1), :] += cols_of(weight)

    def packed(i, j, weight):
        upper = jnp.where(iota(shape, 0) < iota(shape, 1), weight, 0.0)
        lower = jnp.where(iota(shape, 0) > iota(shape, 1), weight, 0.0)
        total[pl.ds(i, 1), :] += rows_of(upper) + cols_of(upper)
        total[pl.ds(j, 1), :] += rows_of(lower) + cols_of(lower)

    for place in range(size // 2):
        options = [sets[r // 2][2 * place + r % 2] for r in range(4)]
        i, j = by_rep([t[0] for t in options]), by_rep([t[1] for t in options])
        kinds = [t[2] for t in options]
        weight = weigh(sums[place * LANES : (place + 1) * LANES, :], inner_cut)
        if not any(kinds):
            plain(i, j, weight)
        else:
            kind = by_rep([int(k) for k in kinds])
            pl.when(kind == 1)(functools.partial(packed, i, j, weight))
            pl.when(kind == 0)(functools.partial(plain, i, j, weight))
    if size % 2:
        options = [sets[r // 2][size - 1] for r in range(4)]
        i, j = by_rep([t[0] for t in options]), by_rep([t[1] for t in options])
        start = size // 2 * LANES
        weight = weigh(sums[start : start + LANES // 2, :], inner_cut)
        halves = [jnp.where(core == k, weight, 0.0) for k in range(2)]
        plain(i, j, jnp.concatenate(halves, axis=0))

    height = logits.shape[0] // sources
    out[...] = logits[...]
    board = total[...]
    lane = iota((1, LANES), 1)
    for shift in range(0, LANES, 8):
        turned = pltpu.roll(board, (LANES - shift) % LANES, 1)
        for source in range(sources):
            block, offset = divmod(source * CAPS, LANES)
            if offset == shift:
                line = turned[block : block + 1, :]
                if offset + CAPS > LANES:
                    line = jnp.where(lane < LANES - offset, line, turned[block + 1 : block + 2, :])
                at = slice(source * height, source * height + 1)
                out[at, :] = jnp.where(lane < CAPS, line, logits[at, :])


def final_kernel(clusters, reps, slots, sums, out):
    height = sums.shape[0] // (clusters * reps)
    half = clusters // 2
    slot = slots[...]

    def part(q, row):
        return sums[pl.ds(q * height + row, clusters, stride=reps * height), :]

    inner = sum(part(q, 0) for q in range(reps))
    edges = []
    for row in range(height):
        logits = [part(core, row) + part(core + 2, row) for core in range(2)]
        edges.append(sum(jax.nn.sigmoid(slope_gain * (x - edge_cut)) for x in logits))
    for k in range(GROUPS):
        mine = [edges[r] for r in range(height) if 1 <= r * GROUPS + k <= half]
        if mine:
            inner += pltpu.roll(sum(mine), (-k * CAPS) % LANES, 1)
    board = 1.0 / (1.0 + inner)
    result = jnp.ones(slot.shape, jnp.float32)
    for c in range(clusters):
        keep = jnp.broadcast_to(board[c : c + 1, :], slot.shape)
        rank = slot - c * CAPS
        mine = (rank >= 0) & (rank < CAPS)
        found = jnp.take_along_axis(keep, jnp.where(mine, rank, 0), axis=1)
        result = jnp.where(mine, found, result)
    out[...] = result


def local(embeddings, assignment, block_mask, cluster_cap, adjacent):
    dp_count, reps = lax.axis_size("dp"), lax.axis_size("rep")
    devices = dp_count * reps
    rows_dev, depth = embeddings.shape
    blocks = block_mask.shape[0]
    clusters = cluster_cap.shape[0]
    quarter = depth // reps
    tiles = quarter // LANES
    chunk = tiles * CAPS
    picks = clusters * CAPS
    steps = rows_dev // ROW_STEP
    smem = pl.BlockSpec(memory_space=pltpu.SMEM)
    vmem = pl.BlockSpec(memory_space=pltpu.VMEM)
    anywhere = pl.BlockSpec(memory_space=pl.ANY)

    inputs = (
        cluster_cap, adjacent, block_mask, assignment.reshape(blocks, LANES), embeddings
    )
    send, slots = pl.pallas_call(
        functools.partial(select_kernel, clusters, reps),
        in_specs=[anywhere] * 5,
        out_specs=[vmem, vmem],
        out_shape=[
            jax.ShapeDtypeStruct((devices, chunk, LANES), jnp.bfloat16),
            jax.ShapeDtypeStruct((blocks, LANES), jnp.int32),
        ],
        scratch_shapes=[
            pltpu.SMEM((clusters,), jnp.int32),
            pltpu.SMEM((clusters,), jnp.int32),
            pltpu.SMEM((blocks,), jnp.int32),
            pltpu.VMEM((blocks, LANES), jnp.int32),
            pltpu.VMEM((steps, ROW_STEP, depth), jnp.bfloat16),
            pltpu.VMEM((picks, rows_dev), jnp.bfloat16),
            pltpu.VMEM((picks, LANES), jnp.float32),
            pltpu.VMEM((picks, depth), jnp.float32),
            pltpu.VMEM((picks, LANES), jnp.float32),
            pltpu.SemaphoreType.DMA((steps,)),
            pltpu.SemaphoreType.DMA((4,)),
        ],
        compiler_params=pltpu.CompilerParams(vmem_limit_bytes=SELECT_BYTES),
        name="select_rows",
    )(*[pltpu.with_memory_space_constraint(x, pltpu.HBM) for x in inputs])

    got = lax.all_to_all(send, ALL, split_axis=0, concat_axis=0, tiled=True)

    count = devices * CAPS
    group = count // LANES
    part_rows = set_rows(group)
    height = back_rows(dp_count // 2)
    near_bytes = (2 * part_rows + 2 * devices * height) * LANES * 4
    x, far_parts = pl.pallas_call(
        gather_kernel,
        in_specs=[vmem],
        out_specs=[vmem] * 2,
        out_shape=[
            jax.ShapeDtypeStruct((count, quarter), jnp.bfloat16),
            jax.ShapeDtypeStruct((2, part_rows, LANES), jnp.float32),
        ],
        compiler_params=grant(6 * count * quarter + near_bytes),
        name="gather_far_tiles",
    )(got)
    edge_x = pl.pallas_call(
        functools.partial(first_rows_kernel, reps),
        in_specs=[vmem],
        out_specs=vmem,
        out_shape=jax.ShapeDtypeStruct((reps * dp_count, quarter), jnp.bfloat16),
        compiler_params=grant(4 * count * quarter),
        name="first_rows",
    )(x)

    wire = jnp.float16
    cores = [(0, 1), (1, 0), (2, 3), (3, 2)]
    across = [(0, 2), (2, 0), (1, 3), (3, 1)]
    order = ring(dp_count)
    back_one = [(order[(p + 1) % dp_count], order[p]) for p in range(dp_count)]
    far = lax.ppermute(far_parts[0].astype(wire), "rep", cores)
    edge_x = lax.ppermute(edge_x, "dp", back_one)
    far = (far_parts[1] + far.astype(jnp.float32)).astype(wire)
    far, x = lax.optimization_barrier((far, x))
    far = lax.ppermute(far, "rep", across)
    near_parts = pl.pallas_call(
        near_kernel,
        in_specs=[vmem],
        out_specs=vmem,
        out_shape=jax.ShapeDtypeStruct((2, part_rows, LANES), jnp.float32),
        compiler_params=grant(4 * count * quarter + near_bytes),
        cost_estimate=pl.CostEstimate(
            flops=count * count * quarter, bytes_accessed=2 * count * quarter, transcendentals=0
        ),
        name="near_tiles",
    )(x)
    packed = pl.pallas_call(
        functools.partial(edge_kernel, reps),
        in_specs=[vmem] * 2,
        out_specs=vmem,
        out_shape=jax.ShapeDtypeStruct((2, devices * height, LANES), jnp.float32),
        compiler_params=grant(4 * count * quarter + near_bytes),
        cost_estimate=pl.CostEstimate(
            flops=count * count * quarter, bytes_accessed=2 * count * quarter, transcendentals=0
        ),
        name="edge_logits",
    )(x, edge_x)
    near = jnp.concatenate([near_parts[0], packed[0]]).astype(wire)
    near = lax.ppermute(near, "rep", cores)
    both = near_parts[1] + far.astype(jnp.float32)
    both = lax.optimization_barrier(both) + near[:part_rows].astype(jnp.float32)
    logits = packed[1] + near[part_rows:].astype(jnp.float32)

    sums = pl.pallas_call(
        functools.partial(score_kernel, devices),
        in_specs=[vmem] * 2,
        out_specs=vmem,
        out_shape=jax.ShapeDtypeStruct((devices * height, LANES), jnp.float32),
        scratch_shapes=[pltpu.VMEM((-(-group // 8) * 8, LANES), jnp.float32)],
        compiler_params=grant(near_bytes),
        name="score_tiles",
    )(both, logits).reshape(devices, height, LANES)

    back = lax.all_to_all(sums, ALL, split_axis=0, concat_axis=0, tiled=True)
    keep = pl.pallas_call(
        functools.partial(final_kernel, clusters, reps),
        in_specs=[vmem] * 2,
        out_specs=vmem,
        out_shape=jax.ShapeDtypeStruct((blocks, LANES), jnp.float32),
        compiler_params=grant(0),
        name="final_keep",
    )(slots, back.reshape(devices * height, LANES))
    return keep.reshape(rows_dev)


def solution(mesh):
    placed = (P(ALL, None), P(ALL), P(ALL), P(), P())
    return jax.shard_map(local, mesh=mesh, in_specs=placed, out_specs=P(ALL), check_vma=False)
```

```python
import functools

import jax
import jax.numpy as jnp
from jax import lax
from jax.experimental import pallas as pl
from jax.experimental.pallas import tpu as pltpu
from jax.sharding import PartitionSpec as P

CAPS = 24
LANES = 128
GROUPS = LANES // CAPS
ALL = ("dp", "rep")
FEATURE_STEP = 512
ROW_STEP = 256
EMPTY_MARK = 4.0
PENALTY = -1000.0
SPARE_BYTES = 6 * 1024 * 1024
SELECT_BYTES = 48 * 1024 * 1024

slope_gain = 64.0
inner_cut = 0.12
edge_cut = 0.06


def each(count, body, limit=8):
    if count <= limit:
        for index in range(count):
            body(index)
    else:

        def step(index, carry):
            body(index)
            return carry

        lax.fori_loop(0, count, step, 0)


def grant(size):
    return pltpu.CompilerParams(vmem_limit_bytes=size + SPARE_BYTES)


def iota(shape, dim):
    return lax.broadcasted_iota(jnp.int32, shape, dim)


def ring(count):
    return [*range(0, count, 2), *range(count - 1, 0, -2)]


def select_kernel(
    clusters,
    reps,
    cap_in,
    adjacent_in,
    mask_in,
    assign_in,
    rows,
    out,
    slots,
    cap,
    adjacent,
    mask,
    assign,
    data,
    pick,
    filled,
    chosen,
    squares,
    in_sem,
    small_sem,
):
    steps, deep, _ = data.shape
    reads = [
        pltpu.make_async_copy(rows.at[i * deep : (i + 1) * deep, :], data.at[i], in_sem.at[i])
        for i in range(steps)
    ]
    wanted = ((assign_in, assign), (mask_in, mask), (cap_in, cap), (adjacent_in, adjacent))
    smalls = [
        pltpu.make_async_copy(here, there, small_sem.at[k]) for k, (here, there) in enumerate(wanted)
    ]
    for small in smalls:
        small.start()
    for read in reads:
        read.start()
    for small in smalls:
        small.wait()

    blocks = assign.shape[0]
    depth = chosen.shape[1]
    count = pick.shape[0]
    table = assign[...]
    sub = iota(table.shape, 0)
    active = jnp.zeros(table.shape, jnp.int32)
    for block in range(blocks):
        active = jnp.where(sub == block, mask[block], active)
    owner = jnp.full(table.shape, -1, jnp.int32)
    caps = [None] * clusters
    current = jnp.int32(0)
    for place in ring(clusters):
        owner = jnp.where(table == current, place, owner)
        caps[place] = cap[current]
        current = adjacent[current]
    live = jnp.where(active == 1, owner, -1)
    members = jnp.concatenate(
        [(live == c).astype(jnp.float32) for c in range(clusters)], axis=0
    ).astype(jnp.bfloat16)
    total = clusters * blocks
    earlier = (iota((LANES, LANES), 0) < iota((LANES, LANES), 1)).astype(jnp.bfloat16)
    within = jnp.dot(members, earlier, preferred_element_type=jnp.float32)
    left, right = iota((total, total), 0), iota((total, total), 1)
    same = (left // blocks == right // blocks) & (right < left)
    sums = jnp.dot(
        same.astype(jnp.bfloat16), members, preferred_element_type=jnp.float32
    ).astype(jnp.bfloat16)
    before = jnp.dot(
        sums, jnp.ones((LANES, LANES), jnp.bfloat16), preferred_element_type=jnp.float32
    )
    rank = (within + before).astype(jnp.int32)
    slot = jnp.full(table.shape, -1, jnp.int32)
    for c in range(clusters):
        own = rank[c * blocks : (c + 1) * blocks]
        slot = jnp.where((live == c) & (own < caps[c]), c * CAPS + own, slot)
    slots[...] = slot
    target = iota((count, LANES), 0)
    seen = jnp.zeros((count, LANES), jnp.float32)
    for block in range(blocks):
        hit = (target == slot[block : block + 1]).astype(jnp.float32)
        pick[:, block * LANES : (block + 1) * LANES] = hit.astype(jnp.bfloat16)
        seen += hit
    mark = jnp.sum(seen, axis=1, keepdims=True) < 0.5
    mark = mark & (iota(filled.shape, 1) == 0)
    filled[...] = jnp.where(mark, EMPTY_MARK, 0.0)

    power = jnp.zeros(squares.shape, jnp.float32)
    for i, read in enumerate(reads):
        read.wait()
        chunk_pick = pick[:, i * deep : (i + 1) * deep]
        for start in range(0, depth, FEATURE_STEP):
            cols = slice(start, start + FEATURE_STEP)
            part = jnp.dot(chunk_pick, data[i, :, cols], preferred_element_type=jnp.float32)
            if i:
                part += chosen[:, cols]
            chosen[:, cols] = part
            if i == steps - 1:
                for k in range(FEATURE_STEP // LANES):
                    piece = part[:, k * LANES : (k + 1) * LANES]
                    power += piece * piece

    scale = lax.rsqrt(jnp.sum(power, axis=1, keepdims=True) + 1e-06)
    squares[...] = jnp.broadcast_to(scale, squares.shape)
    quarter = depth // reps
    tiles = quarter // LANES

    def eight(group):
        for k in range(8):
            at = pl.ds(pl.multiple_of((group * 8 + k) * CAPS, 8), CAPS)
            gain, flag = squares[at, :], filled[at, :]
            for q in range(reps):
                pieces = []
                for t in range(tiles):
                    cols = slice(q * quarter + t * LANES, q * quarter + (t + 1) * LANES)
                    pieces.append(chosen[at, cols] * gain)
                pieces[0] += flag
                chunk = jnp.concatenate(pieces, axis=0).astype(jnp.bfloat16)
                out[(group * 8 + k) * reps + q] = chunk

    each(clusters // 8, eight, 1)


def tile_sets(blocks):
    tiles = []
    for p in range(0, blocks, 2):
        tiles.append((p, p + 1, True))
        tiles += [(i, j, False) for i in (p, p + 1) for j in range(i + 1, blocks)]
    half = len(tiles) // 2
    return tiles[:half], tiles[half:]


def set_rows(blocks):
    size = len(tile_sets(blocks)[0])
    return size // 2 * LANES + size % 2 * (LANES // 2)


def back_rows(ranks):
    return -(-(1 + ranks) // GROUPS)


def penalty(marks):
    return jnp.where(marks > 2.0, PENALTY, 0.0)


def emit_tiles(y, core, x, out):
    count, quarter = x.shape
    blocks = count // LANES
    contract = (((1,), (1,)), ((), ()))
    tiles = tile_sets(blocks)[y]
    marker = (iota((16, quarter), 1) == 0).astype(jnp.bfloat16)

    def put(owner, start, value):
        slot = (core == owner).astype(jnp.int32)
        out[slot, start : start + value.shape[0], :] = value

    for p in range(0, blocks, 2):
        mine = [(e, t) for e, t in enumerate(tiles) if t[0] // 2 == p // 2]
        if not mine:
            continue
        row0 = min(t[0] for _, t in mine)
        row1 = max(t[1] if t[2] else t[0] for _, t in mine) + 1
        col0 = min(t[0] if t[2] else t[1] for _, t in mine)
        col1 = max(t[1] for _, t in mine) + 1
        rows = x[row0 * LANES : row1 * LANES, :]
        left = jnp.concatenate([rows, marker], axis=0)
        right = x[col0 * LANES : col1 * LANES, :]
        gram = lax.dot_general(left, right, contract, preferred_element_type=jnp.float32)
        main = rows.shape[0]
        col_pen = penalty(gram[main : main + 1])
        pairs = gram[:main] + penalty(rows[:, :1].astype(jnp.float32)) + col_pen

        def tile(i, j, pairs=pairs, row0=row0, col0=col0):
            i, j = (i - row0) * LANES, (j - col0) * LANES
            return pairs[i : i + LANES, j : j + LANES]

        for e, (i, j, diagonal) in mine:
            if diagonal:
                upper = iota((LANES, LANES), 0) < iota((LANES, LANES), 1)
                value = jnp.where(upper, tile(i, i), tile(j, j))
            else:
                value = tile(i, j)
            if e == len(tiles) - 1 and len(tiles) % 2:
                cut = LANES // 2
                for owner in range(2):
                    put(owner, e // 2 * LANES, value[owner * cut : (owner + 1) * cut])
            else:
                put(e % 2, e // 2 * LANES, value)


def edge_kernel(reps, x, edge_x, packed):
    count = x.shape[0]
    ranks = edge_x.shape[0] // reps
    contract = (((1,), (1,)), ((), ()))
    near = edge_x[...]
    edges = lax.dot_general(near, x[...], contract, preferred_element_type=jnp.float32)
    edges = edges + penalty(near[:, :1].astype(jnp.float32))
    shape = (ranks, LANES)
    lines = []
    for block in range(count // LANES):
        edge = edges[:, block * LANES : (block + 1) * LANES]
        lane_of = lax.rem(lax.div(iota(shape, 1) + block * LANES, CAPS), reps)
        value = edge[:ranks]
        for lane in range(1, reps):
            value = jnp.where(lane_of == lane, edge[lane * ranks : (lane + 1) * ranks], value)
        lines.append(value)

    half = ranks // 2
    height = back_rows(half)
    spot = iota((1, LANES), 1)
    me = lax.axis_index("rep")
    for source in range(count // CAPS):
        block, offset = divmod(source * CAPS, LANES)
        value = lines[block]
        if offset + CAPS > LANES:
            value = jnp.where(iota(shape, 1) >= offset, value, lines[block + 1])
        turned = [pltpu.roll(value, (k * CAPS - offset) % LANES, 1) for k in range(GROUPS)]
        for core in range(2):
            slot = (me % 2 == core).astype(jnp.int32)
            for row in range(height):
                line = jnp.zeros((1, LANES), jnp.float32)
                for k in range(GROUPS):
                    j = row * GROUPS + k - 1
                    if 0 <= j < half:
                        picked = turned[k][core * half + j : core * half + j + 1, :]
                        line = jnp.where(spot >= k * CAPS, picked, line)
                at = source * height + row
                packed[slot, at : at + 1, :] = line


def gather_kernel(got, x, out):
    sources = got.shape[0]
    tiles = x.shape[1] // LANES
    me = lax.axis_index("rep")

    def gather(pair):
        values = [got[2 * pair + k].astype(jnp.float32) for k in range(2)]
        for t in range(tiles):
            rows = slice(t * CAPS, (t + 1) * CAPS)
            both = jnp.concatenate([v[rows] for v in values], axis=0)
            x[pl.ds(pair * 2 * CAPS, 2 * CAPS), t * LANES : (t + 1) * LANES] = both.astype(
                jnp.bfloat16
            )

    each(sources // 2, gather, 16)

    for y in range(2):
        pl.when(me // 2 != y)(functools.partial(emit_tiles, y, me % 2, x, out))


def first_rows_kernel(reps, x, edge_x):
    ranks = edge_x.shape[0] // reps
    shape = (8, x.shape[1])
    sub = iota(shape, 0)
    for first in range(0, edge_x.shape[0], 16):
        halves = []
        for start in (first, first + 8):
            lines = jnp.zeros(shape, jnp.float32)
            for k in range(8):
                lane, rank = divmod(start + k, ranks)
                at = (rank * reps + lane) * CAPS
                rows = x[at // 16 * 16 : at // 16 * 16 + 16, :].astype(jnp.float32)
                line = jnp.broadcast_to(rows[at % 16 : at % 16 + 1], shape)
                lines = jnp.where(sub == k, line, lines)
            halves.append(lines)
        edge_x[first : first + 16, :] = jnp.concatenate(halves, axis=0).astype(jnp.bfloat16)


def near_kernel(x, out):
    me = lax.axis_index("rep")
    for y in range(2):
        pl.when(me // 2 == y)(functools.partial(emit_tiles, y, me % 2, x, out))


def score_kernel(sources, sums, logits, out, total):
    count = sources * CAPS
    blocks = count // LANES
    me = lax.axis_index("rep")
    core = me % 2
    sets = tile_sets(blocks)
    size = len(sets[0])
    total[...] = jnp.zeros_like(total)
    shape = (LANES, LANES)

    def by_rep(values):
        picked = jnp.int32(values[0])
        for k in range(1, len(values)):
            picked = jnp.where(me == k, jnp.int32(values[k]), picked)
        return picked

    def weigh(value, cut):
        return jax.nn.sigmoid(slope_gain * (value - cut))

    def rows_of(weight):
        return jnp.sum(weight.T, axis=0, keepdims=True)

    def cols_of(weight):
        return jnp.sum(weight, axis=0, keepdims=True)

    def plain(i, j, weight):
        total[pl.ds(i, 1), :] += rows_of(weight)
        total[pl.ds(j, 1), :] += cols_of(weight)

    def packed(i, j, weight):
        upper = jnp.where(iota(shape, 0) < iota(shape, 1), weight, 0.0)
        lower = jnp.where(iota(shape, 0) > iota(shape, 1), weight, 0.0)
        total[pl.ds(i, 1), :] += rows_of(upper) + cols_of(upper)
        total[pl.ds(j, 1), :] += rows_of(lower) + cols_of(lower)

    for place in range(size // 2):
        options = [sets[r // 2][2 * place + r % 2] for r in range(4)]
        i, j = by_rep([t[0] for t in options]), by_rep([t[1] for t in options])
        kinds = [t[2] for t in options]
        weight = weigh(sums[place * LANES : (place + 1) * LANES, :], inner_cut)
        if not any(kinds):
            plain(i, j, weight)
        else:
            kind = by_rep([int(k) for k in kinds])
            pl.when(kind == 1)(functools.partial(packed, i, j, weight))
            pl.when(kind == 0)(functools.partial(plain, i, j, weight))
    if size % 2:
        options = [sets[r // 2][size - 1] for r in range(4)]
        i, j = by_rep([t[0] for t in options]), by_rep([t[1] for t in options])
        start = size // 2 * LANES
        weight = weigh(sums[start : start + LANES // 2, :], inner_cut)
        halves = [jnp.where(core == k, weight, 0.0) for k in range(2)]
        plain(i, j, jnp.concatenate(halves, axis=0))

    height = logits.shape[0] // sources
    out[...] = logits[...]
    board = total[...]
    lane = iota((1, LANES), 1)
    for shift in range(0, LANES, 8):
        turned = pltpu.roll(board, (LANES - shift) % LANES, 1)
        for source in range(sources):
            block, offset = divmod(source * CAPS, LANES)
            if offset == shift:
                line = turned[block : block + 1, :]
                if offset + CAPS > LANES:
                    line = jnp.where(lane < LANES - offset, line, turned[block + 1 : block + 2, :])
                at = slice(source * height, source * height + 1)
                out[at, :] = jnp.where(lane < CAPS, line, logits[at, :])


def final_kernel(clusters, reps, slots, sums, out):
    height = sums.shape[0] // (clusters * reps)
    half = clusters // 2
    slot = slots[...]

    def part(q, row):
        return sums[pl.ds(q * height + row, clusters, stride=reps * height), :]

    inner = sum(part(q, 0) for q in range(reps))
    edges = []
    for row in range(height):
        logits = [part(core, row) + part(core + 2, row) for core in range(2)]
        edges.append(sum(jax.nn.sigmoid(slope_gain * (x - edge_cut)) for x in logits))
    for k in range(GROUPS):
        mine = [edges[r] for r in range(height) if 1 <= r * GROUPS + k <= half]
        if mine:
            inner += pltpu.roll(sum(mine), (-k * CAPS) % LANES, 1)
    board = 1.0 / (1.0 + inner)
    result = jnp.ones(slot.shape, jnp.float32)
    for c in range(clusters):
        keep = jnp.broadcast_to(board[c : c + 1, :], slot.shape)
        rank = slot - c * CAPS
        mine = (rank >= 0) & (rank < CAPS)
        found = jnp.take_along_axis(keep, jnp.where(mine, rank, 0), axis=1)
        result = jnp.where(mine, found, result)
    out[...] = result


def local(embeddings, assignment, block_mask, cluster_cap, adjacent):
    dp_count, reps = lax.axis_size("dp"), lax.axis_size("rep")
    devices = dp_count * reps
    rows_dev, depth = embeddings.shape
    blocks = block_mask.shape[0]
    clusters = cluster_cap.shape[0]
    quarter = depth // reps
    tiles = quarter // LANES
    chunk = tiles * CAPS
    picks = clusters * CAPS
    steps = rows_dev // ROW_STEP
    smem = pl.BlockSpec(memory_space=pltpu.SMEM)
    vmem = pl.BlockSpec(memory_space=pltpu.VMEM)
    anywhere = pl.BlockSpec(memory_space=pl.ANY)

    inputs = (
        cluster_cap, adjacent, block_mask, assignment.reshape(blocks, LANES), embeddings
    )
    send, slots = pl.pallas_call(
        functools.partial(select_kernel, clusters, reps),
        in_specs=[anywhere] * 5,
        out_specs=[vmem, vmem],
        out_shape=[
            jax.ShapeDtypeStruct((devices, chunk, LANES), jnp.bfloat16),
            jax.ShapeDtypeStruct((blocks, LANES), jnp.int32),
        ],
        scratch_shapes=[
            pltpu.SMEM((clusters,), jnp.int32),
            pltpu.SMEM((clusters,), jnp.int32),
            pltpu.SMEM((blocks,), jnp.int32),
            pltpu.VMEM((blocks, LANES), jnp.int32),
            pltpu.VMEM((steps, ROW_STEP, depth), jnp.bfloat16),
            pltpu.VMEM((picks, rows_dev), jnp.bfloat16),
            pltpu.VMEM((picks, LANES), jnp.float32),
            pltpu.VMEM((picks, depth), jnp.float32),
            pltpu.VMEM((picks, LANES), jnp.float32),
            pltpu.SemaphoreType.DMA((steps,)),
            pltpu.SemaphoreType.DMA((4,)),
        ],
        compiler_params=pltpu.CompilerParams(vmem_limit_bytes=SELECT_BYTES),
        name="select_rows",
    )(*[pltpu.with_memory_space_constraint(x, pltpu.HBM) for x in inputs])

    got = lax.all_to_all(send, ALL, split_axis=0, concat_axis=0, tiled=True)

    count = devices * CAPS
    group = count // LANES
    part_rows = set_rows(group)
    height = back_rows(dp_count // 2)
    near_bytes = (2 * part_rows + 2 * devices * height) * LANES * 4
    x, far_parts = pl.pallas_call(
        gather_kernel,
        in_specs=[vmem],
        out_specs=[vmem] * 2,
        out_shape=[
            jax.ShapeDtypeStruct((count, quarter), jnp.bfloat16),
            jax.ShapeDtypeStruct((2, part_rows, LANES), jnp.float32),
        ],
        compiler_params=grant(6 * count * quarter + near_bytes),
        name="gather_far_tiles",
    )(got)
    edge_x = pl.pallas_call(
        functools.partial(first_rows_kernel, reps),
        in_specs=[vmem],
        out_specs=vmem,
        out_shape=jax.ShapeDtypeStruct((reps * dp_count, quarter), jnp.bfloat16),
        compiler_params=grant(4 * count * quarter),
        name="first_rows",
    )(x)

    wire = jnp.float16
    cores = [(0, 1), (1, 0), (2, 3), (3, 2)]
    across = [(0, 2), (2, 0), (1, 3), (3, 1)]
    order = ring(dp_count)
    back_one = [(order[(p + 1) % dp_count], order[p]) for p in range(dp_count)]
    far = lax.ppermute(far_parts[0].astype(wire), "rep", cores)
    edge_x = lax.ppermute(edge_x, "dp", back_one)
    far = (far_parts[1] + far.astype(jnp.float32)).astype(wire)
    far, x = lax.optimization_barrier((far, x))
    far = lax.ppermute(far, "rep", across)
    near_parts = pl.pallas_call(
        near_kernel,
        in_specs=[vmem],
        out_specs=vmem,
        out_shape=jax.ShapeDtypeStruct((2, part_rows, LANES), jnp.float32),
        compiler_params=grant(4 * count * quarter + near_bytes),
        cost_estimate=pl.CostEstimate(
            flops=count * count * quarter, bytes_accessed=2 * count * quarter, transcendentals=0
        ),
        name="near_tiles",
    )(x)
    packed = pl.pallas_call(
        functools.partial(edge_kernel, reps),
        in_specs=[vmem] * 2,
        out_specs=vmem,
        out_shape=jax.ShapeDtypeStruct((2, devices * height, LANES), jnp.float32),
        compiler_params=grant(4 * count * quarter + near_bytes),
        cost_estimate=pl.CostEstimate(
            flops=count * count * quarter, bytes_accessed=2 * count * quarter, transcendentals=0
        ),
        name="edge_logits",
    )(x, edge_x)
    near = jnp.concatenate([near_parts[0], packed[0]]).astype(wire)
    near = lax.ppermute(near, "rep", cores)
    both = near_parts[1] + far.astype(jnp.float32)
    both = lax.optimization_barrier(both) + near[:part_rows].astype(jnp.float32)
    logits = packed[1] + near[part_rows:].astype(jnp.float32)

    sums = pl.pallas_call(
        functools.partial(score_kernel, devices),
        in_specs=[vmem] * 2,
        out_specs=vmem,
        out_shape=jax.ShapeDtypeStruct((devices * height, LANES), jnp.float32),
        scratch_shapes=[pltpu.VMEM((-(-group // 8) * 8, LANES), jnp.float32)],
        compiler_params=grant(near_bytes),
        name="score_tiles",
    )(both, logits).reshape(devices, height, LANES)

    back = lax.all_to_all(sums, ALL, split_axis=0, concat_axis=0, tiled=True)
    keep = pl.pallas_call(
        functools.partial(final_kernel, clusters, reps),
        in_specs=[vmem] * 2,
        out_specs=vmem,
        out_shape=jax.ShapeDtypeStruct((blocks, LANES), jnp.float32),
        compiler_params=grant(0),
        name="final_keep",
    )(slots, back.reshape(devices * height, LANES))
    return keep.reshape(rows_dev)


def solution(mesh):
    placed = (P(ALL, None), P(ALL), P(ALL), P(), P())
    return jax.shard_map(local, mesh=mesh, in_specs=placed, out_specs=P(ALL), check_vma=False)
```

```python
import functools

import jax
import jax.numpy as jnp
from jax import lax
from jax.experimental import pallas as pl
from jax.experimental.pallas import tpu as pltpu
from jax.sharding import PartitionSpec as P

CAPS = 24
LANES = 128
GROUPS = LANES // CAPS
ALL = ("dp", "rep")
FEATURE_STEP = 1024
ROW_STEP = 256
EMPTY_MARK = 4.0
PENALTY = -1000.0
SPARE_BYTES = 6 * 1024 * 1024
SELECT_BYTES = 48 * 1024 * 1024

slope_gain = 64.0
inner_cut = 0.12
edge_cut = 0.06


def each(count, body, limit=8):
    if count <= limit:
        for index in range(count):
            body(index)
    else:

        def step(index, carry):
            body(index)
            return carry

        lax.fori_loop(0, count, step, 0)


def grant(size):
    return pltpu.CompilerParams(vmem_limit_bytes=size + SPARE_BYTES)


def iota(shape, dim):
    return lax.broadcasted_iota(jnp.int32, shape, dim)


def ring(count):
    return [*range(0, count, 2), *range(count - 1, 0, -2)]


def select_kernel(
    clusters,
    reps,
    cap_in,
    adjacent_in,
    mask_in,
    assign_in,
    rows,
    out,
    slots,
    cap,
    adjacent,
    mask,
    assign,
    data,
    pick,
    filled,
    chosen,
    squares,
    in_sem,
    small_sem,
):
    steps, deep, _ = data.shape
    reads = [
        pltpu.make_async_copy(rows.at[i * deep : (i + 1) * deep, :], data.at[i], in_sem.at[i])
        for i in range(steps)
    ]
    for read in reads:
        read.start()
    wanted = ((assign_in, assign), (mask_in, mask), (cap_in, cap), (adjacent_in, adjacent))
    smalls = [
        pltpu.make_async_copy(here, there, small_sem.at[k]) for k, (here, there) in enumerate(wanted)
    ]
    for small in smalls:
        small.start()
    for small in smalls:
        small.wait()

    blocks = assign.shape[0]
    depth = chosen.shape[1]
    count = pick.shape[0]
    table = assign[...]
    sub = iota(table.shape, 0)
    active = jnp.zeros(table.shape, jnp.int32)
    for block in range(blocks):
        active = jnp.where(sub == block, mask[block], active)
    owner = jnp.full(table.shape, -1, jnp.int32)
    caps = [None] * clusters
    current = jnp.int32(0)
    for place in ring(clusters):
        owner = jnp.where(table == current, place, owner)
        caps[place] = cap[current]
        current = adjacent[current]
    live = jnp.where(active == 1, owner, -1)
    members = jnp.concatenate(
        [(live == c).astype(jnp.float32) for c in range(clusters)], axis=0
    ).astype(jnp.bfloat16)
    total = clusters * blocks
    earlier = (iota((LANES, LANES), 0) < iota((LANES, LANES), 1)).astype(jnp.bfloat16)
    within = jnp.dot(members, earlier, preferred_element_type=jnp.float32)
    left, right = iota((total, total), 0), iota((total, total), 1)
    same = (left // blocks == right // blocks) & (right < left)
    sums = jnp.dot(
        same.astype(jnp.bfloat16), members, preferred_element_type=jnp.float32
    ).astype(jnp.bfloat16)
    before = jnp.dot(
        sums, jnp.ones((LANES, LANES), jnp.bfloat16), preferred_element_type=jnp.float32
    )
    rank = (within + before).astype(jnp.int32)
    slot = jnp.full(table.shape, -1, jnp.int32)
    for c in range(clusters):
        own = rank[c * blocks : (c + 1) * blocks]
        slot = jnp.where((live == c) & (own < caps[c]), c * CAPS + own, slot)
    slots[...] = slot
    target = iota((count, LANES), 0)
    seen = jnp.zeros((count, LANES), jnp.float32)
    for block in range(blocks):
        hit = (target == slot[block : block + 1]).astype(jnp.float32)
        pick[:, block * LANES : (block + 1) * LANES] = hit.astype(jnp.bfloat16)
        seen += hit
    mark = jnp.sum(seen, axis=1, keepdims=True) < 0.5
    mark = mark & (iota(filled.shape, 1) == 0)
    filled[...] = jnp.where(mark, EMPTY_MARK, 0.0)

    power = jnp.zeros(squares.shape, jnp.float32)
    for i, read in enumerate(reads):
        read.wait()
        chunk_pick = pick[:, i * deep : (i + 1) * deep]
        for start in range(0, depth, FEATURE_STEP):
            cols = slice(start, start + FEATURE_STEP)
            part = jnp.dot(chunk_pick, data[i, :, cols], preferred_element_type=jnp.float32)
            if i:
                part += chosen[:, cols]
            chosen[:, cols] = part
            if i == steps - 1:
                for k in range(FEATURE_STEP // LANES):
                    piece = part[:, k * LANES : (k + 1) * LANES]
                    power += piece * piece

    scale = lax.rsqrt(jnp.sum(power, axis=1, keepdims=True) + 1e-06)
    squares[...] = jnp.broadcast_to(scale, squares.shape)
    quarter = depth // reps
    tiles = quarter // LANES

    def eight(group):
        for k in range(8):
            at = pl.ds(pl.multiple_of((group * 8 + k) * CAPS, 8), CAPS)
            gain, flag = squares[at, :], filled[at, :]
            for q in range(reps):
                pieces = []
                for t in range(tiles):
                    cols = slice(q * quarter + t * LANES, q * quarter + (t + 1) * LANES)
                    pieces.append(chosen[at, cols] * gain)
                pieces[0] += flag
                chunk = jnp.concatenate(pieces, axis=0).astype(jnp.bfloat16)
                out[(group * 8 + k) * reps + q] = chunk

    each(clusters // 8, eight, 1)


def tile_sets(blocks):
    tiles = []
    for p in range(0, blocks, 2):
        tiles.append((p, p + 1, True))
        tiles += [(i, j, False) for i in (p, p + 1) for j in range(i + 1, blocks)]
    half = len(tiles) // 2
    return tiles[:half], tiles[half:]


def set_rows(blocks):
    size = len(tile_sets(blocks)[0])
    return size // 2 * LANES + size % 2 * (LANES // 2)


def back_rows(ranks):
    return -(-(1 + ranks) // GROUPS)


def penalty(marks):
    return jnp.where(marks > 2.0, PENALTY, 0.0)


def emit_tiles(y, core, x, out):
    count, quarter = x.shape
    blocks = count // LANES
    contract = (((1,), (1,)), ((), ()))
    tiles = tile_sets(blocks)[y]
    marker = (iota((16, quarter), 1) == 0).astype(jnp.bfloat16)

    def put(owner, start, value):
        slot = (core == owner).astype(jnp.int32)
        out[slot, start : start + value.shape[0], :] = value

    for p in range(0, blocks, 2):
        mine = [(e, t) for e, t in enumerate(tiles) if t[0] // 2 == p // 2]
        if not mine:
            continue
        row0 = min(t[0] for _, t in mine)
        row1 = max(t[1] if t[2] else t[0] for _, t in mine) + 1
        col0 = min(t[0] if t[2] else t[1] for _, t in mine)
        col1 = max(t[1] for _, t in mine) + 1
        rows = x[row0 * LANES : row1 * LANES, :]
        left = jnp.concatenate([rows, marker], axis=0)
        right = x[col0 * LANES : col1 * LANES, :]
        gram = lax.dot_general(left, right, contract, preferred_element_type=jnp.float32)
        main = rows.shape[0]
        col_pen = penalty(gram[main : main + 1])
        pairs = gram[:main] + penalty(rows[:, :1].astype(jnp.float32)) + col_pen

        def tile(i, j, pairs=pairs, row0=row0, col0=col0):
            i, j = (i - row0) * LANES, (j - col0) * LANES
            return pairs[i : i + LANES, j : j + LANES]

        for e, (i, j, diagonal) in mine:
            if diagonal:
                upper = iota((LANES, LANES), 0) < iota((LANES, LANES), 1)
                value = jnp.where(upper, tile(i, i), tile(j, j))
            else:
                value = tile(i, j)
            if e == len(tiles) - 1 and len(tiles) % 2:
                cut = LANES // 2
                for owner in range(2):
                    put(owner, e // 2 * LANES, value[owner * cut : (owner + 1) * cut])
            else:
                put(e % 2, e // 2 * LANES, value)


def edge_kernel(reps, x, edge_x, packed):
    count = x.shape[0]
    ranks = edge_x.shape[0] // reps
    contract = (((1,), (1,)), ((), ()))
    near = edge_x[...]
    edges = lax.dot_general(near, x[...], contract, preferred_element_type=jnp.float32)
    edges = edges + penalty(near[:, :1].astype(jnp.float32))
    shape = (ranks, LANES)
    lines = []
    for block in range(count // LANES):
        edge = edges[:, block * LANES : (block + 1) * LANES]
        lane_of = lax.rem(lax.div(iota(shape, 1) + block * LANES, CAPS), reps)
        value = edge[:ranks]
        for lane in range(1, reps):
            value = jnp.where(lane_of == lane, edge[lane * ranks : (lane + 1) * ranks], value)
        lines.append(value)

    half = ranks // 2
    height = back_rows(half)
    spot = iota((1, LANES), 1)
    me = lax.axis_index("rep")
    for source in range(count // CAPS):
        block, offset = divmod(source * CAPS, LANES)
        value = lines[block]
        if offset + CAPS > LANES:
            value = jnp.where(iota(shape, 1) >= offset, value, lines[block + 1])
        turned = [pltpu.roll(value, (k * CAPS - offset) % LANES, 1) for k in range(GROUPS)]
        for core in range(2):
            slot = (me % 2 == core).astype(jnp.int32)
            for row in range(height):
                line = jnp.zeros((1, LANES), jnp.float32)
                for k in range(GROUPS):
                    j = row * GROUPS + k - 1
                    if 0 <= j < half:
                        picked = turned[k][core * half + j : core * half + j + 1, :]
                        line = jnp.where(spot >= k * CAPS, picked, line)
                at = source * height + row
                packed[slot, at : at + 1, :] = line


def gather_kernel(got, x, out):
    sources = got.shape[0]
    tiles = x.shape[1] // LANES
    me = lax.axis_index("rep")

    def gather(pair):
        values = [got[2 * pair + k].astype(jnp.float32) for k in range(2)]
        for t in range(tiles):
            rows = slice(t * CAPS, (t + 1) * CAPS)
            both = jnp.concatenate([v[rows] for v in values], axis=0)
            x[pl.ds(pair * 2 * CAPS, 2 * CAPS), t * LANES : (t + 1) * LANES] = both.astype(
                jnp.bfloat16
            )

    each(sources // 2, gather, 16)

    for y in range(2):
        pl.when(me // 2 != y)(functools.partial(emit_tiles, y, me % 2, x, out))


def first_rows_kernel(reps, x, edge_x):
    ranks = edge_x.shape[0] // reps
    shape = (8, x.shape[1])
    sub = iota(shape, 0)
    for first in range(0, edge_x.shape[0], 16):
        halves = []
        for start in (first, first + 8):
            lines = jnp.zeros(shape, jnp.float32)
            for k in range(8):
                lane, rank = divmod(start + k, ranks)
                at = (rank * reps + lane) * CAPS
                rows = x[at // 16 * 16 : at // 16 * 16 + 16, :].astype(jnp.float32)
                line = jnp.broadcast_to(rows[at % 16 : at % 16 + 1], shape)
                lines = jnp.where(sub == k, line, lines)
            halves.append(lines)
        edge_x[first : first + 16, :] = jnp.concatenate(halves, axis=0).astype(jnp.bfloat16)


def near_kernel(x, out):
    me = lax.axis_index("rep")
    for y in range(2):
        pl.when(me // 2 == y)(functools.partial(emit_tiles, y, me % 2, x, out))


def score_kernel(sources, sums, logits, out, total):
    count = sources * CAPS
    blocks = count // LANES
    me = lax.axis_index("rep")
    core = me % 2
    sets = tile_sets(blocks)
    size = len(sets[0])
    total[...] = jnp.zeros_like(total)
    shape = (LANES, LANES)

    def by_rep(values):
        picked = jnp.int32(values[0])
        for k in range(1, len(values)):
            picked = jnp.where(me == k, jnp.int32(values[k]), picked)
        return picked

    def weigh(value, cut):
        return jax.nn.sigmoid(slope_gain * (value - cut))

    def rows_of(weight):
        return jnp.sum(weight.T, axis=0, keepdims=True)

    def cols_of(weight):
        return jnp.sum(weight, axis=0, keepdims=True)

    def plain(i, j, weight):
        total[pl.ds(i, 1), :] += rows_of(weight)
        total[pl.ds(j, 1), :] += cols_of(weight)

    def packed(i, j, weight):
        upper = jnp.where(iota(shape, 0) < iota(shape, 1), weight, 0.0)
        lower = jnp.where(iota(shape, 0) > iota(shape, 1), weight, 0.0)
        total[pl.ds(i, 1), :] += rows_of(upper) + cols_of(upper)
        total[pl.ds(j, 1), :] += rows_of(lower) + cols_of(lower)

    for place in range(size // 2):
        options = [sets[r // 2][2 * place + r % 2] for r in range(4)]
        i, j = by_rep([t[0] for t in options]), by_rep([t[1] for t in options])
        kinds = [t[2] for t in options]
        weight = weigh(sums[place * LANES : (place + 1) * LANES, :], inner_cut)
        if not any(kinds):
            plain(i, j, weight)
        else:
            kind = by_rep([int(k) for k in kinds])
            pl.when(kind == 1)(functools.partial(packed, i, j, weight))
            pl.when(kind == 0)(functools.partial(plain, i, j, weight))
    if size % 2:
        options = [sets[r // 2][size - 1] for r in range(4)]
        i, j = by_rep([t[0] for t in options]), by_rep([t[1] for t in options])
        start = size // 2 * LANES
        weight = weigh(sums[start : start + LANES // 2, :], inner_cut)
        halves = [jnp.where(core == k, weight, 0.0) for k in range(2)]
        plain(i, j, jnp.concatenate(halves, axis=0))

    height = logits.shape[0] // sources
    out[...] = logits[...]
    board = total[...]
    lane = iota((1, LANES), 1)
    for shift in range(0, LANES, 8):
        turned = pltpu.roll(board, (LANES - shift) % LANES, 1)
        for source in range(sources):
            block, offset = divmod(source * CAPS, LANES)
            if offset == shift:
                line = turned[block : block + 1, :]
                if offset + CAPS > LANES:
                    line = jnp.where(lane < LANES - offset, line, turned[block + 1 : block + 2, :])
                at = slice(source * height, source * height + 1)
                out[at, :] = jnp.where(lane < CAPS, line, logits[at, :])


def final_kernel(clusters, reps, slots, sums, out):
    height = sums.shape[0] // (clusters * reps)
    half = clusters // 2
    slot = slots[...]

    def part(q, row):
        return sums[pl.ds(q * height + row, clusters, stride=reps * height), :]

    inner = sum(part(q, 0) for q in range(reps))
    edges = []
    for row in range(height):
        logits = [part(core, row) + part(core + 2, row) for core in range(2)]
        edges.append(sum(jax.nn.sigmoid(slope_gain * (x - edge_cut)) for x in logits))
    for k in range(GROUPS):
        mine = [edges[r] for r in range(height) if 1 <= r * GROUPS + k <= half]
        if mine:
            inner += pltpu.roll(sum(mine), (-k * CAPS) % LANES, 1)
    board = 1.0 / (1.0 + inner)
    result = jnp.ones(slot.shape, jnp.float32)
    for c in range(clusters):
        keep = jnp.broadcast_to(board[c : c + 1, :], slot.shape)
        rank = slot - c * CAPS
        mine = (rank >= 0) & (rank < CAPS)
        found = jnp.take_along_axis(keep, jnp.where(mine, rank, 0), axis=1)
        result = jnp.where(mine, found, result)
    out[...] = result


def local(embeddings, assignment, block_mask, cluster_cap, adjacent):
    dp_count, reps = lax.axis_size("dp"), lax.axis_size("rep")
    devices = dp_count * reps
    rows_dev, depth = embeddings.shape
    blocks = block_mask.shape[0]
    clusters = cluster_cap.shape[0]
    quarter = depth // reps
    tiles = quarter // LANES
    chunk = tiles * CAPS
    picks = clusters * CAPS
    steps = rows_dev // ROW_STEP
    smem = pl.BlockSpec(memory_space=pltpu.SMEM)
    vmem = pl.BlockSpec(memory_space=pltpu.VMEM)
    anywhere = pl.BlockSpec(memory_space=pl.ANY)

    inputs = (
        cluster_cap, adjacent, block_mask, assignment.reshape(blocks, LANES), embeddings
    )
    send, slots = pl.pallas_call(
        functools.partial(select_kernel, clusters, reps),
        in_specs=[anywhere] * 5,
        out_specs=[vmem, vmem],
        out_shape=[
            jax.ShapeDtypeStruct((devices, chunk, LANES), jnp.bfloat16),
            jax.ShapeDtypeStruct((blocks, LANES), jnp.int32),
        ],
        scratch_shapes=[
            pltpu.SMEM((clusters,), jnp.int32),
            pltpu.SMEM((clusters,), jnp.int32),
            pltpu.SMEM((blocks,), jnp.int32),
            pltpu.VMEM((blocks, LANES), jnp.int32),
            pltpu.VMEM((steps, ROW_STEP, depth), jnp.bfloat16),
            pltpu.VMEM((picks, rows_dev), jnp.bfloat16),
            pltpu.VMEM((picks, LANES), jnp.float32),
            pltpu.VMEM((picks, depth), jnp.float32),
            pltpu.VMEM((picks, LANES), jnp.float32),
            pltpu.SemaphoreType.DMA((steps,)),
            pltpu.SemaphoreType.DMA((4,)),
        ],
        compiler_params=pltpu.CompilerParams(vmem_limit_bytes=SELECT_BYTES),
        name="select_rows",
    )(*[pltpu.with_memory_space_constraint(x, pltpu.HBM) for x in inputs])

    got = lax.all_to_all(send, ALL, split_axis=0, concat_axis=0, tiled=True)

    count = devices * CAPS
    group = count // LANES
    part_rows = set_rows(group)
    height = back_rows(dp_count // 2)
    near_bytes = (2 * part_rows + 2 * devices * height) * LANES * 4
    x, far_parts = pl.pallas_call(
        gather_kernel,
        in_specs=[vmem],
        out_specs=[vmem] * 2,
        out_shape=[
            jax.ShapeDtypeStruct((count, quarter), jnp.bfloat16),
            jax.ShapeDtypeStruct((2, part_rows, LANES), jnp.float32),
        ],
        compiler_params=grant(6 * count * quarter + near_bytes),
        name="gather_far_tiles",
    )(got)
    edge_x = pl.pallas_call(
        functools.partial(first_rows_kernel, reps),
        in_specs=[vmem],
        out_specs=vmem,
        out_shape=jax.ShapeDtypeStruct((reps * dp_count, quarter), jnp.bfloat16),
        compiler_params=grant(4 * count * quarter),
        name="first_rows",
    )(x)

    wire = jnp.float16
    cores = [(0, 1), (1, 0), (2, 3), (3, 2)]
    across = [(0, 2), (2, 0), (1, 3), (3, 1)]
    order = ring(dp_count)
    back_one = [(order[(p + 1) % dp_count], order[p]) for p in range(dp_count)]
    far = lax.ppermute(far_parts[0].astype(wire), "rep", cores)
    edge_x = lax.ppermute(edge_x, "dp", back_one)
    far = (far_parts[1] + far.astype(jnp.float32)).astype(wire)
    far, x = lax.optimization_barrier((far, x))
    far = lax.ppermute(far, "rep", across)
    near_parts = pl.pallas_call(
        near_kernel,
        in_specs=[vmem],
        out_specs=vmem,
        out_shape=jax.ShapeDtypeStruct((2, part_rows, LANES), jnp.float32),
        compiler_params=grant(4 * count * quarter + near_bytes),
        cost_estimate=pl.CostEstimate(
            flops=count * count * quarter, bytes_accessed=2 * count * quarter, transcendentals=0
        ),
        name="near_tiles",
    )(x)
    packed = pl.pallas_call(
        functools.partial(edge_kernel, reps),
        in_specs=[vmem] * 2,
        out_specs=vmem,
        out_shape=jax.ShapeDtypeStruct((2, devices * height, LANES), jnp.float32),
        compiler_params=grant(4 * count * quarter + near_bytes),
        cost_estimate=pl.CostEstimate(
            flops=count * count * quarter, bytes_accessed=2 * count * quarter, transcendentals=0
        ),
        name="edge_logits",
    )(x, edge_x)
    near = jnp.concatenate([near_parts[0], packed[0]]).astype(wire)
    near = lax.ppermute(near, "rep", cores)
    both = near_parts[1] + far.astype(jnp.float32)
    both = lax.optimization_barrier(both) + near[:part_rows].astype(jnp.float32)
    logits = packed[1] + near[part_rows:].astype(jnp.float32)

    sums = pl.pallas_call(
        functools.partial(score_kernel, devices),
        in_specs=[vmem] * 2,
        out_specs=vmem,
        out_shape=jax.ShapeDtypeStruct((devices * height, LANES), jnp.float32),
        scratch_shapes=[pltpu.VMEM((-(-group // 8) * 8, LANES), jnp.float32)],
        compiler_params=grant(near_bytes),
        name="score_tiles",
    )(both, logits).reshape(devices, height, LANES)

    back = lax.all_to_all(sums, ALL, split_axis=0, concat_axis=0, tiled=True)
    keep = pl.pallas_call(
        functools.partial(final_kernel, clusters, reps),
        in_specs=[vmem] * 2,
        out_specs=vmem,
        out_shape=jax.ShapeDtypeStruct((blocks, LANES), jnp.float32),
        compiler_params=grant(0),
        name="final_keep",
    )(slots, back.reshape(devices * height, LANES))
    return keep.reshape(rows_dev)


def solution(mesh):
    placed = (P(ALL, None), P(ALL), P(ALL), P(), P())
    return jax.shard_map(local, mesh=mesh, in_specs=placed, out_specs=P(ALL), check_vma=False)
```
